32 devices in a mesh: wide: 16 (over z, x, core), narrow: 2 (over y).
Axes of the slice: x: 2, y: 2, z: 4, core: 2. Of those that a mesh axis runs over, the one named last changes fastest.
Arguments:
- tokens: bfloat16 [16384, 768], P(('wide', 'narrow')), may hold values from -6 to 6
- cotangent: bfloat16 [16384, 768], P(('wide', 'narrow')), may hold values from -6 to 6
- w_in: bfloat16 [768, 2304], P(('wide', 'narrow')), may hold values from -0.21875 to 0.21875
- w_out: bfloat16 [768, 768], P(('wide', 'narrow')), may hold values from -0.4375 to 0.4375
- w_gu: bfloat16 [768, 6144], P(('wide', 'narrow')), may hold values from -0.21875 to 0.21875
- w_down: bfloat16 [3072, 768], P(('wide', 'narrow')), may hold values from -0.21875 to 0.21875
- gain_mix: bfloat16 [768], P(('wide', 'narrow')), may hold values from 0.3984375 to 1.59375
- gain_ffn: bfloat16 [768], P(('wide', 'narrow')), may hold values from 0.3984375 to 1.59375
- buckets: int32 [32], P(('wide', 'narrow')), may hold values from 0 to 2, as said below
- lengths: int32 [32, 4], P(('wide', 'narrow')), may hold values from 0 to 512, as said below
Outputs:
- layer_out: bfloat16 [16384, 768], P(('wide', 'narrow'))
- grad_tokens: bfloat16 [16384, 768], P(('wide', 'narrow'))
- grad_w_in: float32 [768, 2304], P(('wide', 'narrow'))
- grad_w_out: float32 [768, 768], P(('wide', 'narrow'))
- grad_w_gu: float32 [768, 6144], P(('wide', 'narrow'))
- grad_w_down: float32 [3072, 768], P(('wide', 'narrow'))
- grad_gain_mix: float32 [768], P(('wide', 'narrow'))
- grad_gain_ffn: float32 [768], P(('wide', 'narrow'))
- kernel_norms: float32 [768], P(('wide', 'narrow'))
The draws below stay inside these ranges and needn't reach their ends.
Inputs may be any that keep to these rules, and one draw needn't show every extreme that they name: `buckets`: bucket of each device block: 0 holds 4 rows of 128 slots, 1 holds 2 rows of 256, 2 holds one row of 512; some block has bucket 2. `lengths`: valid slots at the front of each row of a block; row slots past the bucket's row count are 0; every used row is at least half valid and the first row of each block is fully valid.
All inputs are finite; a program needn't handle non-finite values.
Results may differ from the reference program's by a relative error of at most 0.018.
Values may be sent and summed in bfloat16 or wider, within the bound.
No kernel may reach another device: no remote copies, remote signals or barrier semaphores. Data moves between devices by JAX's collectives and lax.ppermute only.
A program may use at most 256 MiB of HBM per device.

```python
import jax
import jax.numpy as jnp
from jax import lax

D = 768
FF = 3072
TOK_DEV = 512
GROUPS = 32
TOKENS = 16384


def bucket_pick(key):
    bucket_key = jax.random.fold_in(key, 101)
    bucket_ids = jax.random.randint(bucket_key, (GROUPS,), 0, 3)
    forced_spot = jax.random.randint(jax.random.fold_in(bucket_key, 7), (), 0, GROUPS)
    return jnp.where(jnp.arange(GROUPS) == forced_spot, 2, bucket_ids).astype(jnp.int32)


def draw_buckets(key, part):
    bucket_ids = bucket_pick(key)
    return bucket_ids


def draw_lengths(key, part):
    bucket_ids = bucket_pick(key)
    key = jax.random.fold_in(key, 5)
    row_total = jnp.where(bucket_ids == 0, 4, jnp.where(bucket_ids == 1, 2, 1)).astype(jnp.int32)
    row_length = TOK_DEV // row_total
    half_length = row_length // 2
    offsets = jax.random.randint(key, (GROUPS, 4), 0, TOK_DEV)
    chosen = half_length[:, None] + offsets % (half_length[:, None] + 1)
    slot_ids = jnp.arange(4, dtype=jnp.int32)[None, :]
    chosen = jnp.where(slot_ids == 0, row_length[:, None], chosen)
    return jnp.where(slot_ids < row_total[:, None], chosen, 0).astype(jnp.int32)


def levels(key, shape, split, low, top_value):
    def one(dim, shards_of):
        heights = jax.random.uniform(jax.random.fold_in(jax.random.fold_in(key, 6), dim), (shards_of,), jnp.float32, low / len(split), top_value / len(split))
        return jnp.repeat(jnp.exp(heights), shape[dim] // shards_of).reshape((-1,) + (1,) * (len(shape) - dim - 1))

    loudness = one(*split[0])
    for cut in split[1:]:
        loudness = loudness * one(*cut)
    return loudness


def normal_values(own_key, dims, deviation, bound, shards=(), held_as=jnp.bfloat16):
    array = deviation * jax.random.normal(own_key, dims, jnp.float32)
    if shards:
        array = array * levels(own_key, dims, shards, -0.22, 0.18)
    return jnp.clip(array, -bound, bound).astype(held_as)


def setup_inputs(seed: int = 0) -> dict:
    key_of = jax.random.split(jax.random.key(seed), 11)
    tokens = normal_values(key_of[0], (TOKENS, D), 1.0, 6.0, ((0, 32),))
    cotangent = normal_values(key_of[1], (TOKENS, D), 1.0, 6.0, ((0, 32),))
    w_in = normal_values(key_of[2], (D, 3 * D), D ** -0.5, 0.21875, ((0, 32),))
    w_out = normal_values(key_of[3], (D, D), (D // 4) ** -0.5, 0.4375, ((0, 32),))
    w_gu = normal_values(key_of[4], (D, 2 * FF), D ** -0.5, 0.21875, ((0, 32),))
    w_down = normal_values(key_of[5], (FF, D), (FF // 4) ** -0.5, 0.21875, ((0, 32),))
    gain_mix = jnp.clip(1.0 + 0.12 * jax.random.normal(key_of[6], (D,), jnp.float32), 0.3984375, 1.59375).astype(jnp.bfloat16)
    gain_ffn = jnp.clip(1.0 + 0.12 * jax.random.normal(key_of[7], (D,), jnp.float32), 0.3984375, 1.59375).astype(jnp.bfloat16)
    buckets = draw_buckets(jax.random.fold_in(key_of[10], 71), 0)
    lengths = draw_lengths(jax.random.fold_in(key_of[10], 71), 0)
    return dict(tokens=tokens, cotangent=cotangent, w_in=w_in, w_out=w_out, w_gu=w_gu, w_down=w_down, gain_mix=gain_mix, gain_ffn=gain_ffn, buckets=buckets, lengths=lengths)


HIGHEST_PRECISION = lax.Precision.HIGHEST

@jax.custom_vjp
def low(v):
    return lax.optimization_barrier(v.astype(jnp.bfloat16)).astype(jnp.float32)

@jax.custom_vjp
def low_back(v):
    return v

def low_keep(v):
    return (low(v), None)

def low_pass(kept, grad):
    return (grad,)

def back_keep(v):
    return (v, None)

def back_low(kept, grad):
    return (low(grad),)
low.defvjp(low_keep, low_pass)
low_back.defvjp(back_keep, back_low)

def row_mask(bucket_id, length_row, tok_count):
    row_total = jnp.where(bucket_id == 0, 4, jnp.where(bucket_id == 1, 2, 1)).astype(jnp.int32)
    row_length = tok_count // row_total
    position = jnp.arange(tok_count, dtype=jnp.int32)
    slot_index = position // row_length
    within_row = position - slot_index * row_length
    slot_ids = jnp.arange(4, dtype=jnp.int32)
    length_here = lax.optimization_barrier(jnp.sum(jnp.where(slot_index[:, None] == slot_ids[None, :], length_row[None, :], 0), axis=1))
    return (within_row < length_here).astype(jnp.float32)[:, None]

def rms_scale(values, gain):
    return values * lax.rsqrt(lax.optimization_barrier(jnp.mean(values * values, axis=-1, keepdims=True)) + 1e-06) * gain

def fft_branch(row_total):

    def convolve(kernel, values):
        tok_count, model_width = kernel.shape
        row_length = tok_count // row_total
        kernel_rows = kernel.reshape(row_total, row_length, model_width)
        value_rows = values.reshape(row_total, row_length, model_width)
        squares = lax.optimization_barrier(jnp.sum(kernel_rows * kernel_rows, axis=1, keepdims=True))
        norms = jnp.sqrt(squares + 1e-05)
        unit_rows = kernel_rows / norms
        spectrum = jnp.fft.rfft(unit_rows, axis=1) * jnp.fft.rfft(value_rows, axis=1)
        mixed_rows = jnp.fft.irfft(spectrum, n=row_length, axis=1)
        return (mixed_rows.reshape(tok_count, model_width), lax.optimization_barrier(jnp.mean(norms[:, 0, :], axis=0)))
    return convolve

def layer_block(activations, gain_one, gain_two, full_in, full_out, full_gu, full_down, bucket_id, length_row):
    pad_mask = row_mask(bucket_id, length_row, activations.shape[0])
    model_width = activations.shape[1]
    normed = low(rms_scale(activations, gain_one))
    projected = low_back(jnp.dot(normed, full_in, precision=HIGHEST_PRECISION))
    kernel = jnp.tanh(projected[:, :model_width]) * pad_mask
    gate_mix = projected[:, model_width:2 * model_width]
    values = projected[:, 2 * model_width:] * pad_mask
    mixed_rows, norm_mean = lax.switch(bucket_id, [fft_branch(4), fft_branch(2), fft_branch(1)], kernel, values)
    gated_mix = low(mixed_rows * jax.nn.sigmoid(gate_mix) * pad_mask)
    branch_mix = low_back(jnp.dot(gated_mix, full_out, precision=HIGHEST_PRECISION))
    middle = activations + branch_mix
    normed_ffn = low(rms_scale(middle, gain_two))
    gate_up = low_back(jnp.dot(normed_ffn, full_gu, precision=HIGHEST_PRECISION))
    hidden = low(jax.nn.silu(gate_up[:, :FF]) * gate_up[:, FF:])
    branch_ffn = low_back(jnp.dot(hidden, full_down, precision=HIGHEST_PRECISION))
    return ((middle + branch_ffn) * pad_mask, norm_mean)

def reference(tokens, cotangent, w_in, w_out, w_gu, w_down, gain_mix, gain_ffn, buckets, lengths):
    blocks = tokens.astype(jnp.float32).reshape(GROUPS, TOK_DEV, D)

    def forward(blocks, gain_one, gain_two, full_in, full_out, full_gu, full_down):
        block_step = jax.checkpoint(layer_block)

        def per_block(block_items):
            return block_step(block_items[0], gain_one, gain_two, full_in, full_out, full_gu, full_down, block_items[1], block_items[2])
        results, norm_terms = lax.map(per_block, (blocks, buckets, lengths))
        return (results, norm_terms)
    results, pullback, norm_terms = jax.vjp(forward, blocks, gain_mix.astype(jnp.float32), gain_ffn.astype(jnp.float32), w_in.astype(jnp.float32), w_out.astype(jnp.float32), w_gu.astype(jnp.float32), w_down.astype(jnp.float32), has_aux=True)
    grads = pullback(cotangent.astype(jnp.float32).reshape(GROUPS, TOK_DEV, D))
    layer_out = results.reshape(TOKENS, D).astype(jnp.bfloat16)
    grad_tokens = grads[0].reshape(TOKENS, D).astype(jnp.bfloat16)
    kernel_norms = lax.optimization_barrier(jnp.mean(norm_terms, axis=0))
    return (layer_out, grad_tokens, grads[3], grads[4], grads[5], grads[6], grads[1], grads[2], kernel_norms)
```

```python
import functools

import jax
import jax.numpy as jnp
import ml_dtypes
import numpy as np
from jax import lax
from jax.experimental import pallas as pl
from jax.experimental.pallas import tpu as pltpu
from jax.sharding import PartitionSpec as P

F32 = jnp.float32
BF16 = jnp.bfloat16
ROW_SLOTS = 4
BUCKETS = 3
VMEM_BYTES = 56 * 1024 * 1024


def transform_tables(tok_count):
    highs, lows = [], []
    for bucket in range(BUCKETS):
        rows = ROW_SLOTS >> bucket
        length = tok_count // rows
        half = length // 2
        angle = 2.0 * np.pi * (np.arange(half)[:, None] * np.arange(length)[None, :] % length) / length
        real = np.cos(angle) * np.sqrt(2.0 / length)
        imag = -np.sin(angle) * np.sqrt(2.0 / length)
        real[0] = 1.0 / np.sqrt(length)
        imag[0] = (1.0 - 2.0 * (np.arange(length) % 2)) / np.sqrt(length)
        table = np.zeros((tok_count, tok_count))
        for row in range(rows):
            at = slice(row * length, (row + 1) * length)
            table[row * half : (row + 1) * half, at] = real
            table[tok_count // 2 + row * half : tok_count // 2 + (row + 1) * half, at] = imag
        high = table.astype(ml_dtypes.bfloat16)
        highs.append(high)
        lows.append((table - high.astype(np.float64)).astype(ml_dtypes.bfloat16))
    high, low = np.stack(highs), np.stack(lows)
    return high, low, np.ascontiguousarray(high.transpose(0, 2, 1)), np.ascontiguousarray(low.transpose(0, 2, 1))


def mm(left, right):
    return jnp.dot(left, right, preferred_element_type=F32)


def mm_nt(left, right):
    return lax.dot_general(left, right, (((1,), (1,)), ((), ())), preferred_element_type=F32)


def mm_tn(left, right):
    return lax.dot_general(left, right, (((0,), (0,)), ((), ())), preferred_element_type=F32)


def transform(high, low, values):
    top = values.astype(BF16)
    rest = (values - top.astype(F32)).astype(BF16)
    return mm(high, top) + (mm(high, rest) + mm(low, top))


def bin_facts(bucket, shape, tok_count):
    half = lax.shift_left(jnp.int32(tok_count // (2 * ROW_SLOTS)), bucket)
    spot = lax.broadcasted_iota(jnp.int32, shape, 0)
    edge = (spot & (half - 1)) == 0
    length = (2 * half).astype(F32)
    scale = jnp.where(edge, jnp.sqrt(length), jnp.sqrt(0.5 * length))
    return edge, scale


def pad_mask(bucket, lengths, shape, tok_count):
    quarter = tok_count // ROW_SLOTS
    shift = (quarter.bit_length() - 1) + bucket
    spot = lax.broadcasted_iota(jnp.int32, shape, 0)
    slot = lax.shift_right_logical(spot, jnp.broadcast_to(shift, shape))
    within = spot - lax.shift_left(slot, jnp.broadcast_to(shift, shape))
    length = jnp.where(
        slot == 0, lengths[0], jnp.where(slot == 1, lengths[1], jnp.where(slot == 2, lengths[2], lengths[3]))
    )
    return (within < length).astype(F32)


def row_sums(bucket, values, tok_count):
    quarter = tok_count // ROW_SLOTS
    s = [jnp.sum(values[i * quarter : (i + 1) * quarter], axis=0, keepdims=True) for i in range(ROW_SLOTS)]
    left, right = s[0] + s[1], s[2] + s[3]
    whole = left + right
    pairs = (left, left, right, right)
    return [jnp.where(bucket == 0, s[i], jnp.where(bucket == 1, pairs[i], whole)) for i in range(ROW_SLOTS)]


def over_rows(parts, tok_count):
    quarter = tok_count // ROW_SLOTS
    return jnp.concatenate([jnp.broadcast_to(p, (quarter, p.shape[1])) for p in parts], axis=0)


def mix_forward_kernel(
    facts, x_ref, g1_ref, g2_ref, wa_ref, wc_ref, wv_ref, wo_ref, mh_ref, ml_ref, th_ref, tl_ref,
    normed_ref, gated_ref, mid_ref, nf_ref, t_ref, s_ref, mix_ref, kf_ref, vf_ref, norm_ref, acc_ref,
):
    step = pl.program_id(0)
    tok_count = x_ref.shape[0]
    bucket = facts[0]
    lengths = [facts[1 + i] for i in range(ROW_SLOTS)]

    @pl.when(step == 0)
    def _():
        x = x_ref[...].astype(F32)
        r = lax.rsqrt(jnp.mean(x * x, axis=-1, keepdims=True) + 1e-06)
        normed_ref[...] = (x * r * g1_ref[...]).astype(BF16)

    normed = normed_ref[...]
    a = mm(normed, wa_ref[...])
    c = mm(normed, wc_ref[...])
    v = mm(normed, wv_ref[...])
    mask = pad_mask(bucket, lengths, a.shape, tok_count)
    t = jnp.tanh(a) * mask
    v = v * mask
    squares = [s + 1e-05 for s in row_sums(bucket, t * t, tok_count)]
    norms = [jnp.sqrt(s) for s in squares]
    norm_ref[...] = (norms[0] + norms[1] + norms[2] + norms[3]) * 0.25
    unit = t * over_rows([1.0 / n for n in norms], tok_count)
    half = tok_count // 2
    kf = transform(mh_ref[0], ml_ref[0], unit)
    vf = transform(mh_ref[0], ml_ref[0], v)
    kf_ref[...] = kf
    vf_ref[...] = vf
    edge, scale = bin_facts(bucket, (half, a.shape[1]), tok_count)
    kr, ki, vr, vi = kf[:half], kf[half:], vf[:half], vf[half:]
    kivi = ki * vi
    pr = (kr * vr - jnp.where(edge, 0.0, kivi)) * scale
    pi = jnp.where(edge, kivi, kr * vi + ki * vr) * scale
    mixed = transform(th_ref[0], tl_ref[0], jnp.concatenate([pr, pi], axis=0))
    sig = 1.0 / (1.0 + jnp.exp(-c))
    t_ref[...] = t
    s_ref[...] = sig
    mix_ref[...] = mixed
    gated = (mixed * sig * mask).astype(BF16)
    gated_ref[...] = gated
    part = mm(gated, wo_ref[...])

    @pl.when(step == 0)
    def _():
        acc_ref[...] = part

    @pl.when(step > 0)
    def _():
        acc_ref[...] += part

    @pl.when(step == pl.num_programs(0) - 1)
    def _():
        mid = x_ref[...].astype(F32) + acc_ref[...]
        mid_ref[...] = mid
        r = lax.rsqrt(jnp.mean(mid * mid, axis=-1, keepdims=True) + 1e-06)
        nf_ref[...] = (mid * r * g2_ref[...]).astype(BF16)


def mix_forward(facts, x, g1, g2, half0, half1, tables):
    tok, width = x.shape
    tile = 256
    steps = width // tile
    whole = lambda shape: pl.BlockSpec(shape, lambda j, s: (0,) * len(shape))
    table = pl.BlockSpec((1, tok, tok), lambda j, s: (s[0], 0, 0))
    column = pl.BlockSpec((tok, tile), lambda j, s: (0, j))
    return pl.pallas_call(
        mix_forward_kernel,
        grid_spec=pltpu.PrefetchScalarGridSpec(
            num_scalar_prefetch=1,
            grid=(steps,),
            in_specs=[
                whole((tok, width)), whole((1, width)), whole((1, width)),
                pl.BlockSpec((width, tile), lambda j, s: (0, j)),
                pl.BlockSpec((width, tile), lambda j, s: (0, steps + j)),
                pl.BlockSpec((width, tile), lambda j, s: (0, j)),
                pl.BlockSpec((tile, width), lambda j, s: (j, 1)),
                table, table, table, table,
            ],
            out_specs=[
                whole((tok, width)), column, whole((tok, width)), whole((tok, width)),
                column, column, column, column, column,
                pl.BlockSpec((1, tile), lambda j, s: (0, j)),
            ],
            scratch_shapes=[pltpu.VMEM((tok, width), F32)],
        ),
        out_shape=[
            jax.ShapeDtypeStruct((tok, width), BF16), jax.ShapeDtypeStruct((tok, width), BF16),
            jax.ShapeDtypeStruct((tok, width), F32), jax.ShapeDtypeStruct((tok, width), BF16),
            *[jax.ShapeDtypeStruct((tok, width), F32)] * 5,
            jax.ShapeDtypeStruct((1, width), F32),
        ],
        compiler_params=pltpu.CompilerParams(vmem_limit_bytes=VMEM_BYTES),
        name="mix_forward",
    )(facts, x, g1, g2, half0, half0, half1, half1, *tables)


def rms_back(values, gain, grad):
    r = lax.rsqrt(jnp.mean(values * values, axis=-1, keepdims=True) + 1e-06)
    scaled = values * r
    inner = grad * gain
    dot = jnp.mean(inner * scaled, axis=-1, keepdims=True)
    return r * (inner - scaled * dot), grad * scaled


def mix_back_kernel(
    facts, x_ref, cot_ref, g1_ref, g2_ref, mid_ref, own_ref, sib_ref, normed_ref, gated_ref,
    t_ref, s_ref, mix_ref, kf_ref, vf_ref, wa_ref, wc_ref, wv_ref, wo_ref, mh_ref, ml_ref, th_ref, tl_ref,
    tok_ref, ga_ref, gc_ref, gv_ref, go_ref, gain1_ref, gain2_ref, gm_ref, low_ref, acc_ref,
):
    step = pl.program_id(0)
    tok_count = x_ref.shape[0]
    bucket = facts[0]
    lengths = [facts[1 + i] for i in range(ROW_SLOTS)]

    @pl.when(step == 0)
    def _():
        outer = cot_ref[...].astype(F32) * pad_mask(bucket, lengths, cot_ref.shape, tok_count)
        grad = own_ref[...] + sib_ref[...].astype(F32)
        back, terms = rms_back(mid_ref[...], g2_ref[...], grad)
        gain2_ref[...] = jnp.sum(terms, axis=0, keepdims=True)
        grad_mid = outer + back
        gm_ref[...] = grad_mid
        low_ref[...] = grad_mid.astype(BF16)

    low = low_ref[...]
    grad_gated = mm_nt(low, wo_ref[...])
    go_ref[...] = mm_tn(gated_ref[...], low).astype(BF16)
    mask = pad_mask(bucket, lengths, grad_gated.shape, tok_count)
    grad_gated = grad_gated * mask
    sig = s_ref[...]
    grad_c = grad_gated * mix_ref[...] * (sig * (1.0 - sig))
    half = tok_count // 2
    df = transform(mh_ref[0], ml_ref[0], grad_gated * sig)
    edge, scale = bin_facts(bucket, (half, sig.shape[1]), tok_count)
    kf, vf = kf_ref[...], vf_ref[...]
    kr, ki, vr, vi = kf[:half], kf[half:], vf[:half], vf[half:]
    dr, di = df[:half] * scale, df[half:] * scale
    divi, diki = di * vi, di * ki
    dkr = dr * vr + jnp.where(edge, 0.0, divi)
    dki = jnp.where(edge, divi, di * vr - dr * vi)
    dvr = dr * kr + jnp.where(edge, 0.0, diki)
    dvi = jnp.where(edge, diki, di * kr - dr * ki)
    du = transform(th_ref[0], tl_ref[0], jnp.concatenate([dkr, dki], axis=0))
    dv = transform(th_ref[0], tl_ref[0], jnp.concatenate([dvr, dvi], axis=0)) * mask
    t = t_ref[...]
    inverse = [lax.rsqrt(s + 1e-05) for s in row_sums(bucket, t * t, tok_count)]
    dots = row_sums(bucket, du * t, tok_count)
    coupling = [d * i * i * i for d, i in zip(dots, inverse)]
    dt = du * over_rows(inverse, tok_count) - t * over_rows(coupling, tok_count)
    da = (dt * mask * (1.0 - t * t)).astype(BF16)
    dc = grad_c.astype(BF16)
    dv = dv.astype(BF16)
    normed = normed_ref[...]
    ga_ref[...] = mm_tn(normed, da).astype(BF16)
    gc_ref[...] = mm_tn(normed, dc).astype(BF16)
    gv_ref[...] = mm_tn(normed, dv).astype(BF16)
    part = mm_nt(da, wa_ref[...]) + mm_nt(dc, wc_ref[...]) + mm_nt(dv, wv_ref[...])

    @pl.when(step == 0)
    def _():
        acc_ref[...] = part

    @pl.when(step > 0)
    def _():
        acc_ref[...] += part

    @pl.when(step == pl.num_programs(0) - 1)
    def _():
        back, terms = rms_back(x_ref[...].astype(F32), g1_ref[...], acc_ref[...])
        gain1_ref[...] = jnp.sum(terms, axis=0, keepdims=True)
        tok_ref[...] = (gm_ref[...] + back).astype(BF16)


def mix_back(facts, x, cot, g1, g2, mid, own, sib, normed, gated, kept, half0, half1, tables):
    tok, width = x.shape
    tile = 256
    steps = width // tile
    whole = lambda shape: pl.BlockSpec(shape, lambda j, s: (0,) * len(shape))
    table = pl.BlockSpec((1, tok, tok), lambda j, s: (s[0], 0, 0))
    column = pl.BlockSpec((tok, tile), lambda j, s: (0, j))
    tall = pl.BlockSpec((width, tile), lambda j, s: (0, j))
    rows = (tok, width)
    return pl.pallas_call(
        mix_back_kernel,
        grid_spec=pltpu.PrefetchScalarGridSpec(
            num_scalar_prefetch=1,
            grid=(steps,),
            in_specs=[
                whole(rows), whole(rows), whole((1, width)), whole((1, width)), whole(rows), whole(rows), whole(rows),
                whole(rows), column, column, column, column, column, column,
                tall,
                pl.BlockSpec((width, tile), lambda j, s: (0, steps + j)),
                tall,
                pl.BlockSpec((tile, width), lambda j, s: (j, 1)),
                table, table, table, table,
            ],
            out_specs=[
                whole(rows), tall, tall, tall,
                pl.BlockSpec((tile, width), lambda j, s: (j, 0)),
                whole((1, width)), whole((1, width)),
            ],
            scratch_shapes=[pltpu.VMEM(rows, F32), pltpu.VMEM(rows, BF16), pltpu.VMEM(rows, F32)],
        ),
        out_shape=[
            jax.ShapeDtypeStruct(rows, BF16),
            *[jax.ShapeDtypeStruct((width, width), BF16)] * 4,
            jax.ShapeDtypeStruct((1, width), F32), jax.ShapeDtypeStruct((1, width), F32),
        ],
        compiler_params=pltpu.CompilerParams(vmem_limit_bytes=VMEM_BYTES),
        name="mix_back",
    )(facts, x, cot, g1, g2, mid, own, sib, normed, gated, *kept, half0, half0, half1, half1, *tables)


def ffn_kernel(nf_ref, gf_ref, wg_ref, wu_ref, wd_ref, h_ref, dg_ref, du_ref, gd_ref):
    nf, gf = nf_ref[...], gf_ref[...]
    g = mm(nf, wg_ref[...])
    u = mm(nf, wu_ref[...])
    dh = mm_nt(gf, wd_ref[...])
    sig = 1.0 / (1.0 + jnp.exp(-g))
    silu = g * sig
    h = (silu * u).astype(BF16)
    h_ref[...] = h
    du_ref[...] = (dh * silu).astype(BF16)
    dg_ref[...] = (dh * u * (sig * (1.0 + g * (1.0 - sig)))).astype(BF16)
    gd_ref[...] = mm_tn(h, gf).astype(BF16)


def ffn(nf, gf, wg, wu, wd):
    tok, width = nf.shape
    units = wg.shape[1]
    tile = 256
    whole = pl.BlockSpec((tok, width), lambda j: (0, 0))
    tall = pl.BlockSpec((width, tile), lambda j: (0, j))
    flat = pl.BlockSpec((tile, width), lambda j: (j, 0))
    column = pl.BlockSpec((tok, tile), lambda j: (0, j))
    return pl.pallas_call(
        ffn_kernel,
        grid=(units // tile,),
        in_specs=[whole, whole, tall, tall, flat],
        out_specs=[column, column, column, flat],
        out_shape=[
            *[jax.ShapeDtypeStruct((tok, units), BF16)] * 3,
            jax.ShapeDtypeStruct((units, width), BF16),
        ],
        compiler_params=pltpu.CompilerParams(vmem_limit_bytes=VMEM_BYTES),
        name="ffn",
    )(nf, gf, wg, wu, wd)


class Links:
    def __init__(self):
        self.wide = lax.axis_size("wide")
        self.narrow = lax.axis_size("narrow")
        self.core = lax.axis_index("wide") % 2
        self.outer = self.wide // 2
        place = lax.axis_index("wide")
        spot = lax.axis_index("narrow")
        self.bits = []
        span = self.outer
        while span > 1:
            span //= 2
            self.bits.append(("wide", self.wide, 2 * span, (place // (2 * span)) % 2))
        self.outer_bits = len(self.bits)
        span = self.narrow
        while span > 1:
            span //= 2
            self.bits.append(("narrow", self.narrow, span, (spot // span) % 2))

    def chain(self, turn):
        rest = list(range(1, len(self.bits)))
        turn %= len(rest)
        return [0] + rest[turn:] + rest[:turn]

    def swap_core(self, values):
        return lax.ppermute(values, "wide", [(i, i ^ 1) for i in range(self.wide)])

    def exchange(self, values, p):
        axis, size, stride, _ = self.bits[p]
        return lax.ppermute(values, axis, [(i, i ^ stride) for i in range(size)])

    def split(self, p, have, middle, rows):
        before = 2 ** sum(q < p for q in have)
        after = 2 ** sum(q > p for q in have)
        if p < self.outer_bits:
            return before, after * middle * rows
        return before * middle, after * rows

    def gather_step(self, block, p, have, middle):
        rows = block.shape[0] // (middle * 2 ** len(have))
        before, after = self.split(p, have, middle, rows)
        mine = block.reshape(before, 1, after, block.shape[1])
        other = self.exchange(block, p).reshape(mine.shape)
        bit = self.bits[p][3]
        both = jnp.where(
            bit == 0, jnp.concatenate([mine, other], axis=1), jnp.concatenate([other, mine], axis=1)
        )
        return both.reshape(-1, block.shape[1])

    def scatter_step(self, block, p, have, middle):
        rows = block.shape[0] // (middle * 2 ** len(have))
        before, after = self.split(p, have - {p}, middle, rows)
        parts = block.reshape(before, 2, after, block.shape[1])
        bit = self.bits[p][3]
        sent = lax.dynamic_index_in_dim(parts, 1 - bit, 1, keepdims=False)
        kept = lax.dynamic_index_in_dim(parts, bit, 1, keepdims=False)
        sent = sent.reshape(-1, block.shape[1])
        total = kept.reshape(sent.shape).astype(F32) + self.exchange(sent, p).astype(F32)
        return total.astype(BF16)

    def gather(self, blocks, chains, middles):
        have = [set() for _ in blocks]
        for k in range(len(self.bits)):
            for i, chain in enumerate(chains):
                blocks[i] = self.gather_step(blocks[i], chain[k], have[i], middles[i])
                have[i] = have[i] | {chain[k]}
        return blocks

    def scatter(self, blocks, chains, middles):
        have = [set(chain) for chain in chains]
        for k in reversed(range(len(self.bits))):
            for i, chain in enumerate(chains):
                blocks[i] = self.scatter_step(blocks[i], chain[k], have[i], middles[i])
                have[i] = have[i] - {chain[k]}
        return blocks


def unit_order(width, chunk):
    columns = np.arange(width)
    pairs = width // (2 * chunk)
    source = np.concatenate(
        [np.concatenate([(2 * i + core) * chunk + np.arange(chunk) for i in range(pairs)]) for core in range(2)]
    )
    return (columns[:, None] == source[None, :]).astype(ml_dtypes.bfloat16)


def on_device(tokens, cotangent, w_in, w_out, w_gu, w_down, gain_mix, gain_ffn, buckets, lengths):
    links = Links()
    core = links.core
    tok, width = tokens.shape
    rows = w_in.shape[0]
    ff = w_gu.shape[1] // 2
    units = ff // 2
    lanes = 128
    half_width = 2 * width + lanes

    tables = [jnp.asarray(t) for t in transform_tables(tok)]
    order = jnp.asarray(unit_order(width, ff // links.wide))
    facts = jnp.concatenate([buckets, lengths[0]]).astype(jnp.int32)

    gains = jnp.pad(jnp.stack([gain_mix, gain_ffn], axis=1), ((0, 0), (0, lanes - 2)))
    half0 = jnp.concatenate([w_in[:, : 2 * width], gains], axis=1)
    half1 = jnp.concatenate([w_in[:, 2 * width :], w_out, gains], axis=1)
    sorted_gu = mm(w_gu.reshape(rows * (2 * ff // width), width), order).astype(BF16)
    sorted_gu = sorted_gu.reshape(rows, 2 * ff // width, 2, width // 2)
    gu0 = sorted_gu[:, :, 0].reshape(rows, 2 * units)
    gu1 = sorted_gu[:, :, 1].reshape(rows, 2 * units)
    pack0 = jnp.concatenate([half0, gu0], axis=1)
    pack1 = jnp.concatenate([half1, gu1], axis=1)
    mine = jnp.where(core == 0, pack0, pack1)
    other = links.swap_core(jnp.where(core == 0, pack1, pack0))
    block = jnp.where(
        core == 0, jnp.concatenate([mine, other], axis=0), jnp.concatenate([other, mine], axis=0)
    )
    cuts = (0, 512, 1024, half_width)
    mixer_parts = [block[:, a:b] for a, b in zip(cuts[:-1], cuts[1:])]
    mixer_chains = [links.chain(i) for i in range(3)]
    mixer_parts = links.gather(mixer_parts, mixer_chains, [2, 2, 2])
    mixer_half = jnp.concatenate(mixer_parts, axis=1)
    mixer_sib = links.swap_core(mixer_half)
    full0 = jnp.where(core == 0, mixer_half, mixer_sib)
    full1 = jnp.where(core == 0, mixer_sib, mixer_half)
    gain_rows = full0[:, 2 * width : 2 * width + 2].astype(F32).T
    g1, g2 = gain_rows[0:1], gain_rows[1:2]

    ffn_parts = [block[:, half_width : half_width + units], block[:, half_width + units :], w_down]
    ffn_chains = [links.chain(i) for i in range(3)]
    middles = [2, 2, 1]
    wg, wu, wd = links.gather(ffn_parts, ffn_chains, middles)

    normed, gated, mid, nf, t, s, mixed, kf, vf, norms = mix_forward(facts, tokens, g1, g2, full0, full1, tables)

    mask = pad_mask(facts[0], [facts[1 + i] for i in range(ROW_SLOTS)], (tok, 1), tok)
    gf = (cotangent.astype(F32) * mask).astype(BF16)
    gf2 = jnp.concatenate([gf, links.swap_core(gf)], axis=0)
    nf2 = jnp.concatenate([nf, links.swap_core(nf)], axis=0)
    h, dg, du, grad_down = ffn(nf2, gf2, wg, wu, wd)
    grad_gate = mm_tn(nf2, dg).astype(BF16)
    grad_up = mm_tn(nf2, du).astype(BF16)
    dnf = mm_nt(dg, wg) + mm_nt(du, wu)
    dnf_sib = links.swap_core(dnf[tok:].astype(BF16))
    out = mm(h, wd)
    out_sib = links.swap_core(out[tok:].astype(BF16))
    layer_out = ((mid + out[:tok] + out_sib.astype(F32)) * mask).astype(BF16)

    sum_gate, sum_up, sum_down = links.scatter([grad_gate, grad_up, grad_down], ffn_chains, middles)

    grad_tokens, ga, gc, gv, go, gain1, gain2 = mix_back(
        facts, tokens, cotangent, g1, g2, mid, dnf[:tok], dnf_sib, normed, gated, (t, s, mixed, kf, vf), full0, full1, tables
    )
    devices = links.wide * links.narrow
    extras = jnp.concatenate([gain1, gain2, norms * (1.0 / devices)], axis=0).T.astype(BF16)
    extras = jnp.pad(extras, ((0, 0), (0, lanes - 3)))
    grad0 = jnp.concatenate([ga, gc, extras], axis=1)
    grad1 = jnp.concatenate([gv, go, extras * 0], axis=1)
    kept = jnp.where(core == 0, grad0, grad1)
    got = links.swap_core(jnp.where(core == 0, grad1, grad0))
    grad_half = (kept.astype(F32) + got.astype(F32)).astype(BF16)
    grad_parts = [grad_half[:, a:b] for a, b in zip(cuts[:-1], cuts[1:])]
    grad_parts = links.scatter(grad_parts, mixer_chains, [2, 2, 2])

    final = jnp.concatenate([*grad_parts, sum_gate, sum_up], axis=1).reshape(2, rows, half_width + 2 * units)
    own = lax.dynamic_index_in_dim(final, core, 0, keepdims=False)
    far = links.swap_core(lax.dynamic_index_in_dim(final, 1 - core, 0, keepdims=False))
    first = jnp.where(core == 0, own, far)
    second = jnp.where(core == 0, far, own)
    grad_w_in = jnp.concatenate([first[:, : 2 * width], second[:, :width]], axis=1).astype(F32)
    grad_w_out = second[:, width : 2 * width].astype(F32)
    extra = first[:, 2 * width : half_width].astype(F32).T
    groups = 2 * ff // width
    gu_pair = jnp.concatenate(
        [
            first[:, half_width:].reshape(rows, groups, width // 2),
            second[:, half_width:].reshape(rows, groups, width // 2),
        ],
        axis=2,
    )
    grad_w_gu = mm_nt(gu_pair.reshape(rows * groups, width), order).reshape(rows, 2 * ff)
    return (
        layer_out, grad_tokens, grad_w_in, grad_w_out, grad_w_gu, sum_down.astype(F32), extra[0], extra[1], extra[2],
    )


def solution(mesh):
    both = ("wide", "narrow")
    flat, tall = P(both), P(both, None)
    return jax.shard_map(
        on_device,
        mesh=mesh,
        in_specs=(tall, tall, tall, tall, tall, tall, flat, flat, flat, tall),
        out_specs=(tall, tall, tall, tall, tall, tall, flat, flat, flat),
        check_vma=False,
    )
```

```python
import functools

import jax
import jax.numpy as jnp
import ml_dtypes
import numpy as np
from jax import lax
from jax.experimental import pallas as pl
from jax.experimental.pallas import tpu as pltpu
from jax.sharding import PartitionSpec as P

F32 = jnp.float32
BF16 = jnp.bfloat16
ROW_SLOTS = 4
BUCKETS = 3
VMEM_BYTES = 56 * 1024 * 1024


def transform_tables(tok_count):
    highs, lows = [], []
    for bucket in range(BUCKETS):
        rows = ROW_SLOTS >> bucket
        length = tok_count // rows
        half = length // 2
        angle = 2.0 * np.pi * (np.arange(half)[:, None] * np.arange(length)[None, :] % length) / length
        real = np.cos(angle) * np.sqrt(2.0 / length)
        imag = -np.sin(angle) * np.sqrt(2.0 / length)
        real[0] = 1.0 / np.sqrt(length)
        imag[0] = (1.0 - 2.0 * (np.arange(length) % 2)) / np.sqrt(length)
        table = np.zeros((tok_count, tok_count))
        for row in range(rows):
            at = slice(row * length, (row + 1) * length)
            table[row * half : (row + 1) * half, at] = real
            table[tok_count // 2 + row * half : tok_count // 2 + (row + 1) * half, at] = imag
        high = table.astype(ml_dtypes.bfloat16)
        highs.append(high)
        lows.append((table - high.astype(np.float64)).astype(ml_dtypes.bfloat16))
    high, low = np.stack(highs), np.stack(lows)
    return high, low, np.ascontiguousarray(high.transpose(0, 2, 1)), np.ascontiguousarray(low.transpose(0, 2, 1))


def mm(left, right):
    return jnp.dot(left, right, preferred_element_type=F32)


def mm_nt(left, right):
    return lax.dot_general(left, right, (((1,), (1,)), ((), ())), preferred_element_type=F32)


def mm_tn(left, right):
    return lax.dot_general(left, right, (((0,), (0,)), ((), ())), preferred_element_type=F32)


def transform(high, low, values):
    top = values.astype(BF16)
    rest = (values - top.astype(F32)).astype(BF16)
    return mm(high, top) + (mm(high, rest) + mm(low, top))


def bin_facts(bucket, shape, tok_count):
    half = lax.shift_left(jnp.int32(tok_count // (2 * ROW_SLOTS)), bucket)
    spot = lax.broadcasted_iota(jnp.int32, shape, 0)
    edge = (spot & (half - 1)) == 0
    length = (2 * half).astype(F32)
    scale = jnp.where(edge, jnp.sqrt(length), jnp.sqrt(0.5 * length))
    return edge, scale


def pad_mask(bucket, lengths, shape, tok_count):
    quarter = tok_count // ROW_SLOTS
    shift = (quarter.bit_length() - 1) + bucket
    spot = lax.broadcasted_iota(jnp.int32, shape, 0)
    slot = lax.shift_right_logical(spot, jnp.broadcast_to(shift, shape))
    within = spot - lax.shift_left(slot, jnp.broadcast_to(shift, shape))
    length = jnp.where(
        slot == 0, lengths[0], jnp.where(slot == 1, lengths[1], jnp.where(slot == 2, lengths[2], lengths[3]))
    )
    return (within < length).astype(F32)


def row_sums(bucket, values, tok_count):
    quarter = tok_count // ROW_SLOTS
    s = [jnp.sum(values[i * quarter : (i + 1) * quarter], axis=0, keepdims=True) for i in range(ROW_SLOTS)]
    left, right = s[0] + s[1], s[2] + s[3]
    whole = left + right
    pairs = (left, left, right, right)
    return [jnp.where(bucket == 0, s[i], jnp.where(bucket == 1, pairs[i], whole)) for i in range(ROW_SLOTS)]


def over_rows(parts, tok_count):
    quarter = tok_count // ROW_SLOTS
    return jnp.concatenate([jnp.broadcast_to(p, (quarter, p.shape[1])) for p in parts], axis=0)


TILES = 3
LANES = 128
ANY = pl.BlockSpec(memory_space=pl.ANY)
INSIDE = pl.BlockSpec(memory_space=pltpu.VMEM)


class Weights:
    def __init__(self, core, carried, sibling, halves, sems):
        self.core, self.carried, self.sibling, self.halves, self.sems = core, carried, sibling, halves, sems

    def copies(self, i, first, second):
        spot = self.halves[0][i]
        at = (slice(None), pl.ds(i * self.halves[0][0].shape[1], spot.shape[1]))
        return (
            pltpu.make_async_copy(first.at[at], spot, self.sems.at[0, i]),
            pltpu.make_async_copy(second.at[at], self.halves[1][i], self.sems.at[1, i]),
        )

    def start(self, order):
        @pl.when(self.core == 0)
        def _():
            for i in order:
                for copy in self.copies(i, self.carried, self.sibling):
                    copy.start()

        @pl.when(self.core != 0)
        def _():
            for i in order:
                for copy in self.copies(i, self.sibling, self.carried):
                    copy.start()

    def wait(self, i):
        for copy in self.copies(i, self.carried, self.sibling):
            copy.wait()


def load_tables(bucket, tables, spots, sems):
    copies = [pltpu.make_async_copy(t.at[bucket], s, sems.at[i]) for i, (t, s) in enumerate(zip(tables, spots))]
    for copy in copies:
        copy.start()
    return copies


def mix_forward_kernel(facts, x_ref, *refs):
    carried, sibling, tables = refs[0], refs[1], refs[2:6]
    (
        normed_ref, gated_ref, mid_ref, nf_ref, norm_ref, gain_ref, t_out, s_out, mix_out, kf_out, vf_out,
        first, second, spots, kept, w_sems, t_sems, k_sems,
    ) = refs[6:]
    tok_count, width = x_ref.shape
    tile = width // TILES
    bucket = facts[0]
    lengths = [facts[1 + i] for i in range(ROW_SLOTS)]
    weights = Weights(facts[1 + ROW_SLOTS], carried, sibling, (first, second), w_sems)
    weights.start([TILES - 1, *range(TILES - 1)])
    copies = load_tables(bucket, tables, spots, t_sems)
    x = x_ref[...].astype(F32)
    r = lax.rsqrt(jnp.mean(x * x, axis=-1, keepdims=True) + 1e-06)
    scaled = x * r
    mask = pad_mask(bucket, lengths, (tok_count, tile), tok_count)
    weights.wait(TILES - 1)
    gains = first[TILES - 1][:, 2 * tile :].astype(F32).T[:8]
    gain_ref[...] = gains
    normed = (scaled * gains[0:1]).astype(BF16)
    normed_ref[...] = normed
    edge, scale = bin_facts(bucket, (tok_count // 2, tile), tok_count)
    half = tok_count // 2
    outs = (t_out, s_out, mix_out, kf_out, vf_out)
    stores = []
    for n, j in enumerate([TILES - 1, *range(TILES - 1)]):
        if n > 0:
            weights.wait(j)
        at = slice(j * tile, (j + 1) * tile)
        a = mm(normed, first[j][:, :tile])
        c = mm(normed, first[j][:, tile : 2 * tile])
        v = mm(normed, second[j][:, :tile]) * mask
        t = jnp.tanh(a) * mask
        norms = [jnp.sqrt(s + 1e-05) for s in row_sums(bucket, t * t, tok_count)]
        norm_ref[:, at] = (norms[0] + norms[1] + norms[2] + norms[3]) * (1.0 / ROW_SLOTS)
        unit = t * over_rows([1.0 / n for n in norms], tok_count)
        if n == 0:
            for copy in copies:
                copy.wait()
        kf = transform(spots[0][...], spots[1][...], unit)
        vf = transform(spots[0][...], spots[1][...], v)
        kr, ki, vr, vi = kf[:half], kf[half:], vf[:half], vf[half:]
        kivi = ki * vi
        pr = (kr * vr - jnp.where(edge, 0.0, kivi)) * scale
        pi = jnp.where(edge, kivi, kr * vi + ki * vr) * scale
        mixed = transform(spots[2][...], spots[3][...], jnp.concatenate([pr, pi], axis=0))
        sig = 1.0 / (1.0 + jnp.exp(-c))
        gated_ref[:, at] = (mixed * sig * mask).astype(BF16)
        for i, value in enumerate((t, sig, mixed, kf, vf)):
            kept[i][j] = value.astype(kept[i].dtype)
            store = pltpu.make_async_copy(kept[i].at[j], outs[i].at[j], k_sems.at[i, j])
            store.start()
            stores.append(store)
    gated = gated_ref[...]
    for i in range(TILES):
        at = slice(i * tile, (i + 1) * tile)
        mid_ref[:, at] = x_ref[:, at].astype(F32) + mm(gated, second[i][:, tile : 2 * tile])
    mid = mid_ref[...]
    r = lax.rsqrt(jnp.mean(mid * mid, axis=-1, keepdims=True) + 1e-06)
    nf_ref[...] = (mid * r * gains[1:2]).astype(BF16)
    for store in stores:
        store.wait()


def table_spots(tok):
    return tuple(pltpu.VMEM((tok, tok), BF16) for _ in range(4))


def half_spots(width):
    tile = width // TILES
    shapes = [(width, 2 * tile)] * (TILES - 1) + [(width, 2 * tile + LANES)]
    return tuple(pltpu.VMEM(shape, BF16) for shape in shapes)


def mix_forward(facts, x, carried, sibling, tables):
    tok, width = x.shape
    tile = width // TILES
    kinds = (F32, F32, BF16, BF16, BF16)
    return pl.pallas_call(
        mix_forward_kernel,
        in_specs=[pl.BlockSpec(memory_space=pltpu.SMEM), INSIDE, *[ANY] * 6],
        out_specs=[*[INSIDE] * 6, *[ANY] * 5],
        out_shape=[
            jax.ShapeDtypeStruct((tok, width), BF16), jax.ShapeDtypeStruct((tok, width), BF16),
            jax.ShapeDtypeStruct((tok, width), F32), jax.ShapeDtypeStruct((tok, width), BF16),
            jax.ShapeDtypeStruct((1, width), F32), jax.ShapeDtypeStruct((8, width), F32),
            *[jax.ShapeDtypeStruct((TILES, tok, tile), kind) for kind in kinds],
        ],
        scratch_shapes=[
            half_spots(width), half_spots(width), table_spots(tok),
            tuple(pltpu.VMEM((TILES, tok, tile), kind) for kind in kinds),
            pltpu.SemaphoreType.DMA((2, TILES)), pltpu.SemaphoreType.DMA((4,)), pltpu.SemaphoreType.DMA((5, TILES)),
        ],
        compiler_params=pltpu.CompilerParams(vmem_limit_bytes=VMEM_BYTES),
        name="mix_forward",
    )(facts, x, carried, sibling, *tables)


def rms_back(values, gain, grad):
    r = lax.rsqrt(jnp.mean(values * values, axis=-1, keepdims=True) + 1e-06)
    scaled = values * r
    inner = grad * gain
    dot = jnp.mean(inner * scaled, axis=-1, keepdims=True)
    return r * (inner - scaled * dot), grad * scaled


def mix_back_kernel(facts, x_ref, cot_ref, gain_ref, mid_ref, own_ref, sib_ref, normed_ref, gated_ref, norm_ref, *refs):
    residuals, refs = refs[:5], refs[5:]
    (carried, sibling), tables, (tok_ref, keep, send), refs = refs[:2], refs[2:6], refs[6:9], refs[9:]
    first, second, spots, held, gm_ref, acc_ref, w_sems, t_sems, k_sems = refs
    tok_count, width = x_ref.shape
    tile = width // TILES
    half = tok_count // 2
    bucket = facts[0]
    lengths = [facts[1 + i] for i in range(ROW_SLOTS)]
    core = facts[1 + ROW_SLOTS]
    weights = Weights(core, carried, sibling, (first, second), w_sems)
    weights.start(range(TILES))
    copies = load_tables(bucket, tables, spots, t_sems)
    loads = [
        [pltpu.make_async_copy(residuals[i].at[j], held[i].at[j], k_sems.at[i, j]) for i in range(5)]
        for j in range(TILES)
    ]
    for group in loads:
        for load in group:
            load.start()
    outer = cot_ref[...].astype(F32) * pad_mask(bucket, lengths, cot_ref.shape, tok_count)
    grad = own_ref[...] + sib_ref[...].astype(F32)
    back, terms = rms_back(mid_ref[...], gain_ref[1:2, :], grad)
    gain2 = jnp.sum(terms, axis=0, keepdims=True)
    grad_mid = outer + back
    gm_ref[...] = grad_mid
    low = grad_mid.astype(BF16)
    normed, gated = normed_ref[...], gated_ref[...]
    mask = pad_mask(bucket, lengths, (tok_count, tile), tok_count)
    edge, scale = bin_facts(bucket, (half, tile), tok_count)
    for i in range(TILES):
        weights.wait(i)
    for copy in copies:
        copy.wait()
    for j in range(TILES):
        at = slice(j * tile, (j + 1) * tile)
        grad_gated = sum(
            mm_nt(low[:, i * tile : (i + 1) * tile], second[i][at, tile : 2 * tile]) for i in range(TILES)
        )
        go = mm_tn(gated, low[:, at])
        grad_gated = grad_gated * mask
        for load in loads[j]:
            load.wait()
        t, sig, mixed, kf, vf = (h[j].astype(F32) for h in held)
        dc = (grad_gated * mixed * (sig * (1.0 - sig))).astype(BF16)
        df = transform(spots[0][...], spots[1][...], grad_gated * sig)
        kr, ki, vr, vi = kf[:half], kf[half:], vf[:half], vf[half:]
        dr, di = df[:half] * scale, df[half:] * scale
        divi, diki = di * vi, di * ki
        dkr = dr * vr + jnp.where(edge, 0.0, divi)
        dki = jnp.where(edge, divi, di * vr - dr * vi)
        dvr = dr * kr + jnp.where(edge, 0.0, diki)
        dvi = jnp.where(edge, diki, di * kr - dr * ki)
        du = transform(spots[2][...], spots[3][...], jnp.concatenate([dkr, dki], axis=0))
        dv = (transform(spots[2][...], spots[3][...], jnp.concatenate([dvr, dvi], axis=0)) * mask).astype(BF16)
        inverse = [lax.rsqrt(s + 1e-05) for s in row_sums(bucket, t * t, tok_count)]
        dots = row_sums(bucket, du * t, tok_count)
        coupling = [d * i * i * i for d, i in zip(dots, inverse)]
        dt = du * over_rows(inverse, tok_count) - t * over_rows(coupling, tok_count)
        da = (dt * mask * (1.0 - t * t)).astype(BF16)
        pairs = ((mm_tn(normed, da), mm_tn(normed, dv)), (mm_tn(normed, dc), go))
        for i, (one, two) in enumerate(pairs):
            to = slice((2 * j + i) * tile, (2 * j + i + 1) * tile)
            keep[:, to] = jnp.where(core == 0, one, two).astype(BF16)
            send[:, to] = jnp.where(core == 0, two, one).astype(BF16)
        part = (
            mm_nt(da, first[j][:, :tile]) + mm_nt(dc, first[j][:, tile : 2 * tile]) + mm_nt(dv, second[j][:, :tile])
        )
        if j == 0:
            acc_ref[...] = part
        else:
            acc_ref[...] += part
    back, terms = rms_back(x_ref[...].astype(F32), gain_ref[0:1, :], acc_ref[...])
    gain1 = jnp.sum(terms, axis=0, keepdims=True)
    tok_ref[...] = (gm_ref[...] + back).astype(BF16)
    extras = jnp.concatenate([gain1, gain2, norm_ref[...], jnp.zeros((LANES - 3, width), F32)], axis=0).T
    keep[:, 2 * width :] = jnp.where(core == 0, extras, 0.0).astype(BF16)
    send[:, 2 * width :] = jnp.where(core == 0, 0.0, extras).astype(BF16)


def mix_back(facts, x, cot, gains, mid, own, sib, normed, gated, norms, kept, carried, sibling, tables):
    tok, width = x.shape
    tile = width // TILES
    part = jax.ShapeDtypeStruct((width, 2 * width + LANES), BF16)
    assert TILES * tile == width
    return pl.pallas_call(
        mix_back_kernel,
        grid=(1,),
        in_specs=[
            pl.BlockSpec(memory_space=pltpu.SMEM), *[INSIDE] * 4,
            pl.BlockSpec((tok, width), lambda i: (0, 0)), *[INSIDE] * 4, *[ANY] * (5 + 2 + 4),
        ],
        out_specs=[INSIDE] * 3,
        out_shape=[jax.ShapeDtypeStruct((tok, width), BF16), part, part],
        scratch_shapes=[
            half_spots(width), half_spots(width), table_spots(tok),
            tuple(pltpu.VMEM(k.shape, k.dtype) for k in kept),
            pltpu.VMEM((tok, width), F32), pltpu.VMEM((tok, width), F32),
            pltpu.SemaphoreType.DMA((2, TILES)), pltpu.SemaphoreType.DMA((4,)), pltpu.SemaphoreType.DMA((5, TILES)),
        ],
        compiler_params=pltpu.CompilerParams(vmem_limit_bytes=VMEM_BYTES),
        name="mix_back",
    )(facts, x, cot, gains, mid, own, sib, normed, gated, norms, *kept, carried, sibling, *tables)


def ffn_kernel(
    nfo_ref, nfs_ref, gfo_ref, gfs_ref, wg_ref, wu_ref, wd_ref, nf_ref, h_ref, dg_ref, du_ref, gd_ref, gf_ref
):
    tok = nfo_ref.shape[0]

    @pl.when(pl.program_id(0) == 0)
    def _():
        nf_ref[:tok] = nfo_ref[...]
        nf_ref[tok:] = nfs_ref[...]
        gf_ref[:tok] = gfo_ref[...]
        gf_ref[tok:] = gfs_ref[...]

    nf, gf = nf_ref[...], gf_ref[...]
    g = mm(nf, wg_ref[...])
    u = mm(nf, wu_ref[...])
    dh = mm_nt(gf, wd_ref[...])
    sig = 1.0 / (1.0 + jnp.exp(-g))
    silu = g * sig
    h = (silu * u).astype(BF16)
    h_ref[...] = h
    du_ref[...] = (dh * silu).astype(BF16)
    dg_ref[...] = (dh * u * (sig * (1.0 + g * (1.0 - sig)))).astype(BF16)
    gd_ref[...] = mm_tn(h, gf).astype(BF16)


def ffn(nf_own, nf_sib, gf_own, gf_sib, wg, wu, wd):
    tok, width = nf_own.shape
    units = wg.shape[1]
    tile = 256
    whole = pl.BlockSpec((tok, width), lambda j: (0, 0))
    tall = pl.BlockSpec((width, tile), lambda j: (0, j))
    flat = pl.BlockSpec((tile, width), lambda j: (j, 0))
    column = pl.BlockSpec((2 * tok, tile), lambda j: (0, j))
    return pl.pallas_call(
        ffn_kernel,
        grid=(units // tile,),
        in_specs=[whole, whole, whole, whole, tall, tall, flat],
        out_specs=[pl.BlockSpec((2 * tok, width), lambda j: (0, 0)), column, column, column, flat],
        out_shape=[
            jax.ShapeDtypeStruct((2 * tok, width), BF16),
            *[jax.ShapeDtypeStruct((2 * tok, units), BF16)] * 3,
            jax.ShapeDtypeStruct((units, width), BF16),
        ],
        scratch_shapes=[pltpu.VMEM((2 * tok, width), BF16)],
        compiler_params=pltpu.CompilerParams(vmem_limit_bytes=VMEM_BYTES),
        name="ffn",
    )(nf_own, nf_sib, gf_own, gf_sib, wg, wu, wd)


def pack_mixer_kernel(facts, in_ref, out_ref, gain_ref, mine_ref, send_ref):
    core = facts[1 + ROW_SLOTS]
    width = out_ref.shape[1]
    tile = width // TILES
    for j in range(TILES):
        at = slice(j * tile, (j + 1) * tile)
        pairs = (
            (in_ref[:, j * tile : (j + 1) * tile], in_ref[:, 2 * width + j * tile : 2 * width + (j + 1) * tile]),
            (in_ref[:, width + j * tile : width + (j + 1) * tile], out_ref[:, at]),
        )
        for i, (one, two) in enumerate(pairs):
            to = slice((2 * j + i) * tile, (2 * j + i + 1) * tile)
            mine_ref[:, to] = jnp.where(core == 0, one, two)
            send_ref[:, to] = jnp.where(core == 0, two, one)
    mine_ref[:, 2 * width :] = gain_ref[...]
    send_ref[:, 2 * width :] = gain_ref[...]


def pack_mixer(facts, w_in, w_out, gains):
    rows, width = w_out.shape
    return pl.pallas_call(
        pack_mixer_kernel,
        in_specs=[pl.BlockSpec(memory_space=pltpu.SMEM), INSIDE, INSIDE, INSIDE],
        out_specs=[INSIDE, INSIDE],
        out_shape=[jax.ShapeDtypeStruct((rows, 2 * width + LANES), BF16)] * 2,
        name="pack_mixer",
    )(facts, w_in, w_out, gains)


def pack_units_kernel(facts, gu_ref, order_ref, mine_ref, send_ref, stack_ref):
    core = facts[1 + ROW_SLOTS]
    rows = gu_ref.shape[0]
    width = order_ref.shape[0]
    half = width // 2
    groups = gu_ref.shape[1] // width
    pitch = stack_ref.shape[0] // groups
    for i in range(groups):
        stack_ref[i * pitch : i * pitch + rows] = gu_ref[:, i * width : (i + 1) * width].astype(F32)
    sorted_rows = mm(stack_ref[...].astype(BF16), order_ref[...])
    for i in range(groups):
        block = sorted_rows[i * pitch : i * pitch + rows]
        to = slice(i * half, (i + 1) * half)
        mine_ref[:, to] = jnp.where(core == 0, block[:, :half], block[:, half:]).astype(BF16)
        send_ref[:, to] = jnp.where(core == 0, block[:, half:], block[:, :half]).astype(BF16)


def pack_units(facts, w_gu, order):
    rows, columns = w_gu.shape
    width = order.shape[0]
    pitch = -(-rows // 8) * 8
    return pl.pallas_call(
        pack_units_kernel,
        in_specs=[pl.BlockSpec(memory_space=pltpu.SMEM), INSIDE, INSIDE],
        out_specs=[INSIDE, INSIDE],
        out_shape=[jax.ShapeDtypeStruct((rows, columns // 2), BF16)] * 2,
        scratch_shapes=[pltpu.VMEM((columns // width * pitch, width), F32)],
        name="pack_units",
    )(facts, w_gu, order)


class Links:
    def __init__(self):
        self.outer = lax.axis_size("outer")
        self.narrow = lax.axis_size("narrow")
        self.core = lax.axis_index("core")
        self.bits = []
        for axis, size in (("outer", self.outer), ("narrow", self.narrow)):
            spot = lax.axis_index(axis)
            span = size
            while span > 1:
                span //= 2
                self.bits.append((axis, size, span, (spot // span) % 2))
        self.outer_bits = sum(bit[0] == "outer" for bit in self.bits)

    def chain(self, turn):
        rest = list(range(1, len(self.bits)))
        turn %= len(rest)
        return [0] + rest[turn:] + rest[:turn]

    def swap_core(self, values):
        return lax.ppermute(values, "core", [(0, 1), (1, 0)])

    def exchange(self, values, p):
        axis, size, stride, _ = self.bits[p]
        return lax.ppermute(values, axis, [(i, i ^ stride) for i in range(size)])

    def split(self, p, have, middle, rows):
        before = 2 ** sum(q < p for q in have)
        after = 2 ** sum(q > p for q in have)
        if p < self.outer_bits:
            return before, after * middle * rows
        return before * middle, after * rows

    def gather_step(self, block, p, have, middle):
        rows = block.shape[0] // (middle * 2 ** len(have))
        before, after = self.split(p, have, middle, rows)
        mine = block.reshape(before, 1, after, block.shape[1])
        other = self.exchange(block, p).reshape(mine.shape)
        bit = self.bits[p][3]
        side = lax.broadcasted_iota(jnp.int32, (1, 2, 1, 1), 1)
        both = jnp.where(side == bit, mine, other)
        return both.reshape(-1, block.shape[1])

    def scatter_step(self, block, p, have, middle):
        rows = block.shape[0] // (middle * 2 ** len(have))
        before, after = self.split(p, have - {p}, middle, rows)
        parts = block.reshape(before, 2, after, block.shape[1])
        bit = self.bits[p][3]
        sent = lax.dynamic_index_in_dim(parts, 1 - bit, 1, keepdims=False)
        kept = lax.dynamic_index_in_dim(parts, bit, 1, keepdims=False)
        sent = sent.reshape(-1, block.shape[1])
        total = kept.reshape(sent.shape).astype(F32) + self.exchange(sent, p).astype(F32)
        return total.astype(BF16)

    def gather(self, blocks, chains, middles):
        have = [set() for _ in blocks]
        for k in range(len(self.bits)):
            for i, chain in enumerate(chains):
                blocks[i] = self.gather_step(blocks[i], chain[k], have[i], middles[i])
                have[i] = have[i] | {chain[k]}
        return blocks

    def scatter(self, blocks, chains, middles):
        have = [set(chain) for chain in chains]
        for k in reversed(range(len(self.bits))):
            for i, chain in enumerate(chains):
                blocks[i] = self.scatter_step(blocks[i], chain[k], have[i], middles[i])
                have[i] = have[i] - {chain[k]}
        return blocks


def unit_order(width, chunk):
    columns = np.arange(width)
    pairs = width // (2 * chunk)
    source = np.concatenate(
        [np.concatenate([(2 * i + core) * chunk + np.arange(chunk) for i in range(pairs)]) for core in range(2)]
    )
    return (columns[:, None] == source[None, :]).astype(ml_dtypes.bfloat16)


def on_device(tokens, cotangent, w_in, w_out, w_gu, w_down, gain_mix, gain_ffn, buckets, lengths):
    links = Links()
    core = links.core
    tok, width = tokens.shape
    rows = w_in.shape[0]
    ff = w_gu.shape[1] // 2
    units = ff // 2
    tile = width // TILES
    fence = lax.optimization_barrier

    tables = [jnp.asarray(t) for t in transform_tables(tok)]
    order = jnp.asarray(unit_order(width, ff // (2 * links.outer)))
    facts = jnp.concatenate([buckets, lengths[0], core[None]]).astype(jnp.int32)
    chains = [links.chain(i) for i in range(3)]
    middles = [2, 2, 1]
    count = len(links.bits)

    def grow(blocks, k, middles):
        return [links.gather_step(b, chain[k], set(chain[:k]), m) for b, chain, m in zip(blocks, chains, middles)]

    def shrink(blocks, k, middles):
        return [links.scatter_step(b, chain[k], set(chain[: k + 1]), m) for b, chain, m in zip(blocks, chains, middles)]

    def both_rows(mine, send):
        other = links.swap_core(send)
        side = lax.broadcasted_iota(jnp.int32, (2, 1, 1), 0)
        return jnp.where(side == core, mine[None], other[None]).reshape(2 * mine.shape[0], mine.shape[1])

    gains = jnp.pad(jnp.stack([gain_mix, gain_ffn], axis=1), ((0, 0), (0, LANES - 2)))
    mine, send = pack_mixer(facts, w_in, w_out, gains)
    mine_gu, send_gu = pack_units(facts, w_gu, order)
    mixer = links.gather_step(both_rows(mine, send), 0, set(), 2)
    gu = both_rows(mine_gu, send_gu)
    mixer, gu, wd = fence((mixer, gu, w_down))
    gu = links.gather_step(gu, 0, set(), 2)
    wd = links.gather_step(wd, 0, set(), 1)
    cuts = [2 * tile * j for j in range(TILES)] + [mine.shape[1]]
    parts = [mixer[:, a:b] for a, b in zip(cuts[:-1], cuts[1:])]
    weights = [gu[:, :units], gu[:, units:], wd]
    for k in range(1, count - 1):
        parts = grow(parts, k, [2] * TILES)
    parts, weights = fence((parts, weights))
    parts = grow(parts, count - 1, [2] * TILES)
    for k in range(1, count - 2):
        weights = grow(weights, k, middles)
    parts, weights = fence((parts, weights))
    parts = jnp.concatenate(parts, axis=1)
    siblings = links.swap_core(parts)
    weights = grow(weights, count - 2, middles)
    parts, siblings, weights = fence((parts, siblings, weights))
    wg, wu, wd = grow(weights, count - 1, middles)

    normed, gated, mid, nf, norms, gains, *kept = mix_forward(facts, tokens, parts, siblings, tables)

    mask = pad_mask(facts[0], [facts[1 + i] for i in range(ROW_SLOTS)], (tok, 1), tok)
    gf = (cotangent.astype(F32) * mask).astype(BF16)
    nf2, h, dg, du, grad_down = ffn(nf, links.swap_core(nf), gf, links.swap_core(gf), wg, wu, wd)
    back = mm_nt(dg, wg) + mm_nt(du, wu)
    back_sib = links.swap_core(back[tok:].astype(BF16))
    grads = [mm_tn(nf2, dg).astype(BF16), mm_tn(nf2, du).astype(BF16), grad_down]
    grads = shrink(grads, count - 1, middles)

    devices = 2 * links.outer * links.narrow
    grad_tokens, keep, send = mix_back(
        facts, tokens, cotangent, gains, mid, back, back_sib, normed, gated, norms * (1.0 / devices), kept,
        parts, siblings, tables,
    )
    grads, keep, send, h = fence((grads, keep, send, h))
    sums = (keep.astype(F32) + links.swap_core(send).astype(F32)).astype(BF16)
    grads = shrink(grads, count - 2, middles)
    grads, sums, h = fence((grads, sums, h))
    out = mm(h, wd)
    out_sib = links.swap_core(out[tok:].astype(BF16))
    layer_out = ((mid + out[:tok] + out_sib.astype(F32)) * mask).astype(BF16)
    for k in reversed(range(1, count - 2)):
        grads = shrink(grads, k, middles)
    sums = [sums[:, a:b] for a, b in zip(cuts[:-1], cuts[1:])]
    sums = shrink(sums, count - 1, [2] * TILES)
    grads, sums = fence((grads, sums))
    for k in reversed(range(1, count - 1)):
        sums = shrink(sums, k, [2] * TILES)
    sum_gate, sum_up, sum_down = shrink(grads, 0, middles)
    sums = links.scatter_step(jnp.concatenate(sums, axis=1), 0, {0}, 2)

    final = jnp.concatenate([sums, sum_gate, sum_up], axis=1).reshape(2, rows, mine.shape[1] + 2 * units)
    own = lax.dynamic_index_in_dim(final, core, 0, keepdims=False)
    far = links.swap_core(lax.dynamic_index_in_dim(final, 1 - core, 0, keepdims=False))
    one = jnp.where(core == 0, own, far)
    two = jnp.where(core == 0, far, own)
    columns = lambda half, offset: [half[:, (2 * j + offset) * tile : (2 * j + offset + 1) * tile] for j in range(TILES)]
    grad_w_in = jnp.concatenate(columns(one, 0) + columns(one, 1) + columns(two, 0), axis=1).astype(F32)
    grad_w_out = jnp.concatenate(columns(two, 1), axis=1).astype(F32)
    extra = one[:, 2 * width : 2 * width + LANES].astype(F32).T
    groups = 2 * ff // width
    pair = [half[:, mine.shape[1] :].reshape(rows, groups, width // 2) for half in (one, two)]
    grad_w_gu = mm_nt(jnp.concatenate(pair, axis=2).reshape(rows * groups, width), order).reshape(rows, 2 * ff)
    return (
        layer_out, grad_tokens, grad_w_in, grad_w_out, grad_w_gu, sum_down.astype(F32), extra[0], extra[1], extra[2],
    )


def solution(mesh):
    wide, narrow = mesh.devices.shape
    split = jax.sharding.Mesh(mesh.devices.reshape(wide // 2, 2, narrow), ("outer", "core", "narrow"))
    every = ("outer", "core", "narrow")
    flat, tall = P(every), P(every, None)
    return jax.shard_map(
        on_device,
        mesh=split,
        in_specs=(tall, tall, tall, tall, tall, tall, flat, flat, flat, tall),
        out_specs=(tall, tall, tall, tall, tall, tall, flat, flat, flat),
        check_vma=False,
    )
```

```python
import math

import jax
import jax.numpy as jnp
import ml_dtypes
import numpy as np
from jax import lax
from jax.experimental import pallas as pl
from jax.experimental.pallas import tpu as pltpu
from jax.sharding import PartitionSpec as P

F32 = jnp.float32
BF16 = jnp.bfloat16
ROW_SLOTS = 4
BUCKETS = 3
VMEM_BYTES = 56 * 1024 * 1024


def transform_tables(tok_count):
    highs, lows = [], []
    for bucket in range(BUCKETS):
        rows = ROW_SLOTS >> bucket
        length = tok_count // rows
        half = length // 2
        angle = 2.0 * np.pi * (np.arange(half)[:, None] * np.arange(length)[None, :] % length) / length
        real = np.cos(angle) * np.sqrt(2.0 / length)
        imag = -np.sin(angle) * np.sqrt(2.0 / length)
        real[0] = 1.0 / np.sqrt(length)
        imag[0] = (1.0 - 2.0 * (np.arange(length) % 2)) / np.sqrt(length)
        table = np.zeros((tok_count, tok_count))
        for row in range(rows):
            at = slice(row * length, (row + 1) * length)
            table[row * half : (row + 1) * half, at] = real
            table[tok_count // 2 + row * half : tok_count // 2 + (row + 1) * half, at] = imag
        high = table.astype(ml_dtypes.bfloat16)
        highs.append(high)
        lows.append((table - high.astype(np.float64)).astype(ml_dtypes.bfloat16))
    high, low = np.stack(highs), np.stack(lows)
    return high, low, np.ascontiguousarray(high.transpose(0, 2, 1)), np.ascontiguousarray(low.transpose(0, 2, 1))


def mm(left, right):
    return jnp.dot(left, right, preferred_element_type=F32)


def mm_nt(left, right):
    return lax.dot_general(left, right, (((1,), (1,)), ((), ())), preferred_element_type=F32)


def mm_tn(left, right):
    return lax.dot_general(left, right, (((0,), (0,)), ((), ())), preferred_element_type=F32)


def transform(high, low, values):
    top = values.astype(BF16)
    rest = (values - top.astype(F32)).astype(BF16)
    return mm(high, top) + (mm(high, rest) + mm(low, top))


def bin_facts(bucket, shape, tok_count):
    half = lax.shift_left(jnp.int32(tok_count // (2 * ROW_SLOTS)), bucket)
    spot = lax.broadcasted_iota(jnp.int32, shape, 0)
    edge = (spot & (half - 1)) == 0
    length = (2 * half).astype(F32)
    scale = jnp.where(edge, jnp.sqrt(length), jnp.sqrt(0.5 * length))
    return edge, scale


def pad_mask(bucket, lengths, shape, tok_count):
    quarter = tok_count // ROW_SLOTS
    shift = (quarter.bit_length() - 1) + bucket
    spot = lax.broadcasted_iota(jnp.int32, shape, 0)
    slot = lax.shift_right_logical(spot, jnp.broadcast_to(shift, shape))
    within = spot - lax.shift_left(slot, jnp.broadcast_to(shift, shape))
    length = jnp.where(
        slot == 0, lengths[0], jnp.where(slot == 1, lengths[1], jnp.where(slot == 2, lengths[2], lengths[3]))
    )
    return (within < length).astype(F32)


def row_sums(bucket, values, tok_count):
    quarter = tok_count // ROW_SLOTS
    s = [jnp.sum(values[i * quarter : (i + 1) * quarter], axis=0, keepdims=True) for i in range(ROW_SLOTS)]
    left, right = s[0] + s[1], s[2] + s[3]
    whole = left + right
    pairs = (left, left, right, right)
    return [jnp.where(bucket == 0, s[i], jnp.where(bucket == 1, pairs[i], whole)) for i in range(ROW_SLOTS)]


def over_rows(parts, tok_count):
    quarter = tok_count // ROW_SLOTS
    return jnp.concatenate([jnp.broadcast_to(p, (quarter, p.shape[1])) for p in parts], axis=0)


TILES = 3
LANES = 128
ANY = pl.BlockSpec(memory_space=pl.ANY)
INSIDE = pl.BlockSpec(memory_space=pltpu.VMEM)


class Weights:
    def __init__(self, core, carried, sibling, halves, sems):
        self.core, self.carried, self.sibling, self.halves, self.sems = core, carried, sibling, halves, sems

    def copies(self, i, first, second):
        spot = self.halves[0][i]
        at = (slice(None), pl.ds(i * self.halves[0][0].shape[1], spot.shape[1]))
        return (
            pltpu.make_async_copy(first.at[at], spot, self.sems.at[0, i]),
            pltpu.make_async_copy(second.at[at], self.halves[1][i], self.sems.at[1, i]),
        )

    def start(self, order):
        @pl.when(self.core == 0)
        def _():
            for i in order:
                for copy in self.copies(i, self.carried, self.sibling):
                    copy.start()

        @pl.when(self.core != 0)
        def _():
            for i in order:
                for copy in self.copies(i, self.sibling, self.carried):
                    copy.start()

    def wait(self, i):
        for copy in self.copies(i, self.carried, self.sibling):
            copy.wait()


def load_tables(bucket, tables, spots, sems):
    copies = [pltpu.make_async_copy(t.at[bucket], s, sems.at[i]) for i, (t, s) in enumerate(zip(tables, spots))]
    for copy in copies:
        copy.start()
    return copies


def mix_forward_kernel(facts, x_ref, *refs):
    carried, sibling, tables = refs[0], refs[1], refs[2:6]
    (
        normed_ref, gated_ref, mid_ref, nf_ref, norm_ref, gain_ref, t_out, s_out, mix_out, kf_out, vf_out,
        first, second, spots, kept, w_sems, t_sems, k_sems,
    ) = refs[6:]
    tok_count, width = x_ref.shape
    tile = width // TILES
    bucket = facts[0]
    lengths = [facts[1 + i] for i in range(ROW_SLOTS)]
    weights = Weights(facts[1 + ROW_SLOTS], carried, sibling, (first, second), w_sems)
    weights.start([TILES - 1, *range(TILES - 1)])
    copies = load_tables(bucket, tables, spots, t_sems)
    x = x_ref[...].astype(F32)
    r = lax.rsqrt(jnp.mean(x * x, axis=-1, keepdims=True) + 1e-06)
    scaled = x * r
    mask = pad_mask(bucket, lengths, (tok_count, tile), tok_count)
    weights.wait(TILES - 1)
    gains = first[TILES - 1][:, 2 * tile :].astype(F32).T[:8]
    gain_ref[...] = gains
    normed = (scaled * gains[0:1]).astype(BF16)
    normed_ref[...] = normed
    edge, scale = bin_facts(bucket, (tok_count // 2, tile), tok_count)
    half = tok_count // 2
    outs = (t_out, s_out, mix_out, kf_out, vf_out)
    stores = []
    for n, j in enumerate([TILES - 1, *range(TILES - 1)]):
        if n > 0:
            weights.wait(j)
        at = slice(j * tile, (j + 1) * tile)
        a = mm(normed, first[j][:, :tile])
        c = mm(normed, first[j][:, tile : 2 * tile])
        v = mm(normed, second[j][:, :tile]) * mask
        t = jnp.tanh(a) * mask
        norms = [jnp.sqrt(s + 1e-05) for s in row_sums(bucket, t * t, tok_count)]
        norm_ref[:, at] = (norms[0] + norms[1] + norms[2] + norms[3]) * (1.0 / ROW_SLOTS)
        unit = t * over_rows([1.0 / n for n in norms], tok_count)
        if n == 0:
            for copy in copies:
                copy.wait()
        kf = transform(spots[0][...], spots[1][...], unit)
        vf = transform(spots[0][...], spots[1][...], v)
        kr, ki, vr, vi = kf[:half], kf[half:], vf[:half], vf[half:]
        kivi = ki * vi
        pr = (kr * vr - jnp.where(edge, 0.0, kivi)) * scale
        pi = jnp.where(edge, kivi, kr * vi + ki * vr) * scale
        mixed = transform(spots[2][...], spots[3][...], jnp.concatenate([pr, pi], axis=0))
        sig = 1.0 / (1.0 + jnp.exp(-c))
        gated_ref[:, at] = (mixed * sig * mask).astype(BF16)
        for i, value in enumerate((t, sig, mixed, kf, vf)):
            kept[i][j] = value.astype(kept[i].dtype)
            store = pltpu.make_async_copy(kept[i].at[j], outs[i].at[j], k_sems.at[i, j])
            store.start()
            stores.append(store)
    gated = gated_ref[...]
    for i in range(TILES):
        at = slice(i * tile, (i + 1) * tile)
        mid_ref[:, at] = x_ref[:, at].astype(F32) + mm(gated, second[i][:, tile : 2 * tile])
    mid = mid_ref[...]
    r = lax.rsqrt(jnp.mean(mid * mid, axis=-1, keepdims=True) + 1e-06)
    nf_ref[...] = (mid * r * gains[1:2]).astype(BF16)
    for store in stores:
        store.wait()


def table_spots(tok):
    return tuple(pltpu.VMEM((tok, tok), BF16) for _ in range(4))


def half_spots(width):
    tile = width // TILES
    shapes = [(width, 2 * tile)] * (TILES - 1) + [(width, 2 * tile + LANES)]
    return tuple(pltpu.VMEM(shape, BF16) for shape in shapes)


def mix_forward(facts, x, carried, sibling, tables):
    tok, width = x.shape
    tile = width // TILES
    kinds = (F32, F32, BF16, BF16, BF16)
    return pl.pallas_call(
        mix_forward_kernel,
        in_specs=[pl.BlockSpec(memory_space=pltpu.SMEM), INSIDE, *[ANY] * 6],
        out_specs=[*[INSIDE] * 6, *[ANY] * 5],
        out_shape=[
            jax.ShapeDtypeStruct((tok, width), BF16), jax.ShapeDtypeStruct((tok, width), BF16),
            jax.ShapeDtypeStruct((tok, width), F32), jax.ShapeDtypeStruct((tok, width), BF16),
            jax.ShapeDtypeStruct((1, width), F32), jax.ShapeDtypeStruct((8, width), F32),
            *[jax.ShapeDtypeStruct((TILES, tok, tile), kind) for kind in kinds],
        ],
        scratch_shapes=[
            half_spots(width), half_spots(width), table_spots(tok),
            tuple(pltpu.VMEM((TILES, tok, tile), kind) for kind in kinds),
            pltpu.SemaphoreType.DMA((2, TILES)), pltpu.SemaphoreType.DMA((4,)), pltpu.SemaphoreType.DMA((5, TILES)),
        ],
        compiler_params=pltpu.CompilerParams(vmem_limit_bytes=VMEM_BYTES),
        name="mix_forward",
    )(facts, x, carried, sibling, *tables)


def rms_back(values, gain, grad):
    r = lax.rsqrt(jnp.mean(values * values, axis=-1, keepdims=True) + 1e-06)
    scaled = values * r
    inner = grad * gain
    dot = jnp.mean(inner * scaled, axis=-1, keepdims=True)
    return r * (inner - scaled * dot), grad * scaled


def mix_back_kernel(facts, x_ref, cot_ref, gain_ref, mid_ref, own_ref, sib_ref, normed_ref, gated_ref, norm_ref, *refs):
    residuals, refs = refs[:5], refs[5:]
    (carried, sibling), tables, (tok_ref, keep, send), refs = refs[:2], refs[2:6], refs[6:9], refs[9:]
    first, second, spots, held, gm_ref, acc_ref, w_sems, t_sems, k_sems = refs
    tok_count, width = x_ref.shape
    tile = width // TILES
    half = tok_count // 2
    bucket = facts[0]
    lengths = [facts[1 + i] for i in range(ROW_SLOTS)]
    core = facts[1 + ROW_SLOTS]
    weights = Weights(core, carried, sibling, (first, second), w_sems)
    weights.start(range(TILES))
    copies = load_tables(bucket, tables, spots, t_sems)
    loads = [
        [pltpu.make_async_copy(residuals[i].at[j], held[i].at[j], k_sems.at[i, j]) for i in range(5)]
        for j in range(TILES)
    ]
    for group in loads:
        for load in group:
            load.start()
    outer = cot_ref[...].astype(F32) * pad_mask(bucket, lengths, cot_ref.shape, tok_count)
    grad = own_ref[...] + sib_ref[...].astype(F32)
    back, terms = rms_back(mid_ref[...], gain_ref[1:2, :], grad)
    gain2 = jnp.sum(terms, axis=0, keepdims=True)
    grad_mid = outer + back
    gm_ref[...] = grad_mid
    low = grad_mid.astype(BF16)
    normed, gated = normed_ref[...], gated_ref[...]
    mask = pad_mask(bucket, lengths, (tok_count, tile), tok_count)
    edge, scale = bin_facts(bucket, (half, tile), tok_count)
    for i in range(TILES):
        weights.wait(i)
    for copy in copies:
        copy.wait()
    for j in range(TILES):
        at = slice(j * tile, (j + 1) * tile)
        grad_gated = sum(
            mm_nt(low[:, i * tile : (i + 1) * tile], second[i][at, tile : 2 * tile]) for i in range(TILES)
        )
        go = mm_tn(gated, low[:, at])
        grad_gated = grad_gated * mask
        for load in loads[j]:
            load.wait()
        t, sig, mixed, kf, vf = (h[j].astype(F32) for h in held)
        dc = (grad_gated * mixed * (sig * (1.0 - sig))).astype(BF16)
        df = transform(spots[0][...], spots[1][...], grad_gated * sig)
        kr, ki, vr, vi = kf[:half], kf[half:], vf[:half], vf[half:]
        dr, di = df[:half] * scale, df[half:] * scale
        divi, diki = di * vi, di * ki
        dkr = dr * vr + jnp.where(edge, 0.0, divi)
        dki = jnp.where(edge, divi, di * vr - dr * vi)
        dvr = dr * kr + jnp.where(edge, 0.0, diki)
        dvi = jnp.where(edge, diki, di * kr - dr * ki)
        du = transform(spots[2][...], spots[3][...], jnp.concatenate([dkr, dki], axis=0))
        dv = (transform(spots[2][...], spots[3][...], jnp.concatenate([dvr, dvi], axis=0)) * mask).astype(BF16)
        inverse = [lax.rsqrt(s + 1e-05) for s in row_sums(bucket, t * t, tok_count)]
        dots = row_sums(bucket, du * t, tok_count)
        coupling = [d * i * i * i for d, i in zip(dots, inverse)]
        dt = du * over_rows(inverse, tok_count) - t * over_rows(coupling, tok_count)
        da = (dt * mask * (1.0 - t * t)).astype(BF16)
        pairs = ((mm_tn(normed, da), mm_tn(normed, dv)), (mm_tn(normed, dc), go))
        for i, (one, two) in enumerate(pairs):
            to = slice((2 * j + i) * tile, (2 * j + i + 1) * tile)
            keep[:, to] = jnp.where(core == 0, one, two).astype(BF16)
            send[:, to] = jnp.where(core == 0, two, one).astype(BF16)
        part = (
            mm_nt(da, first[j][:, :tile]) + mm_nt(dc, first[j][:, tile : 2 * tile]) + mm_nt(dv, second[j][:, :tile])
        )
        if j == 0:
            acc_ref[...] = part
        else:
            acc_ref[...] += part
    back, terms = rms_back(x_ref[...].astype(F32), gain_ref[0:1, :], acc_ref[...])
    gain1 = jnp.sum(terms, axis=0, keepdims=True)
    tok_ref[...] = (gm_ref[...] + back).astype(BF16)
    extras = jnp.concatenate([gain1, gain2, norm_ref[...], jnp.zeros((LANES - 3, width), F32)], axis=0).T
    keep[:, 2 * width :] = jnp.where(core == 0, extras, 0.0).astype(BF16)
    send[:, 2 * width :] = jnp.where(core == 0, 0.0, extras).astype(BF16)


def mix_back(facts, x, cot, gains, mid, own, sib, normed, gated, norms, kept, carried, sibling, tables):
    tok, width = x.shape
    tile = width // TILES
    part = jax.ShapeDtypeStruct((width, 2 * width + LANES), BF16)
    assert TILES * tile == width
    return pl.pallas_call(
        mix_back_kernel,
        grid=(1,),
        in_specs=[
            pl.BlockSpec(memory_space=pltpu.SMEM), *[INSIDE] * 4,
            pl.BlockSpec((tok, width), lambda i: (0, 0)), *[INSIDE] * 4, *[ANY] * (5 + 2 + 4),
        ],
        out_specs=[INSIDE] * 3,
        out_shape=[jax.ShapeDtypeStruct((tok, width), BF16), part, part],
        scratch_shapes=[
            half_spots(width), half_spots(width), table_spots(tok),
            tuple(pltpu.VMEM(k.shape, k.dtype) for k in kept),
            pltpu.VMEM((tok, width), F32), pltpu.VMEM((tok, width), F32),
            pltpu.SemaphoreType.DMA((2, TILES)), pltpu.SemaphoreType.DMA((4,)), pltpu.SemaphoreType.DMA((5, TILES)),
        ],
        compiler_params=pltpu.CompilerParams(vmem_limit_bytes=VMEM_BYTES),
        name="mix_back",
    )(facts, x, cot, gains, mid, own, sib, normed, gated, norms, *kept, carried, sibling, *tables)


UNIT_TILE = 256


def ffn_kernel(facts, nfo_ref, nfs_ref, gfo_ref, gfs_ref, *refs):
    pieces, refs = refs[:6], refs[6:]
    nf_ref, h_ref, dg_ref, du_ref, gd_ref, wg_ref, wu_ref, wd_ref, gf_ref, gate, up, downs, sems, down_sems = refs
    step = pl.program_id(0)
    tiles = gate.shape[0]
    tok = nfo_ref.shape[0]
    bits = [facts[2 + ROW_SLOTS + i] for i in range(3)]

    def copies(t):
        found = []
        for i, spot in enumerate((gate, up)):
            for side in range(2):
                half = bits[i] if side == 0 else 1 - bits[i]
                source = pieces[2 * i + side].at[:, :, pl.ds(pl.multiple_of(t * UNIT_TILE, UNIT_TILE), UNIT_TILE)]
                found.append(pltpu.make_async_copy(source, spot.at[t, :, half], sems.at[i, side, t]))
        return found

    def down_copies():
        return [
            pltpu.make_async_copy(pieces[4 + side], downs.at[:, bits[2] if side == 0 else 1 - bits[2]], down_sems.at[side])
            for side in range(2)
        ]

    @pl.when(step == 0)
    def _():
        for copy in copies(0) + down_copies():
            copy.start()
        for t in range(1, tiles):
            for copy in copies(t):
                copy.start()
        nf_ref[:tok] = nfo_ref[...]
        nf_ref[tok:] = nfs_ref[...]
        gf_ref[:tok] = gfo_ref[...]
        gf_ref[tok:] = gfs_ref[...]

    for copy in copies(step):
        copy.wait()

    @pl.when(step == 0)
    def _():
        for copy in down_copies():
            copy.wait()

    nf, gf = nf_ref[...], gf_ref[...]
    wg = gate[step].reshape(nf.shape[1], UNIT_TILE)
    wu = up[step].reshape(nf.shape[1], UNIT_TILE)
    wd = downs.reshape(tiles * UNIT_TILE, nf.shape[1])[pl.ds(pl.multiple_of(step * UNIT_TILE, UNIT_TILE), UNIT_TILE)]
    wg_ref[...], wu_ref[...], wd_ref[...] = wg, wu, wd
    g = mm(nf, wg)
    u = mm(nf, wu)
    dh = mm_nt(gf, wd)
    sig = 1.0 / (1.0 + jnp.exp(-g))
    silu = g * sig
    h = (silu * u).astype(BF16)
    h_ref[...] = h
    du_ref[...] = (dh * silu).astype(BF16)
    dg_ref[...] = (dh * u * (sig * (1.0 + g * (1.0 - sig)))).astype(BF16)
    gd_ref[...] = mm_tn(h, gf).astype(BF16)


def ffn(facts, nf_own, nf_sib, gf_own, gf_sib, pieces):
    tok, width = nf_own.shape
    units = pieces[0].shape[2]
    tiles = units // UNIT_TILE
    whole = pl.BlockSpec((tok, width), lambda j: (0, 0))
    tall = pl.BlockSpec((width, UNIT_TILE), lambda j: (0, j))
    flat = pl.BlockSpec((UNIT_TILE, width), lambda j: (j, 0))
    column = pl.BlockSpec((2 * tok, UNIT_TILE), lambda j: (0, j))
    spots = [
        pltpu.VMEM((tiles, p.shape[0], 2, p.shape[1], UNIT_TILE), BF16) for p in (pieces[0], pieces[2])
    ]
    spots.append(pltpu.VMEM((pieces[4].shape[0], 2, *pieces[4].shape[1:]), BF16))
    return pl.pallas_call(
        ffn_kernel,
        grid=(tiles,),
        in_specs=[pl.BlockSpec(memory_space=pltpu.SMEM), whole, whole, whole, whole, *[ANY] * 6],
        out_specs=[
            pl.BlockSpec((2 * tok, width), lambda j: (0, 0)), column, column, column, flat, tall, tall, flat,
        ],
        out_shape=[
            jax.ShapeDtypeStruct((2 * tok, width), BF16),
            *[jax.ShapeDtypeStruct((2 * tok, units), BF16)] * 3,
            jax.ShapeDtypeStruct((units, width), BF16),
            *[jax.ShapeDtypeStruct((width, units), BF16)] * 2,
            jax.ShapeDtypeStruct((units, width), BF16),
        ],
        scratch_shapes=[
            pltpu.VMEM((2 * tok, width), BF16), *spots,
            pltpu.SemaphoreType.DMA((2, 2, tiles)), pltpu.SemaphoreType.DMA((2,)),
        ],
        compiler_params=pltpu.CompilerParams(vmem_limit_bytes=VMEM_BYTES),
        name="ffn",
    )(facts, nf_own, nf_sib, gf_own, gf_sib, *pieces)


def pack_mixer_kernel(place, in_ref, out_ref, gain_ref, mine_ref, send_ref):
    core = place[0]
    width = out_ref.shape[1]
    tile = width // TILES
    for j in range(TILES):
        at = slice(j * tile, (j + 1) * tile)
        pairs = (
            (in_ref[:, j * tile : (j + 1) * tile], in_ref[:, 2 * width + j * tile : 2 * width + (j + 1) * tile]),
            (in_ref[:, width + j * tile : width + (j + 1) * tile], out_ref[:, at]),
        )
        for i, (one, two) in enumerate(pairs):
            to = slice((2 * j + i) * tile, (2 * j + i + 1) * tile)
            mine_ref[:, to] = jnp.where(core == 0, one, two)
            send_ref[:, to] = jnp.where(core == 0, two, one)
    mine_ref[:, 2 * width :] = gain_ref[...]
    send_ref[:, 2 * width :] = gain_ref[...]


def pack_mixer(place, w_in, w_out, gains):
    rows, width = w_out.shape
    return pl.pallas_call(
        pack_mixer_kernel,
        in_specs=[pl.BlockSpec(memory_space=pltpu.SMEM), INSIDE, INSIDE, INSIDE],
        out_specs=[INSIDE, INSIDE],
        out_shape=[jax.ShapeDtypeStruct((rows, 2 * width + LANES), BF16)] * 2,
        name="pack_mixer",
    )(place, w_in, w_out, gains)


def pack_units_kernel(place, gu_ref, order_ref, mine_ref, send_ref, stack_ref):
    core = place[0]
    rows = gu_ref.shape[0]
    width = order_ref.shape[0]
    half = width // 2
    groups = gu_ref.shape[1] // width
    pitch = stack_ref.shape[0] // groups
    for i in range(groups):
        stack_ref[i * pitch : i * pitch + rows] = gu_ref[:, i * width : (i + 1) * width].astype(F32)
    sorted_rows = mm(stack_ref[...].astype(BF16), order_ref[...])
    for i in range(groups):
        block = sorted_rows[i * pitch : i * pitch + rows]
        to = slice(i * half, (i + 1) * half)
        mine_ref[:, to] = jnp.where(core == 0, block[:, :half], block[:, half:]).astype(BF16)
        send_ref[:, to] = jnp.where(core == 0, block[:, half:], block[:, :half]).astype(BF16)


def pack_units(place, w_gu, order):
    rows, columns = w_gu.shape
    width = order.shape[0]
    pitch = -(-rows // 8) * 8
    return pl.pallas_call(
        pack_units_kernel,
        in_specs=[pl.BlockSpec(memory_space=pltpu.SMEM), INSIDE, INSIDE],
        out_specs=[INSIDE, INSIDE],
        out_shape=[jax.ShapeDtypeStruct((rows, columns // 2), BF16)] * 2,
        scratch_shapes=[pltpu.VMEM((columns // width * pitch, width), F32)],
        name="pack_units",
    )(place, w_gu, order)


class Links:
    def __init__(self):
        self.outer = lax.axis_size("outer")
        self.narrow = lax.axis_size("narrow")
        self.core = lax.axis_index("core")
        self.bits = []
        for axis, size in (("outer", self.outer), ("narrow", self.narrow)):
            spot = lax.axis_index(axis)
            span = size
            while span > 1:
                span //= 2
                self.bits.append((axis, size, span, (spot // span) % 2))
        self.outer_bits = sum(bit[0] == "outer" for bit in self.bits)

    def chain(self, turn):
        rest = list(range(1, len(self.bits)))
        turn %= len(rest)
        return [0] + rest[turn:] + rest[:turn]

    def narrow_last(self):
        return [0] + [p for p in range(1, len(self.bits)) if p != self.outer_bits] + [self.outer_bits]

    def swap_core(self, values):
        return lax.ppermute(values, "core", [(0, 1), (1, 0)])

    def exchange(self, values, p):
        axis, size, stride, _ = self.bits[p]
        return lax.ppermute(values, axis, [(i, i ^ stride) for i in range(size)])

    def split(self, p, have, middle, rows):
        before = 2 ** sum(q < p for q in have)
        after = 2 ** sum(q > p for q in have)
        if p < self.outer_bits:
            return before, after * middle * rows
        return before * middle, after * rows

    def gather_step(self, block, p, have, middle):
        rows = block.shape[0] // (middle * 2 ** len(have))
        before, after = self.split(p, have, middle, rows)
        mine = block.reshape(before, 1, after, block.shape[1])
        other = self.exchange(block, p).reshape(mine.shape)
        bit = self.bits[p][3]
        side = lax.broadcasted_iota(jnp.int32, (1, 2, 1, 1), 1)
        both = jnp.where(side == bit, mine, other)
        return both.reshape(-1, block.shape[1])

    def gather_pieces(self, block, p, have, middle):
        rows = block.shape[0] // (middle * 2 ** len(have))
        before, after = self.split(p, have, middle, rows)
        shape = (before, after, block.shape[1])
        return block.reshape(shape), self.exchange(block, p).reshape(shape)

    def far_gather(self, blocks):
        rows = blocks[0].shape[0]
        flat = [b[i : i + rows] for b in blocks for i in range(0, b.shape[0], rows)]
        got = self.exchange(jnp.concatenate(flat, axis=1), 0)
        side = lax.broadcasted_iota(jnp.int32, (2, 1, 1), 0)
        grown, at = [], 0
        for b in blocks:
            other = []
            for _ in range(b.shape[0] // rows):
                other.append(got[:, at : at + b.shape[1]])
                at += b.shape[1]
            other = jnp.concatenate(other, axis=0)
            grown.append(jnp.where(side == self.bits[0][3], b[None], other[None]).reshape(-1, b.shape[1]))
        return grown

    def spread(self, block, middle):
        shape = (2,) * self.outer_bits + (middle,) + (2,) * (len(self.bits) - self.outer_bits)
        return [block.reshape(*shape, block.shape[0] // math.prod(shape), block.shape[1])]

    def side(self, terms, p, other):
        bit = self.bits[p][3]
        dim = p if p < self.outer_bits else p + 1
        return [lax.dynamic_slice_in_dim(t, 1 - bit if other else bit, 1, dim) for t in terms]

    def scatter_step(self, terms, p):
        return [*self.side(terms, p, False), self.exchange(total(self.side(terms, p, True)), p)]

    def far_scatter(self, blocks):
        sent = [flat(total(self.side(terms, 0, True))) for terms in blocks]
        rows = sent[0].shape[0]
        cut = [m[i : i + rows] for m in sent for i in range(0, m.shape[0], rows)]
        got = self.exchange(jnp.concatenate(cut, axis=1), 0)
        sums, at = [], 0
        for terms, m in zip(blocks, sent):
            other = []
            for _ in range(m.shape[0] // rows):
                other.append(got[:, at : at + m.shape[1]])
                at += m.shape[1]
            kept = [flat(t) for t in self.side(terms, 0, False)]
            sums.append(total([*kept, jnp.concatenate(other, axis=0)]))
        return sums


def total(terms):
    return sum(t.astype(F32) for t in terms).astype(BF16)


def flat(block):
    return block.reshape(-1, block.shape[-1])


def unit_order(width, chunk):
    columns = np.arange(width)
    pairs = width // (2 * chunk)
    source = np.concatenate(
        [np.concatenate([(2 * i + core) * chunk + np.arange(chunk) for i in range(pairs)]) for core in range(2)]
    )
    return (columns[:, None] == source[None, :]).astype(ml_dtypes.bfloat16)


def on_device(tokens, cotangent, w_in, w_out, w_gu, w_down, gain_mix, gain_ffn, buckets, lengths):
    links = Links()
    core = links.core
    tok, width = tokens.shape
    rows = w_in.shape[0]
    ff = w_gu.shape[1] // 2
    units = ff // 2
    tile = width // TILES
    fence = lax.optimization_barrier

    tables = [jnp.asarray(t) for t in transform_tables(tok)]
    order = jnp.asarray(unit_order(width, ff // (2 * links.outer)))
    chains = [links.chain(2), links.chain(1), links.narrow_last()]
    bits = [links.bits[chain[-1]][3] for chain in chains]
    facts = jnp.concatenate([buckets, lengths[0], jnp.stack([core, *bits])]).astype(jnp.int32)
    middles = [2, 2, 1]
    count = len(links.bits)

    def grow(blocks, k, middles):
        return [links.gather_step(b, chain[k], set(chain[:k]), m) for b, chain, m in zip(blocks, chains, middles)]

    def shrink(blocks, k):
        return [links.scatter_step(terms, chain[k]) for terms, chain in zip(blocks, chains)]

    def both_rows(mine, send):
        other = links.swap_core(send)
        side = lax.broadcasted_iota(jnp.int32, (2, 1, 1), 0)
        return jnp.where(side == core, mine[None], other[None]).reshape(2 * mine.shape[0], mine.shape[1])

    lane = lax.broadcasted_iota(jnp.int32, (rows, LANES), 1)
    gains = jnp.where(lane == 0, gain_mix[:, None], jnp.where(lane == 1, gain_ffn[:, None], 0))
    place = core.reshape(1).astype(jnp.int32)
    mine, send = pack_mixer(place, w_in, w_out, gains)
    mine_gu, send_gu = pack_units(place, w_gu, order)
    mixer = links.gather_step(both_rows(mine, send), 0, set(), 2)
    gu = both_rows(mine_gu, send_gu)
    mixer, gu, wd = fence((mixer, gu, w_down))
    gu, wd = links.far_gather([gu, wd])
    cuts = [2 * tile * j for j in range(TILES)] + [mine.shape[1]]
    parts = [mixer[:, a:b] for a, b in zip(cuts[:-1], cuts[1:])]
    weights = [gu[:, :units], gu[:, units:], wd]
    for k in range(1, count):
        parts = grow(parts, k, [2] * TILES)
    for k in range(1, count - 2):
        weights = grow(weights, k, middles)
    parts, weights = fence((parts, weights))
    parts = jnp.concatenate(parts, axis=1)
    siblings = links.swap_core(parts)
    parts, siblings, weights = fence((parts, siblings, weights))
    weights = grow(weights, count - 2, middles)

    normed, gated, mid, nf, norms, gains, *kept = mix_forward(facts, tokens, parts, siblings, tables)

    nf, weights = fence((nf, weights))
    pieces = [
        piece
        for w, chain, m in zip(weights, chains, middles)
        for piece in links.gather_pieces(w, chain[-1], set(chain[:-1]), m)
    ]

    mask = pad_mask(facts[0], [facts[1 + i] for i in range(ROW_SLOTS)], (tok, 1), tok)
    gf = (cotangent.astype(F32) * mask).astype(BF16)
    nf2, h, dg, du, grad_down, wg, wu, wd = ffn(facts, nf, links.swap_core(nf), gf, links.swap_core(gf), pieces)
    back = mm_nt(dg, wg) + mm_nt(du, wu)
    back_sib = links.swap_core(back[tok:].astype(BF16))
    grads = [mm_tn(nf2, dg).astype(BF16), mm_tn(nf2, du).astype(BF16), grad_down]
    grads = [links.spread(g, m) for g, m in zip(grads, middles)]
    grads = shrink(grads, count - 1)

    devices = 2 * links.outer * links.narrow
    grad_tokens, keep, send = mix_back(
        facts, tokens, cotangent, gains, mid, back, back_sib, normed, gated, norms * (1.0 / devices), kept,
        parts, siblings, tables,
    )
    grads, keep, send, h = fence((grads, keep, send, h))
    got = links.swap_core(send)
    grads = shrink(grads, count - 2)
    grads, keep, got = fence((grads, keep, got))
    sums = total([keep, got])
    sums = [links.spread(sums[:, a:b], 2) for a, b in zip(cuts[:-1], cuts[1:])]
    for k in reversed(range(1, count - 2)):
        grads = shrink(grads, k)
    sums = [[total(terms)] for terms in shrink(sums, count - 1)]
    grads, sums, h = fence((grads, sums, h))
    out = mm(h, wd)
    out_sib = links.swap_core(out[tok:].astype(BF16))
    layer_out = ((mid + out[:tok] + out_sib.astype(F32)) * mask).astype(BF16)
    for k in reversed(range(1, count - 1)):
        sums = [[total(terms)] for terms in shrink(sums, k)]
    sum_gate, sum_up, sum_down = links.far_scatter(grads)
    sums = links.far_scatter(sums)
    def by_half(block):
        halves = block.reshape(2, rows, block.shape[1])
        own = lax.dynamic_index_in_dim(halves, core, 0, keepdims=False)
        far = links.swap_core(lax.dynamic_index_in_dim(halves, 1 - core, 0, keepdims=False))
        return jnp.where(core == 0, own, far), jnp.where(core == 0, far, own)

    groups = 2 * ff // width
    pair = [half.reshape(rows, groups, width // 2) for half in by_half(jnp.concatenate([sum_gate, sum_up], axis=1))]
    grad_w_gu = mm_nt(jnp.concatenate(pair, axis=2).reshape(rows * groups, width), order).reshape(rows, 2 * ff)
    one, two = by_half(jnp.concatenate(sums, axis=1))
    columns = lambda half, offset: [half[:, (2 * j + offset) * tile : (2 * j + offset + 1) * tile] for j in range(TILES)]
    grad_w_in = jnp.concatenate(columns(one, 0) + columns(one, 1) + columns(two, 0), axis=1).astype(F32)
    grad_w_out = jnp.concatenate(columns(two, 1), axis=1).astype(F32)
    extra = one[:, 2 * width : 2 * width + LANES].astype(F32).T
    return (
        layer_out, grad_tokens, grad_w_in, grad_w_out, grad_w_gu, sum_down.astype(F32), extra[0], extra[1], extra[2],
    )


def solution(mesh):
    wide, narrow = mesh.devices.shape
    split = jax.sharding.Mesh(mesh.devices.reshape(wide // 2, 2, narrow), ("outer", "core", "narrow"))
    every = ("outer", "core", "narrow")
    flat, tall = P(every), P(every, None)
    return jax.shard_map(
        on_device,
        mesh=split,
        in_specs=(tall, tall, tall, tall, tall, tall, flat, flat, flat, tall),
        out_specs=(tall, tall, tall, tall, tall, tall, flat, flat, flat),
        check_vma=False,
    )
```

```python
import math

import jax
import jax.numpy as jnp
import ml_dtypes
import numpy as np
from jax import lax
from jax.experimental import pallas as pl
from jax.experimental.pallas import tpu as pltpu
from jax.sharding import PartitionSpec as P

F32 = jnp.float32
BF16 = jnp.bfloat16
ROW_SLOTS = 4
BUCKETS = 3
VMEM_BYTES = 56 * 1024 * 1024


def transform_tables(tok_count):
    highs, lows = [], []
    for bucket in range(BUCKETS):
        rows = ROW_SLOTS >> bucket
        length = tok_count // rows
        half = length // 2
        angle = 2.0 * np.pi * (np.arange(half)[:, None] * np.arange(length)[None, :] % length) / length
        real = np.cos(angle) * np.sqrt(2.0 / length)
        imag = -np.sin(angle) * np.sqrt(2.0 / length)
        real[0] = 1.0 / np.sqrt(length)
        imag[0] = (1.0 - 2.0 * (np.arange(length) % 2)) / np.sqrt(length)
        table = np.zeros((tok_count, tok_count))
        for row in range(rows):
            at = slice(row * length, (row + 1) * length)
            table[row * half : (row + 1) * half, at] = real
            table[tok_count // 2 + row * half : tok_count // 2 + (row + 1) * half, at] = imag
        high = table.astype(ml_dtypes.bfloat16)
        highs.append(high)
        lows.append((table - high.astype(np.float64)).astype(ml_dtypes.bfloat16))
    high, low = np.stack(highs), np.stack(lows)
    return high, low, np.ascontiguousarray(high.transpose(0, 2, 1)), np.ascontiguousarray(low.transpose(0, 2, 1))


def mm(left, right):
    return jnp.dot(left, right, preferred_element_type=F32)


def mm_nt(left, right):
    return lax.dot_general(left, right, (((1,), (1,)), ((), ())), preferred_element_type=F32)


def mm_tn(left, right):
    return lax.dot_general(left, right, (((0,), (0,)), ((), ())), preferred_element_type=F32)


def transform(high, low, values):
    top = values.astype(BF16)
    rest = (values - top.astype(F32)).astype(BF16)
    return mm(high, top) + (mm(high, rest) + mm(low, top))


def transform_once(table, values):
    return mm(table, values.astype(BF16))


def bin_facts(bucket, shape, tok_count):
    half = lax.shift_left(jnp.int32(tok_count // (2 * ROW_SLOTS)), bucket)
    spot = lax.broadcasted_iota(jnp.int32, shape, 0)
    edge = (spot & (half - 1)) == 0
    length = (2 * half).astype(F32)
    scale = jnp.where(edge, jnp.sqrt(length), jnp.sqrt(0.5 * length))
    return edge, scale


def pad_mask(bucket, lengths, shape, tok_count):
    quarter = tok_count // ROW_SLOTS
    shift = (quarter.bit_length() - 1) + bucket
    spot = lax.broadcasted_iota(jnp.int32, shape, 0)
    slot = lax.shift_right_logical(spot, jnp.broadcast_to(shift, shape))
    within = spot - lax.shift_left(slot, jnp.broadcast_to(shift, shape))
    length = jnp.where(
        slot == 0, lengths[0], jnp.where(slot == 1, lengths[1], jnp.where(slot == 2, lengths[2], lengths[3]))
    )
    return (within < length).astype(F32)


def widen(values, width):
    return jnp.concatenate([values] * (width // values.shape[1]), axis=1)


def row_sums(bucket, values, tok_count):
    quarter = tok_count // ROW_SLOTS
    s = [jnp.sum(values[i * quarter : (i + 1) * quarter], axis=0, keepdims=True) for i in range(ROW_SLOTS)]
    left, right = s[0] + s[1], s[2] + s[3]
    whole = left + right
    pairs = (left, left, right, right)
    return [jnp.where(bucket == 0, s[i], jnp.where(bucket == 1, pairs[i], whole)) for i in range(ROW_SLOTS)]


def over_rows(parts, tok_count):
    quarter = tok_count // ROW_SLOTS
    return jnp.concatenate([jnp.broadcast_to(p, (quarter, p.shape[1])) for p in parts], axis=0)


TILES = 3
LANES = 128
ANY = pl.BlockSpec(memory_space=pl.ANY)
INSIDE = pl.BlockSpec(memory_space=pltpu.VMEM)


class Weights:
    def __init__(self, core, carried, sibling, halves, sems):
        self.core, self.carried, self.sibling, self.halves, self.sems = core, carried, sibling, halves, sems

    def copies(self, i, first, second):
        spot = self.halves[0][i]
        at = (slice(None), pl.ds(i * self.halves[0][0].shape[1], spot.shape[1]))
        return (
            lambda: pltpu.make_async_copy(first.at[at], spot, self.sems.at[0, i]),
            lambda: pltpu.make_async_copy(second.at[at], self.halves[1][i], self.sems.at[1, i]),
        )

    def start(self, order, sides=(0, 1)):
        @pl.when(self.core == 0)
        def _():
            for i in order:
                for side in sides:
                    self.copies(i, self.carried, self.sibling)[side]().start()

        @pl.when(self.core != 0)
        def _():
            for i in order:
                for side in sides:
                    self.copies(i, self.sibling, self.carried)[side]().start()

    def wait(self, i, sides=(0, 1)):
        for side in sides:
            self.copies(i, self.carried, self.sibling)[side]().wait()


def load_tables(bucket, tables, spots, sems):
    copies = [pltpu.make_async_copy(t.at[bucket], s, sems.at[i]) for i, (t, s) in enumerate(zip(tables, spots))]
    for copy in copies:
        copy.start()
    return copies


def mix_forward_kernel(facts, x_ref, *refs):
    carried, sibling, tables = refs[0], refs[1], refs[2:6]
    (
        normed_ref, gated_ref, mid_ref, low_mid_ref, nf_ref, norm_ref, gain_ref, t_out, s_out, mix_out, kf_out, vf_out,
        first, second, spots, kept, w_sems, t_sems, k_sems,
    ) = refs[6:]
    tok_count, width = x_ref.shape
    tile = width // TILES
    bucket = facts[0]
    lengths = [facts[1 + i] for i in range(ROW_SLOTS)]
    weights = Weights(facts[1 + ROW_SLOTS], carried, sibling, (first, second), w_sems)
    weights.start([TILES - 1, *range(TILES - 1)])
    copies = load_tables(bucket, tables, spots, t_sems)
    x = x_ref[...].astype(F32)
    r = lax.rsqrt(jnp.mean(x * x, axis=-1, keepdims=True) + 1e-06)
    scaled = x * r
    mask = pad_mask(bucket, lengths, (tok_count, tile), tok_count)
    weights.wait(TILES - 1)
    gains = first[TILES - 1][:, 2 * tile :].astype(F32).T[:8]
    gain_ref[...] = gains
    normed = (scaled * gains[0:1]).astype(BF16)
    normed_ref[...] = normed
    edge, scale = bin_facts(bucket, (tok_count // 2, tile), tok_count)
    half = tok_count // 2
    outs = (t_out, s_out, mix_out, kf_out, vf_out)
    stores = []
    for n, j in enumerate([TILES - 1, *range(TILES - 1)]):
        if n > 0:
            weights.wait(j)
        at = slice(j * tile, (j + 1) * tile)
        a = mm(normed, first[j][:, :tile])
        c = mm(normed, first[j][:, tile : 2 * tile])
        v = mm(normed, second[j][:, :tile]) * mask
        t = jnp.tanh(a) * mask
        norms = [jnp.sqrt(s + 1e-05) for s in row_sums(bucket, t * t, tok_count)]
        norm_ref[:, at] = (norms[0] + norms[1] + norms[2] + norms[3]) * (1.0 / ROW_SLOTS)
        unit = t * over_rows([1.0 / n for n in norms], tok_count)
        if n == 0:
            for copy in copies:
                copy.wait()
        kf = transform(spots[0][...], spots[1][...], unit)
        vf = transform(spots[0][...], spots[1][...], v)
        kr, ki, vr, vi = kf[:half], kf[half:], vf[:half], vf[half:]
        kivi = ki * vi
        pr = (kr * vr - jnp.where(edge, 0.0, kivi)) * scale
        pi = jnp.where(edge, kivi, kr * vi + ki * vr) * scale
        mixed = transform(spots[2][...], spots[3][...], jnp.concatenate([pr, pi], axis=0))
        sig = 1.0 / (1.0 + jnp.exp(-c))
        gated_ref[:, at] = (mixed * sig * mask).astype(BF16)
        for i, value in enumerate((t, sig, mixed, kf, vf)):
            kept[i][j] = value.astype(kept[i].dtype)
            store = pltpu.make_async_copy(kept[i].at[j], outs[i].at[j], k_sems.at[i, j])
            store.start()
            stores.append(store)
    gated = gated_ref[...]
    for i in range(TILES):
        at = slice(i * tile, (i + 1) * tile)
        mid_ref[:, at] = x_ref[:, at].astype(F32) + mm(gated, second[i][:, tile : 2 * tile])
    mid = mid_ref[...]
    low_mid_ref[...] = mid.astype(BF16)
    r = lax.rsqrt(jnp.mean(mid * mid, axis=-1, keepdims=True) + 1e-06)
    nf_ref[...] = (mid * r * gains[1:2]).astype(BF16)
    for store in stores:
        store.wait()


def table_spots(tok, count=4):
    return tuple(pltpu.VMEM((tok, tok), BF16) for _ in range(count))


def half_spots(width):
    tile = width // TILES
    shapes = [(width, 2 * tile)] * (TILES - 1) + [(width, 2 * tile + LANES)]
    return tuple(pltpu.VMEM(shape, BF16) for shape in shapes)


def mix_forward(facts, x, carried, sibling, tables):
    tok, width = x.shape
    tile = width // TILES
    kinds = (F32, F32, BF16, BF16, BF16)
    return pl.pallas_call(
        mix_forward_kernel,
        in_specs=[pl.BlockSpec(memory_space=pltpu.SMEM), INSIDE, *[ANY] * 6],
        out_specs=[*[INSIDE] * 7, *[ANY] * 5],
        out_shape=[
            jax.ShapeDtypeStruct((tok, width), BF16), jax.ShapeDtypeStruct((tok, width), BF16),
            jax.ShapeDtypeStruct((tok, width), F32), jax.ShapeDtypeStruct((tok, width), BF16),
            jax.ShapeDtypeStruct((tok, width), BF16), jax.ShapeDtypeStruct((1, width), F32), jax.ShapeDtypeStruct((8, width), F32),
            *[jax.ShapeDtypeStruct((TILES, tok, tile), kind) for kind in kinds],
        ],
        scratch_shapes=[
            half_spots(width), half_spots(width), table_spots(tok),
            tuple(pltpu.VMEM((TILES, tok, tile), kind) for kind in kinds),
            pltpu.SemaphoreType.DMA((2, TILES)), pltpu.SemaphoreType.DMA((4,)), pltpu.SemaphoreType.DMA((5, TILES)),
        ],
        compiler_params=pltpu.CompilerParams(vmem_limit_bytes=VMEM_BYTES),
        name="mix_forward",
    )(facts, x, carried, sibling, *tables)


def rms_back(values, gain, grad):
    r = lax.rsqrt(jnp.mean(values * values, axis=-1, keepdims=True) + 1e-06)
    scaled = values * r
    inner = grad * gain
    dot = jnp.mean(inner * scaled, axis=-1, keepdims=True)
    return r * (inner - scaled * dot), grad * scaled


def mix_back_kernel(facts, gain_ref, norm_ref, *refs):
    streams, residuals, (carried, sibling), tables, refs = refs[:7], refs[7:12], refs[12:14], refs[14:16], refs[16:]
    (tok_ref, keep, send), (spots_in, first, second, spots, held, g0, g1, gm_ref, acc_ref), sems = refs[:3], refs[3:12], refs[12:]
    s_sems, w_sems, t_sems, k_sems, o_sems = sems
    back_ref, sib_ref, mid_ref, cot_ref, gated_ref, normed_ref, x_ref = spots_in
    tok_count, width = x_ref.shape
    tile = width // TILES
    half = tok_count // 2
    bucket = facts[0]
    lengths = [facts[1 + i] for i in range(ROW_SLOTS)]
    core = facts[1 + ROW_SLOTS]
    sources = [streams[0].at[pl.ds(0, tok_count)], *streams[1:]]
    inputs = [pltpu.make_async_copy(a, b, s_sems.at[i]) for i, (a, b) in enumerate(zip(sources, spots_in))]
    for copy in inputs[:4]:
        copy.start()
    weights = Weights(core, carried, sibling, (first, second), w_sems)
    weights.start(range(TILES), (1,))
    loads = [
        [pltpu.make_async_copy(residuals[i].at[j], held[i].at[j], k_sems.at[i, j]) for i in range(5)]
        for j in range(TILES)
    ]
    mask = pad_mask(bucket, lengths, (tok_count, LANES), tok_count)
    edge, scale = bin_facts(bucket, (half, LANES), tok_count)
    edge = widen(jnp.where(edge, 1.0, 0.0), tile) > 0.5
    scale = widen(scale, tile)
    for copy in inputs[:4]:
        copy.wait()
    for copy in loads[0]:
        copy.start()
    copies = load_tables(bucket, tables, spots, t_sems)
    for copy in inputs[4:6]:
        copy.start()
    grad = back_ref[...].astype(F32) + sib_ref[...].astype(F32)
    back, terms = rms_back(mid_ref[...].astype(F32), gain_ref[1:2, :], grad)
    gain2 = jnp.sum(terms, axis=0, keepdims=True)
    grad_mid = cot_ref[...].astype(F32) * widen(mask, width) + back
    gm_ref[...] = grad_mid
    low = grad_mid.astype(BF16)
    mask = widen(mask, tile)
    for i in range(TILES):
        weights.wait(i, (1,))

    def put(j, act):
        at = (slice(None), pl.ds(2 * j * tile, 2 * tile + (LANES if j == TILES - 1 else 0)))
        for here, (one, two) in ((0, (keep, send)), (1, (send, keep))):
            @pl.when((core == 0) == (here == 0))
            def _():
                for i, (source, target) in enumerate(((g0, one), (g1, two))):
                    act(pltpu.make_async_copy(source.at[at], target.at[at], o_sems.at[i, j]))

    for j in range(TILES):
        at = slice(j * tile, (j + 1) * tile)
        grad_gated = sum(
            mm_nt(low[:, i * tile : (i + 1) * tile], second[i][at, tile : 2 * tile]) for i in range(TILES)
        )
        grad_gated = grad_gated * mask
        if j == 0:
            weights.start([0], (0,))
            for load in loads[1]:
                load.start()
            weights.start([1], (0,))
            for load in loads[2]:
                load.start()
            weights.start([2], (0,))
            inputs[6].start()
        for load in loads[j]:
            load.wait()
        if j == 0:
            for copy in copies:
                copy.wait()
        t, sig, mixed, kf, vf = (h[j].astype(F32) for h in held)
        dc = (grad_gated * mixed * (sig * (1.0 - sig))).astype(BF16)
        df = transform_once(spots[0][...], grad_gated * sig)
        kr, ki, vr, vi = kf[:half], kf[half:], vf[:half], vf[half:]
        dr, di = df[:half] * scale, df[half:] * scale
        divi, diki = di * vi, di * ki
        dkr = dr * vr + jnp.where(edge, 0.0, divi)
        dki = jnp.where(edge, divi, di * vr - dr * vi)
        dvr = dr * kr + jnp.where(edge, 0.0, diki)
        dvi = jnp.where(edge, diki, di * kr - dr * ki)
        du = transform_once(spots[1][...], jnp.concatenate([dkr, dki], axis=0))
        dv = (transform_once(spots[1][...], jnp.concatenate([dvr, dvi], axis=0)) * mask).astype(BF16)
        inverse = [lax.rsqrt(s + 1e-05) for s in row_sums(bucket, t * t, tok_count)]
        dots = row_sums(bucket, du * t, tok_count)
        coupling = [d * i * i * i for d, i in zip(dots, inverse)]
        dt = du * over_rows(inverse, tok_count) - t * over_rows(coupling, tok_count)
        da = (dt * mask * (1.0 - t * t)).astype(BF16)
        if j == 0:
            for copy in inputs[4:6]:
                copy.wait()
        normed, gated = normed_ref[...], gated_ref[...]
        for i, (one, two) in enumerate(
            ((mm_tn(normed, da), mm_tn(normed, dv)), (mm_tn(normed, dc), mm_tn(gated, low[:, at])))
        ):
            to = slice((2 * j + i) * tile, (2 * j + i + 1) * tile)
            g0[:, to] = one.astype(BF16)
            g1[:, to] = two.astype(BF16)
        if j < TILES - 1:
            put(j, lambda copy: copy.start())
        weights.wait(j, (0,))
        part = (
            mm_nt(da, first[j][:, :tile]) + mm_nt(dc, first[j][:, tile : 2 * tile]) + mm_nt(dv, second[j][:, :tile])
        )
        if j == 0:
            acc_ref[...] = part
        else:
            acc_ref[...] += part
    inputs[6].wait()
    back, terms = rms_back(x_ref[...].astype(F32), gain_ref[0:1, :], acc_ref[...])
    gain1 = jnp.sum(terms, axis=0, keepdims=True)
    extras = jnp.concatenate([gain1, gain2, norm_ref[...], jnp.zeros((LANES - 3, width), F32)], axis=0).T
    g0[:, 2 * width :] = extras.astype(BF16)
    g1[:, 2 * width :] = jnp.zeros((width, LANES), BF16)
    put(TILES - 1, lambda copy: copy.start())
    tok_ref[...] = (gm_ref[...] + back).astype(BF16)
    for j in range(TILES):
        put(j, lambda copy: copy.wait())


def mix_back(facts, x, cot, gains, mid, own, sib, normed, gated, norms, kept, carried, sibling, tables):
    tok, width = x.shape
    assert TILES * (width // TILES) == width
    part = jax.ShapeDtypeStruct((width, 2 * width + LANES), BF16)
    spots = [(tok, width)] * 7
    kinds = [BF16] * 7
    return pl.pallas_call(
        mix_back_kernel,
        in_specs=[pl.BlockSpec(memory_space=pltpu.SMEM), INSIDE, INSIDE, *[ANY] * (7 + 5 + 2 + 2)],
        out_specs=[INSIDE, ANY, ANY],
        out_shape=[jax.ShapeDtypeStruct((tok, width), BF16), part, part],
        scratch_shapes=[
            tuple(pltpu.VMEM(shape, kind) for shape, kind in zip(spots, kinds)),
            half_spots(width), half_spots(width), table_spots(tok, 2),
            tuple(pltpu.VMEM(k.shape, k.dtype) for k in kept),
            pltpu.VMEM(part.shape, BF16), pltpu.VMEM(part.shape, BF16),
            pltpu.VMEM((tok, width), F32), pltpu.VMEM((tok, width), F32),
            pltpu.SemaphoreType.DMA((7,)), pltpu.SemaphoreType.DMA((2, TILES)), pltpu.SemaphoreType.DMA((2,)),
            pltpu.SemaphoreType.DMA((5, TILES)), pltpu.SemaphoreType.DMA((2, TILES)),
        ],
        compiler_params=pltpu.CompilerParams(vmem_limit_bytes=VMEM_BYTES),
        name="mix_back",
    )(facts, gains, norms, own, sib, mid, cot, gated, normed, x, *kept, carried, sibling, tables[0], tables[2])


UNIT_TILES = 4


def ffn_kernel(facts, nfo_ref, nfs_ref, gfo_ref, gfs_ref, *refs):
    pieces, refs = refs[:6], refs[6:]
    nf_ref, h_ref, dgu_ref, gd_ref, sent_ref, wgu_ref, wd_ref, gf_ref, gu, downs, sems, down_sems = refs
    step = pl.program_id(0)
    tok, width = nfo_ref.shape
    units = h_ref.shape[1]
    span = gu.shape[2]
    bits = [facts[2 + ROW_SLOTS + i] for i in range(3)]

    def copies(t):
        chain, column = divmod(t, UNIT_TILES // 2)
        for side in range(2):
            half = bits[chain] if side == 0 else 1 - bits[chain]
            piece = pieces[2 * chain + side]
            count = piece.shape[1]
            for b in range(piece.shape[0]):
                yield pltpu.make_async_copy(
                    piece.at[b, :, :, pl.ds(2 * units * column, 2 * units)],
                    gu.at[t, pl.ds((2 * b + half) * count, count)],
                    sems.at[t, side, b],
                )

    def down_copies():
        for side in range(2):
            half = bits[2] if side == 0 else 1 - bits[2]
            yield pltpu.make_async_copy(pieces[4 + side], downs.at[:, half], down_sems.at[side])

    @pl.when(step == 0)
    def _():
        for copy in [*copies(0), *down_copies()]:
            copy.start()
        for t in range(1, UNIT_TILES):
            for copy in copies(t):
                copy.start()
        nf_ref[:tok] = nfo_ref[...]
        nf_ref[tok:] = nfs_ref[...]
        gf_ref[:tok] = gfo_ref[...]
        gf_ref[tok:] = gfs_ref[...]

    for t in range(UNIT_TILES):

        @pl.when(step == t)
        def _():
            for copy in copies(t):
                copy.wait()

    @pl.when(step == 0)
    def _():
        for copy in down_copies():
            copy.wait()

    nf, gf = nf_ref[...], gf_ref[...]
    wgu = gu[step].reshape(gu.shape[1] * span, 2 * units)
    wd = downs.reshape(UNIT_TILES * units, width)[pl.ds(pl.multiple_of(step * units, units), units)]
    wgu_ref[...], wd_ref[...] = wgu, wd
    both = mm(nf, wgu)
    g, u = both[:, :units], both[:, units:]
    dh = mm_nt(gf, wd)
    sig = 0.5 + 0.5 * jnp.tanh(0.5 * g)
    silu = g * sig
    h = (silu * u).astype(BF16)
    h_ref[...] = h
    dgu_ref[:, units:] = (dh * silu).astype(BF16)
    dgu_ref[:, :units] = (dh * u * (sig * (1.0 + g * (1.0 - sig)))).astype(BF16)
    gd = mm_tn(h, gf).astype(BF16)
    gd_ref[...] = gd
    gd = gd.reshape(sent_ref.shape[0], 2, *sent_ref.shape[1:])
    sent_ref[...] = jnp.where(bits[2] == 0, gd[:, 1], gd[:, 0])


def ffn(facts, nf_own, nf_sib, gf_own, gf_sib, pieces):
    tok, width = nf_own.shape
    total_units = pieces[0].shape[2]
    units = total_units // UNIT_TILES
    span = min(pieces[0].shape[1], pieces[2].shape[1])
    cut = [p.reshape(p.shape[0], p.shape[1] // span, span, p.shape[2]) for p in pieces[:4]]
    below, above = pieces[4].shape[1], pieces[4].shape[0]
    whole = pl.BlockSpec((tok, width), lambda j: (0, 0))
    tall = pl.BlockSpec((width, 2 * units), lambda j: (0, j))
    flat = pl.BlockSpec((units, width), lambda j: (j, 0))
    return pl.pallas_call(
        ffn_kernel,
        grid=(UNIT_TILES,),
        in_specs=[pl.BlockSpec(memory_space=pltpu.SMEM), whole, whole, whole, whole, *[ANY] * 6],
        out_specs=[
            pl.BlockSpec((2 * tok, width), lambda j: (0, 0)),
            pl.BlockSpec((2 * tok, units), lambda j: (0, j)),
            pl.BlockSpec((2 * tok, 2 * units), lambda j: (0, j)),
            flat,
            pl.BlockSpec((above // UNIT_TILES, below, width), lambda j: (j, 0, 0)),
            tall, flat,
        ],
        out_shape=[
            jax.ShapeDtypeStruct((2 * tok, width), BF16),
            jax.ShapeDtypeStruct((2 * tok, total_units), BF16),
            jax.ShapeDtypeStruct((2 * tok, 2 * total_units), BF16),
            jax.ShapeDtypeStruct((total_units, width), BF16),
            jax.ShapeDtypeStruct((above, below, width), BF16),
            jax.ShapeDtypeStruct((width, 2 * total_units), BF16),
            jax.ShapeDtypeStruct((total_units, width), BF16),
        ],
        scratch_shapes=[
            pltpu.VMEM((2 * tok, width), BF16),
            pltpu.VMEM((UNIT_TILES, width // span, span, 2 * units), BF16),
            pltpu.VMEM((above, 2, below, width), BF16),
            pltpu.SemaphoreType.DMA((UNIT_TILES, 2, max(p.shape[0] for p in cut))),
            pltpu.SemaphoreType.DMA((2,)),
        ],
        compiler_params=pltpu.CompilerParams(vmem_limit_bytes=VMEM_BYTES),
        name="ffn",
    )(facts, nf_own, nf_sib, gf_own, gf_sib, *cut, *pieces[4:])


def pack_mixer_kernel(place, in_ref, out_ref, gain_ref, mine_ref, send_ref):
    core = place[0]
    width = out_ref.shape[1]
    tile = width // TILES
    for j in range(TILES):
        at = slice(j * tile, (j + 1) * tile)
        pairs = (
            (in_ref[:, j * tile : (j + 1) * tile], in_ref[:, 2 * width + j * tile : 2 * width + (j + 1) * tile]),
            (in_ref[:, width + j * tile : width + (j + 1) * tile], out_ref[:, at]),
        )
        for i, (one, two) in enumerate(pairs):
            to = slice((2 * j + i) * tile, (2 * j + i + 1) * tile)
            mine_ref[:, to] = jnp.where(core == 0, one, two)
            send_ref[:, to] = jnp.where(core == 0, two, one)
    mine_ref[:, 2 * width :] = gain_ref[...]
    send_ref[:, 2 * width :] = gain_ref[...]


def pack_mixer(place, w_in, w_out, gains):
    rows, width = w_out.shape
    return pl.pallas_call(
        pack_mixer_kernel,
        in_specs=[pl.BlockSpec(memory_space=pltpu.SMEM), INSIDE, INSIDE, INSIDE],
        out_specs=[INSIDE, INSIDE],
        out_shape=[jax.ShapeDtypeStruct((rows, 2 * width + LANES), BF16)] * 2,
        name="pack_mixer",
    )(place, w_in, w_out, gains)


def pack_units_kernel(place, gu_ref, order_ref, mine_ref, send_ref, stack_ref):
    core = place[0]
    rows = gu_ref.shape[0]
    width = order_ref.shape[0]
    half = width // 2
    groups = gu_ref.shape[1] // width
    pitch = stack_ref.shape[0] // groups
    for i in range(groups):
        stack_ref[i * pitch : i * pitch + rows] = gu_ref[:, i * width : (i + 1) * width].astype(F32)
    sorted_rows = mm(stack_ref[...].astype(BF16), order_ref[...])
    for i in range(groups):
        block = sorted_rows[i * pitch : i * pitch + rows]
        spot = 2 * i if i < groups // 2 else 2 * i - groups + 1
        to = slice(spot * half, (spot + 1) * half)
        mine_ref[:, to] = jnp.where(core == 0, block[:, :half], block[:, half:]).astype(BF16)
        send_ref[:, to] = jnp.where(core == 0, block[:, half:], block[:, :half]).astype(BF16)


def pack_units(place, w_gu, order):
    rows, columns = w_gu.shape
    width = order.shape[0]
    pitch = -(-rows // 8) * 8
    return pl.pallas_call(
        pack_units_kernel,
        in_specs=[pl.BlockSpec(memory_space=pltpu.SMEM), INSIDE, INSIDE],
        out_specs=[INSIDE, INSIDE],
        out_shape=[jax.ShapeDtypeStruct((rows, columns // 2), BF16)] * 2,
        scratch_shapes=[pltpu.VMEM((columns // width * pitch, width), F32)],
        name="pack_units",
    )(place, w_gu, order)


def unpack_mixer_kernel(place, own_ref, far_ref, in_ref, out_ref, extra_ref):
    core = place[0]
    width = out_ref.shape[1]
    tile = width // TILES
    own, far = own_ref[...].astype(F32), far_ref[...].astype(F32)
    for j in range(TILES):
        for i in range(2):
            at = slice((2 * j + i) * tile, (2 * j + i + 1) * tile)
            one = jnp.where(core == 0, own[:, at], far[:, at])
            two = jnp.where(core == 0, far[:, at], own[:, at])
            in_ref[:, i * width + j * tile : i * width + (j + 1) * tile] = one
            if i == 0:
                in_ref[:, 2 * width + j * tile : 2 * width + (j + 1) * tile] = two
            else:
                out_ref[:, j * tile : (j + 1) * tile] = two
    extra_ref[...] = jnp.where(core == 0, own[:, 2 * width :], far[:, 2 * width :])


def unpack_mixer(place, own, far, width):
    rows = own.shape[0]
    return pl.pallas_call(
        unpack_mixer_kernel,
        in_specs=[pl.BlockSpec(memory_space=pltpu.SMEM), INSIDE, INSIDE],
        out_specs=[INSIDE] * 3,
        out_shape=[jax.ShapeDtypeStruct((rows, n), F32) for n in (3 * width, width, LANES)],
        name="unpack_mixer",
    )(place, own, far)


def unpack_units_kernel(place, own_ref, far_ref, order_ref, gu_ref, stack_ref):
    core = place[0]
    rows = gu_ref.shape[0]
    width = order_ref.shape[0]
    half = width // 2
    groups = gu_ref.shape[1] // width
    pitch = stack_ref.shape[0] // groups
    own, far = own_ref[...].astype(F32), far_ref[...].astype(F32)
    for i in range(groups):
        spot = 2 * i if i < groups // 2 else 2 * i - groups + 1
        at = slice(spot * half, (spot + 1) * half)
        to = slice(i * pitch, i * pitch + rows)
        stack_ref[to, :half] = jnp.where(core == 0, own[:, at], far[:, at])
        stack_ref[to, half:] = jnp.where(core == 0, far[:, at], own[:, at])
    sorted_rows = mm_nt(stack_ref[...].astype(BF16), order_ref[...])
    for i in range(groups):
        gu_ref[:, i * width : (i + 1) * width] = sorted_rows[i * pitch : i * pitch + rows]


def unpack_units(place, own, far, order):
    rows, columns = own.shape
    width = order.shape[0]
    pitch = -(-rows // 8) * 8
    return pl.pallas_call(
        unpack_units_kernel,
        in_specs=[pl.BlockSpec(memory_space=pltpu.SMEM), INSIDE, INSIDE, INSIDE],
        out_specs=INSIDE,
        out_shape=jax.ShapeDtypeStruct((rows, 2 * columns), F32),
        scratch_shapes=[pltpu.VMEM((2 * columns // width * pitch, width), F32)],
        name="unpack_units",
    )(place, own, far, order)


class Links:
    def __init__(self):
        self.outer = lax.axis_size("outer")
        self.narrow = lax.axis_size("narrow")
        self.core = lax.axis_index("core")
        self.bits = []
        for axis, size in (("outer", self.outer), ("narrow", self.narrow)):
            spot = lax.axis_index(axis)
            span = size
            while span > 1:
                span //= 2
                self.bits.append((axis, size, span, (spot // span) % 2))
        self.outer_bits = sum(bit[0] == "outer" for bit in self.bits)

    def chain(self, turn):
        rest = list(range(1, len(self.bits)))
        turn %= len(rest)
        return [0] + rest[turn:] + rest[:turn]

    def narrow_last(self):
        return [0] + [p for p in range(1, len(self.bits)) if p != self.outer_bits] + [self.outer_bits]

    def swap_core(self, values):
        return lax.ppermute(values, "core", [(0, 1), (1, 0)])

    def exchange(self, values, p):
        axis, size, stride, _ = self.bits[p]
        return lax.ppermute(values, axis, [(i, i ^ stride) for i in range(size)])

    def split(self, p, have, middle, rows):
        before = 2 ** sum(q < p for q in have)
        after = 2 ** sum(q > p for q in have)
        if p < self.outer_bits:
            return before, after * middle * rows
        return before * middle, after * rows

    def gather_step(self, block, p, have, middle):
        rows = block.shape[0] // (middle * 2 ** len(have))
        before, after = self.split(p, have, middle, rows)
        mine = block.reshape(before, 1, after, block.shape[1])
        other = self.exchange(block, p).reshape(mine.shape)
        bit = self.bits[p][3]
        side = lax.broadcasted_iota(jnp.int32, (1, 2, 1, 1), 1)
        both = jnp.where(side == bit, mine, other)
        return both.reshape(-1, block.shape[1])

    def gather_pieces(self, block, p, have, middle):
        rows = block.shape[0] // (middle * 2 ** len(have))
        before, after = self.split(p, have, middle, rows)
        shape = (before, after, block.shape[1])
        return block.reshape(shape), self.exchange(block, p).reshape(shape)

    def far_gather(self, blocks):
        rows = blocks[0].shape[0]
        flat = [b[i : i + rows] for b in blocks for i in range(0, b.shape[0], rows)]
        got = self.exchange(jnp.concatenate(flat, axis=1), 0)
        side = lax.broadcasted_iota(jnp.int32, (2, 1, 1), 0)
        grown, at = [], 0
        for b in blocks:
            other = []
            for _ in range(b.shape[0] // rows):
                other.append(got[:, at : at + b.shape[1]])
                at += b.shape[1]
            other = jnp.concatenate(other, axis=0)
            grown.append(jnp.where(side == self.bits[0][3], b[None], other[None]).reshape(-1, b.shape[1]))
        return grown

    def spread(self, block, middle):
        shape = (2,) * self.outer_bits + (middle,) + (2,) * (len(self.bits) - self.outer_bits)
        return [block.reshape(*shape, block.shape[0] // math.prod(shape), block.shape[1])]

    def side(self, terms, p, other):
        bit = self.bits[p][3]
        dim = p if p < self.outer_bits else p + 1
        return [lax.dynamic_slice_in_dim(t, 1 - bit if other else bit, 1, dim) for t in terms]

    def scatter_step(self, terms, p):
        return [*self.side(terms, p, False), self.exchange(total(self.side(terms, p, True)), p)]

    def far_scatter(self, blocks):
        sent = [flat(total(self.side(terms, 0, True))) for terms in blocks]
        rows = sent[0].shape[0]
        cut = [m[i : i + rows] for m in sent for i in range(0, m.shape[0], rows)]
        got = self.exchange(jnp.concatenate(cut, axis=1), 0)
        sums, at = [], 0
        for terms, m in zip(blocks, sent):
            other = []
            for _ in range(m.shape[0] // rows):
                other.append(got[:, at : at + m.shape[1]])
                at += m.shape[1]
            kept = [flat(t) for t in self.side(terms, 0, False)]
            sums.append(total([*kept, jnp.concatenate(other, axis=0)]))
        return sums


def total(terms):
    return sum(t.astype(F32) for t in terms).astype(BF16)


def flat(block):
    return block.reshape(-1, block.shape[-1])


def unit_order(width, chunk):
    columns = np.arange(width)
    pairs = width // (2 * chunk)
    source = np.concatenate(
        [np.concatenate([(2 * i + core) * chunk + np.arange(chunk) for i in range(pairs)]) for core in range(2)]
    )
    return (columns[:, None] == source[None, :]).astype(ml_dtypes.bfloat16)


def on_device(tokens, cotangent, w_in, w_out, w_gu, w_down, gain_mix, gain_ffn, buckets, lengths):
    links = Links()
    core = links.core
    tok, width = tokens.shape
    rows = w_in.shape[0]
    ff = w_gu.shape[1] // 2
    units = ff // 2
    tile = width // TILES
    fence = lax.optimization_barrier

    tables = [jnp.asarray(t) for t in transform_tables(tok)]
    order = jnp.asarray(unit_order(width, ff // (2 * links.outer)))
    chains = [links.chain(2), links.chain(1), links.narrow_last()]
    bits = [links.bits[chain[-1]][3] for chain in chains]
    facts = jnp.concatenate([buckets, lengths[0], jnp.stack([core, *bits])]).astype(jnp.int32)
    middles = [2, 2, 1]
    count = len(links.bits)

    def grow(blocks, k, middles):
        return [links.gather_step(b, chain[k], set(chain[:k]), m) for b, chain, m in zip(blocks, chains, middles)]

    def shrink(blocks, k):
        return [links.scatter_step(terms, chain[k]) for terms, chain in zip(blocks, chains)]

    def both_rows(mine, send):
        other = links.swap_core(send)
        side = lax.broadcasted_iota(jnp.int32, (2, 1, 1), 0)
        return jnp.where(side == core, mine[None], other[None]).reshape(2 * mine.shape[0], mine.shape[1])

    lane = lax.broadcasted_iota(jnp.int32, (rows, LANES), 1)
    gains = jnp.where(lane == 0, gain_mix[:, None], jnp.where(lane == 1, gain_ffn[:, None], 0))
    place = core.reshape(1).astype(jnp.int32)
    mine, send = pack_mixer(place, w_in, w_out, gains)
    mine_gu, send_gu = pack_units(place, w_gu, order)
    mixer = links.gather_step(both_rows(mine, send), 0, set(), 2)
    gu = both_rows(mine_gu, send_gu)
    mixer, gu, wd = fence((mixer, gu, w_down))
    mask = pad_mask(facts[0], [facts[1 + i] for i in range(ROW_SLOTS)], (tok, 1), tok)
    gf = (fence((cotangent, mixer))[0].astype(F32) * mask).astype(BF16)
    gf_sib = links.swap_core(gf)
    gu, wd = links.far_gather([gu, wd])
    cuts = [2 * tile * j for j in range(TILES)] + [mine.shape[1]]
    parts = [mixer[:, a:b] for a, b in zip(cuts[:-1], cuts[1:])]
    weights = [gu[:, :units], gu[:, units:], wd]
    for k in range(1, count):
        parts = grow(parts, k, [2] * TILES)
    for k in range(1, count - 1):
        weights = grow(weights, k, middles)
    parts = fence((parts, weights, gf_sib))[0]
    parts = jnp.concatenate(parts, axis=1)
    siblings = links.swap_core(parts)

    normed, gated, mid, low_mid, nf, norms, gains, *kept = mix_forward(facts, tokens, parts, siblings, tables)

    nf = fence((nf, weights))[0]
    pieces = [
        piece
        for w, chain, m in zip(weights, chains, middles)
        for piece in links.gather_pieces(w, chain[-1], set(chain[:-1]), m)
    ]

    nf2, h, dgu, grad_down, down_sent, wgu, wd = ffn(facts, nf, links.swap_core(nf), gf, gf_sib, pieces)
    back = mm_nt(dgu, wgu).astype(BF16)
    back_sib = links.swap_core(back[tok:])
    grad_gu = mm_tn(nf2, dgu).astype(BF16)
    grads = [grad_gu[:, :units], grad_gu[:, units:], grad_down]
    grads = [links.spread(g, m) for g, m in zip(grads, middles)]
    last = chains[2][-1]
    down_sent = links.exchange(down_sent.reshape(links.side(grads[2], last, True)[0].shape), last)
    grads = shrink(grads[:2], count - 1) + [[*links.side(grads[2], last, False), down_sent]]

    devices = 2 * links.outer * links.narrow
    grad_tokens, keep, send = mix_back(
        facts, tokens, cotangent, gains, low_mid, back, back_sib, normed, gated, norms * (1.0 / devices), kept,
        parts, siblings, tables,
    )
    grads, keep, send, h = fence((grads, keep, send, h))
    sums = total([keep, links.swap_core(send)])
    sums = [links.spread(sums[:, a:b], 2) for a, b in zip(cuts[:-1], cuts[1:])]
    sent = [total(links.side(terms, chain[-1], True)) for terms, chain in zip(sums, chains)]
    kept = [links.side(terms, chain[-1], False) for terms, chain in zip(sums, chains)]
    grads = shrink(grads, count - 2)
    grads, sent, kept = fence((grads, sent, kept))
    for k in reversed(range(1, count - 2)):
        grads = shrink(grads, k)
    grads, h, held = fence((grads, h, sent[-1]))
    sent = [*sent[:-1], held]
    sums = [[total([*k, links.exchange(m, chain[-1])])] for k, m, chain in zip(kept, sent, chains)]
    out = mm(h, wd)
    out_sib = links.swap_core(out[tok:].astype(BF16))
    layer_out = ((mid + out[:tok] + out_sib.astype(F32)) * mask).astype(BF16)
    for k in reversed(range(1, count - 1)):
        sums = [[total(terms)] for terms in shrink(sums, k)]
    sum_gate, sum_up, sum_down = links.far_scatter(grads)
    def own_and_far(block):
        halves = block.reshape(2, rows, block.shape[1])
        own = lax.dynamic_index_in_dim(halves, core, 0, keepdims=False)
        return own, links.swap_core(lax.dynamic_index_in_dim(halves, 1 - core, 0, keepdims=False))

    grad_w_gu = unpack_units(place, *own_and_far(jnp.concatenate([sum_gate, sum_up], axis=1)), order)
    sums = links.far_scatter(fence((sums, grad_w_gu, layer_out))[0])
    grad_w_in, grad_w_out, extra = unpack_mixer(place, *own_and_far(jnp.concatenate(sums, axis=1)), width)
    extra = extra.T
    return (
        layer_out, grad_tokens, grad_w_in, grad_w_out, grad_w_gu, sum_down.astype(F32), extra[0], extra[1], extra[2],
    )


def solution(mesh):
    wide, narrow = mesh.devices.shape
    split = jax.sharding.Mesh(mesh.devices.reshape(wide // 2, 2, narrow), ("outer", "core", "narrow"))
    every = ("outer", "core", "narrow")
    flat, tall = P(every), P(every, None)
    return jax.shard_map(
        on_device,
        mesh=split,
        in_specs=(tall, tall, tall, tall, tall, tall, flat, flat, flat, tall),
        out_specs=(tall, tall, tall, tall, tall, tall, flat, flat, flat),
        check_vma=False,
    )
```

```python
import math

import jax
import jax.numpy as jnp
import ml_dtypes
import numpy as np
from jax import lax
from jax.experimental import pallas as pl
from jax.experimental.pallas import tpu as pltpu
from jax.sharding import PartitionSpec as P

F32 = jnp.float32
BF16 = jnp.bfloat16
ROW_SLOTS = 4
BUCKETS = 3
VMEM_BYTES = 56 * 1024 * 1024


def transform_tables(tok_count):
    highs, lows = [], []
    for bucket in range(BUCKETS):
        rows = ROW_SLOTS >> bucket
        length = tok_count // rows
        half = length // 2
        angle = 2.0 * np.pi * (np.arange(half)[:, None] * np.arange(length)[None, :] % length) / length
        real = np.cos(angle) * np.sqrt(2.0 / length)
        imag = -np.sin(angle) * np.sqrt(2.0 / length)
        real[0] = 1.0 / np.sqrt(length)
        imag[0] = (1.0 - 2.0 * (np.arange(length) % 2)) / np.sqrt(length)
        table = np.zeros((tok_count, tok_count))
        for row in range(rows):
            at = slice(row * length, (row + 1) * length)
            table[row * half : (row + 1) * half, at] = real
            table[tok_count // 2 + row * half : tok_count // 2 + (row + 1) * half, at] = imag
        high = table.astype(ml_dtypes.bfloat16)
        highs.append(high)
        lows.append((table - high.astype(np.float64)).astype(ml_dtypes.bfloat16))
    high, low = np.stack(highs), np.stack(lows)
    return high, low, np.ascontiguousarray(high.transpose(0, 2, 1)), np.ascontiguousarray(low.transpose(0, 2, 1))


def mm(left, right):
    return jnp.dot(left, right, preferred_element_type=F32)


def mm_nt(left, right):
    return lax.dot_general(left, right, (((1,), (1,)), ((), ())), preferred_element_type=F32)


def mm_tn(left, right):
    return lax.dot_general(left, right, (((0,), (0,)), ((), ())), preferred_element_type=F32)


def transform(high, low, values):
    top = values.astype(BF16)
    rest = (values - top.astype(F32)).astype(BF16)
    return mm(high, top) + (mm(high, rest) + mm(low, top))


def transform_once(table, values):
    return mm(table, values.astype(BF16))


def bin_facts(bucket, shape, tok_count):
    half = lax.shift_left(jnp.int32(tok_count // (2 * ROW_SLOTS)), bucket)
    spot = lax.broadcasted_iota(jnp.int32, shape, 0)
    edge = (spot & (half - 1)) == 0
    length = (2 * half).astype(F32)
    scale = jnp.where(edge, jnp.sqrt(length), jnp.sqrt(0.5 * length))
    return edge, scale


def pad_mask(bucket, lengths, shape, tok_count):
    quarter = tok_count // ROW_SLOTS
    shift = (quarter.bit_length() - 1) + bucket
    spot = lax.broadcasted_iota(jnp.int32, shape, 0)
    slot = lax.shift_right_logical(spot, jnp.broadcast_to(shift, shape))
    within = spot - lax.shift_left(slot, jnp.broadcast_to(shift, shape))
    length = jnp.where(
        slot == 0, lengths[0], jnp.where(slot == 1, lengths[1], jnp.where(slot == 2, lengths[2], lengths[3]))
    )
    return (within < length).astype(F32)


def widen(values, width):
    return jnp.concatenate([values] * (width // values.shape[1]), axis=1)


def row_sums(bucket, values, tok_count):
    quarter = tok_count // ROW_SLOTS
    s = [jnp.sum(values[i * quarter : (i + 1) * quarter], axis=0, keepdims=True) for i in range(ROW_SLOTS)]
    left, right = s[0] + s[1], s[2] + s[3]
    whole = left + right
    pairs = (left, left, right, right)
    return [jnp.where(bucket == 0, s[i], jnp.where(bucket == 1, pairs[i], whole)) for i in range(ROW_SLOTS)]


def over_rows(parts, tok_count):
    quarter = tok_count // ROW_SLOTS
    return jnp.concatenate([jnp.broadcast_to(p, (quarter, p.shape[1])) for p in parts], axis=0)


TILES = 3
LANES = 128
ANY = pl.BlockSpec(memory_space=pl.ANY)
INSIDE = pl.BlockSpec(memory_space=pltpu.VMEM)


class Weights:
    def __init__(self, core, carried, sibling, halves, sems):
        self.core, self.carried, self.sibling, self.halves, self.sems = core, carried, sibling, halves, sems

    def copies(self, i, first, second):
        spot = self.halves[0][i]
        at = (slice(None), pl.ds(i * self.halves[0][0].shape[1], spot.shape[1]))
        return (
            lambda: pltpu.make_async_copy(first.at[at], spot, self.sems.at[0, i]),
            lambda: pltpu.make_async_copy(second.at[at], self.halves[1][i], self.sems.at[1, i]),
        )

    def start(self, order, sides=(0, 1)):
        @pl.when(self.core == 0)
        def _():
            for i in order:
                for side in sides:
                    self.copies(i, self.carried, self.sibling)[side]().start()

        @pl.when(self.core != 0)
        def _():
            for i in order:
                for side in sides:
                    self.copies(i, self.sibling, self.carried)[side]().start()

    def wait(self, i, sides=(0, 1)):
        for side in sides:
            self.copies(i, self.carried, self.sibling)[side]().wait()


def load_tables(bucket, tables, spots, sems):
    copies = [pltpu.make_async_copy(t.at[bucket], s, sems.at[i]) for i, (t, s) in enumerate(zip(tables, spots))]
    for copy in copies:
        copy.start()
    return copies


def mix_forward_kernel(facts, x_ref, *refs):
    carried, sibling, tables = refs[0], refs[1], refs[2:6]
    (
        normed_ref, gated_ref, mid_ref, low_mid_ref, nf_ref, norm_ref, gain_ref, t_out, s_out, mix_out, kf_out, vf_out,
        first, second, spots, kept, w_sems, t_sems, k_sems,
    ) = refs[6:]
    tok_count, width = x_ref.shape
    tile = width // TILES
    bucket = facts[0]
    lengths = [facts[1 + i] for i in range(ROW_SLOTS)]
    weights = Weights(facts[1 + ROW_SLOTS], carried, sibling, (first, second), w_sems)
    weights.start([TILES - 1, *range(TILES - 1)])
    copies = load_tables(bucket, tables, spots, t_sems)
    x = x_ref[...].astype(F32)
    r = lax.rsqrt(jnp.mean(x * x, axis=-1, keepdims=True) + 1e-06)
    scaled = x * r
    mask = pad_mask(bucket, lengths, (tok_count, tile), tok_count)
    weights.wait(TILES - 1)
    gains = first[TILES - 1][:, 2 * tile :].astype(F32).T[:8]
    gain_ref[...] = gains
    normed = (scaled * gains[0:1]).astype(BF16)
    normed_ref[...] = normed
    edge, scale = bin_facts(bucket, (tok_count // 2, tile), tok_count)
    half = tok_count // 2
    outs = (t_out, s_out, mix_out, kf_out, vf_out)
    stores = []
    for n, j in enumerate([TILES - 1, *range(TILES - 1)]):
        if n > 0:
            weights.wait(j)
        at = slice(j * tile, (j + 1) * tile)
        a = mm(normed, first[j][:, :tile])
        c = mm(normed, first[j][:, tile : 2 * tile])
        v = mm(normed, second[j][:, :tile]) * mask
        t = jnp.tanh(a) * mask
        norms = [jnp.sqrt(s + 1e-05) for s in row_sums(bucket, t * t, tok_count)]
        norm_ref[:, at] = (norms[0] + norms[1] + norms[2] + norms[3]) * (1.0 / ROW_SLOTS)
        unit = t * over_rows([1.0 / n for n in norms], tok_count)
        if n == 0:
            for copy in copies:
                copy.wait()
        kf = transform(spots[0][...], spots[1][...], unit)
        vf = transform(spots[0][...], spots[1][...], v)
        kr, ki, vr, vi = kf[:half], kf[half:], vf[:half], vf[half:]
        kivi = ki * vi
        pr = (kr * vr - jnp.where(edge, 0.0, kivi)) * scale
        pi = jnp.where(edge, kivi, kr * vi + ki * vr) * scale
        mixed = transform(spots[2][...], spots[3][...], jnp.concatenate([pr, pi], axis=0))
        sig = 1.0 / (1.0 + jnp.exp(-c))
        gated_ref[:, at] = (mixed * sig * mask).astype(BF16)
        for i, value in enumerate((t, sig, mixed, kf, vf)):
            kept[i][j] = value.astype(kept[i].dtype)
            store = pltpu.make_async_copy(kept[i].at[j], outs[i].at[j], k_sems.at[i, j])
            store.start()
            stores.append(store)
    gated = gated_ref[...]
    for i in range(TILES):
        at = slice(i * tile, (i + 1) * tile)
        mid_ref[:, at] = x_ref[:, at].astype(F32) + mm(gated, second[i][:, tile : 2 * tile])
    mid = mid_ref[...]
    low_mid_ref[...] = mid.astype(BF16)
    r = lax.rsqrt(jnp.mean(mid * mid, axis=-1, keepdims=True) + 1e-06)
    nf_ref[...] = (mid * r * gains[1:2]).astype(BF16)
    for store in stores:
        store.wait()


def table_spots(tok, count=4):
    return tuple(pltpu.VMEM((tok, tok), BF16) for _ in range(count))


def half_spots(width):
    tile = width // TILES
    shapes = [(width, 2 * tile)] * (TILES - 1) + [(width, 2 * tile + LANES)]
    return tuple(pltpu.VMEM(shape, BF16) for shape in shapes)


def mix_forward(facts, x, carried, sibling, tables):
    tok, width = x.shape
    tile = width // TILES
    kinds = (F32, F32, BF16, BF16, BF16)
    return pl.pallas_call(
        mix_forward_kernel,
        in_specs=[pl.BlockSpec(memory_space=pltpu.SMEM), INSIDE, *[ANY] * 6],
        out_specs=[*[INSIDE] * 7, *[ANY] * 5],
        out_shape=[
            jax.ShapeDtypeStruct((tok, width), BF16), jax.ShapeDtypeStruct((tok, width), BF16),
            jax.ShapeDtypeStruct((tok, width), F32), jax.ShapeDtypeStruct((tok, width), BF16),
            jax.ShapeDtypeStruct((tok, width), BF16), jax.ShapeDtypeStruct((1, width), F32), jax.ShapeDtypeStruct((8, width), F32),
            *[jax.ShapeDtypeStruct((TILES, tok, tile), kind) for kind in kinds],
        ],
        scratch_shapes=[
            half_spots(width), half_spots(width), table_spots(tok),
            tuple(pltpu.VMEM((TILES, tok, tile), kind) for kind in kinds),
            pltpu.SemaphoreType.DMA((2, TILES)), pltpu.SemaphoreType.DMA((4,)), pltpu.SemaphoreType.DMA((5, TILES)),
        ],
        compiler_params=pltpu.CompilerParams(vmem_limit_bytes=VMEM_BYTES),
        name="mix_forward",
    )(facts, x, carried, sibling, *tables)


def rms_back(values, gain, grad):
    r = lax.rsqrt(jnp.mean(values * values, axis=-1, keepdims=True) + 1e-06)
    scaled = values * r
    inner = grad * gain
    dot = jnp.mean(inner * scaled, axis=-1, keepdims=True)
    return r * (inner - scaled * dot), grad * scaled


def mix_back_kernel(facts, gain_ref, norm_ref, *refs):
    streams, residuals, (carried, sibling), tables, refs = refs[:7], refs[7:12], refs[12:14], refs[14:16], refs[16:]
    (tok_ref, keep, send), (spots_in, first, second, spots, held, g0, g1, gm_ref, acc_ref), sems = refs[:3], refs[3:12], refs[12:]
    s_sems, w_sems, t_sems, k_sems, o_sems = sems
    back_ref, sib_ref, mid_ref, cot_ref, gated_ref, normed_ref, x_ref = spots_in
    tok_count, width = x_ref.shape
    tile = width // TILES
    half = tok_count // 2
    bucket = facts[0]
    lengths = [facts[1 + i] for i in range(ROW_SLOTS)]
    core = facts[1 + ROW_SLOTS]
    sources = [streams[0].at[pl.ds(0, tok_count)], *streams[1:]]
    inputs = [pltpu.make_async_copy(a, b, s_sems.at[i]) for i, (a, b) in enumerate(zip(sources, spots_in))]
    for copy in inputs[:4]:
        copy.start()
    weights = Weights(core, carried, sibling, (first, second), w_sems)
    weights.start(range(TILES), (1,))
    loads = [
        [pltpu.make_async_copy(residuals[i].at[j], held[i].at[j], k_sems.at[i, j]) for i in range(5)]
        for j in range(TILES)
    ]
    mask = pad_mask(bucket, lengths, (tok_count, LANES), tok_count)
    edge, scale = bin_facts(bucket, (half, LANES), tok_count)
    edge = widen(jnp.where(edge, 1.0, 0.0), tile) > 0.5
    scale = widen(scale, tile)
    for copy in inputs[:4]:
        copy.wait()
    for copy in loads[0]:
        copy.start()
    copies = load_tables(bucket, tables, spots, t_sems)
    for copy in inputs[4:6]:
        copy.start()
    grad = back_ref[...].astype(F32) + sib_ref[...].astype(F32)
    back, terms = rms_back(mid_ref[...].astype(F32), gain_ref[1:2, :], grad)
    gain2 = jnp.sum(terms, axis=0, keepdims=True)
    grad_mid = cot_ref[...].astype(F32) * widen(mask, width) + back
    gm_ref[...] = grad_mid
    low = grad_mid.astype(BF16)
    mask = widen(mask, tile)
    for i in range(TILES):
        weights.wait(i, (1,))

    def put(j, act):
        at = (slice(None), pl.ds(2 * j * tile, 2 * tile + (LANES if j == TILES - 1 else 0)))
        for here, (one, two) in ((0, (keep, send)), (1, (send, keep))):
            @pl.when((core == 0) == (here == 0))
            def _():
                for i, (source, target) in enumerate(((g0, one), (g1, two))):
                    act(pltpu.make_async_copy(source.at[at], target.at[at], o_sems.at[i, j]))

    for j in range(TILES):
        at = slice(j * tile, (j + 1) * tile)
        grad_gated = sum(
            mm_nt(low[:, i * tile : (i + 1) * tile], second[i][at, tile : 2 * tile]) for i in range(TILES)
        )
        grad_gated = grad_gated * mask
        if j == 0:
            weights.start([0], (0,))
            for load in loads[1]:
                load.start()
            weights.start([1], (0,))
            for load in loads[2]:
                load.start()
            weights.start([2], (0,))
            inputs[6].start()
        for load in loads[j]:
            load.wait()
        if j == 0:
            for copy in copies:
                copy.wait()
        t, sig, mixed, kf, vf = (h[j].astype(F32) for h in held)
        dc = (grad_gated * mixed * (sig * (1.0 - sig))).astype(BF16)
        df = transform_once(spots[0][...], grad_gated * sig)
        kr, ki, vr, vi = kf[:half], kf[half:], vf[:half], vf[half:]
        dr, di = df[:half] * scale, df[half:] * scale
        divi, diki = di * vi, di * ki
        dkr = dr * vr + jnp.where(edge, 0.0, divi)
        dki = jnp.where(edge, divi, di * vr - dr * vi)
        dvr = dr * kr + jnp.where(edge, 0.0, diki)
        dvi = jnp.where(edge, diki, di * kr - dr * ki)
        du = transform_once(spots[1][...], jnp.concatenate([dkr, dki], axis=0))
        dv = (transform_once(spots[1][...], jnp.concatenate([dvr, dvi], axis=0)) * mask).astype(BF16)
        inverse = [lax.rsqrt(s + 1e-05) for s in row_sums(bucket, t * t, tok_count)]
        dots = row_sums(bucket, du * t, tok_count)
        coupling = [d * i * i * i for d, i in zip(dots, inverse)]
        dt = du * over_rows(inverse, tok_count) - t * over_rows(coupling, tok_count)
        da = (dt * mask * (1.0 - t * t)).astype(BF16)
        if j == 0:
            for copy in inputs[4:6]:
                copy.wait()
        normed, gated = normed_ref[...], gated_ref[...]
        for i, (one, two) in enumerate(
            ((mm_tn(normed, da), mm_tn(normed, dv)), (mm_tn(normed, dc), mm_tn(gated, low[:, at])))
        ):
            to = slice((2 * j + i) * tile, (2 * j + i + 1) * tile)
            g0[:, to] = one.astype(BF16)
            g1[:, to] = two.astype(BF16)
        if j < TILES - 1:
            put(j, lambda copy: copy.start())
        weights.wait(j, (0,))
        part = (
            mm_nt(da, first[j][:, :tile]) + mm_nt(dc, first[j][:, tile : 2 * tile]) + mm_nt(dv, second[j][:, :tile])
        )
        if j == 0:
            acc_ref[...] = part
        else:
            acc_ref[...] += part
    inputs[6].wait()
    back, terms = rms_back(x_ref[...].astype(F32), gain_ref[0:1, :], acc_ref[...])
    gain1 = jnp.sum(terms, axis=0, keepdims=True)
    extras = jnp.concatenate([gain1, gain2, norm_ref[...], jnp.zeros((LANES - 3, width), F32)], axis=0).T
    g0[:, 2 * width :] = extras.astype(BF16)
    g1[:, 2 * width :] = jnp.zeros((width, LANES), BF16)
    put(TILES - 1, lambda copy: copy.start())
    tok_ref[...] = (gm_ref[...] + back).astype(BF16)
    for j in range(TILES):
        put(j, lambda copy: copy.wait())


def mix_back(facts, x, cot, gains, mid, own, sib, normed, gated, norms, kept, carried, sibling, tables):
    tok, width = x.shape
    assert TILES * (width // TILES) == width
    part = jax.ShapeDtypeStruct((width, 2 * width + LANES), BF16)
    spots = [(tok, width)] * 7
    kinds = [BF16] * 7
    return pl.pallas_call(
        mix_back_kernel,
        in_specs=[pl.BlockSpec(memory_space=pltpu.SMEM), INSIDE, INSIDE, *[ANY] * (7 + 5 + 2 + 2)],
        out_specs=[INSIDE, ANY, ANY],
        out_shape=[jax.ShapeDtypeStruct((tok, width), BF16), part, part],
        scratch_shapes=[
            tuple(pltpu.VMEM(shape, kind) for shape, kind in zip(spots, kinds)),
            half_spots(width), half_spots(width), table_spots(tok, 2),
            tuple(pltpu.VMEM(k.shape, k.dtype) for k in kept),
            pltpu.VMEM(part.shape, BF16), pltpu.VMEM(part.shape, BF16),
            pltpu.VMEM((tok, width), F32), pltpu.VMEM((tok, width), F32),
            pltpu.SemaphoreType.DMA((7,)), pltpu.SemaphoreType.DMA((2, TILES)), pltpu.SemaphoreType.DMA((2,)),
            pltpu.SemaphoreType.DMA((5, TILES)), pltpu.SemaphoreType.DMA((2, TILES)),
        ],
        compiler_params=pltpu.CompilerParams(vmem_limit_bytes=VMEM_BYTES),
        name="mix_back",
    )(facts, gains, norms, own, sib, mid, cot, gated, normed, x, *kept, carried, sibling, tables[0], tables[2])


UNIT_TILES = 4


def ffn_kernel(facts, nfo_ref, nfs_ref, gfo_ref, gfs_ref, *refs):
    pieces, refs = refs[:6], refs[6:]
    nf_ref, h_ref, dgu_ref, kept_ref, sent_ref, wgu_ref, wd_ref, gf_ref, gu, downs, sems, down_sems = refs
    step = pl.program_id(0)
    tok, width = nfo_ref.shape
    units = h_ref.shape[1]
    span = gu.shape[2]
    bits = [facts[2 + ROW_SLOTS + i] for i in range(3)]

    def copies(t):
        chain, column = divmod(t, UNIT_TILES // 2)
        for side in range(2):
            half = bits[chain] if side == 0 else 1 - bits[chain]
            piece = pieces[2 * chain + side]
            count = piece.shape[1]
            for b in range(piece.shape[0]):
                yield pltpu.make_async_copy(
                    piece.at[b, :, :, pl.ds(2 * units * column, 2 * units)],
                    gu.at[t, pl.ds((2 * b + half) * count, count)],
                    sems.at[t, side, b],
                )

    def down_copies():
        for side in range(2):
            half = bits[2] if side == 0 else 1 - bits[2]
            yield pltpu.make_async_copy(pieces[4 + side], downs.at[:, half], down_sems.at[side])

    @pl.when(step == 0)
    def _():
        for copy in [*copies(0), *down_copies()]:
            copy.start()
        for t in range(1, UNIT_TILES):
            for copy in copies(t):
                copy.start()
        nf_ref[:tok] = nfo_ref[...]
        nf_ref[tok:] = nfs_ref[...]
        gf_ref[:tok] = gfo_ref[...]
        gf_ref[tok:] = gfs_ref[...]

    for t in range(UNIT_TILES):

        @pl.when(step == t)
        def _():
            for copy in copies(t):
                copy.wait()

    @pl.when(step == 0)
    def _():
        for copy in down_copies():
            copy.wait()

    nf, gf = nf_ref[...], gf_ref[...]
    wgu = gu[step].reshape(gu.shape[1] * span, 2 * units)
    wd = downs.reshape(UNIT_TILES * units, width)[pl.ds(pl.multiple_of(step * units, units), units)]
    wgu_ref[...], wd_ref[...] = wgu, wd
    both = mm(nf, wgu)
    g, u = both[:, :units], both[:, units:]
    dh = mm_nt(gf, wd)
    sig = 0.5 + 0.5 * jnp.tanh(0.5 * g)
    silu = g * sig
    h = (silu * u).astype(BF16)
    h_ref[...] = h
    dgu_ref[:, units:] = (dh * silu).astype(BF16)
    dgu_ref[:, :units] = (dh * u * (sig * (1.0 + g * (1.0 - sig)))).astype(BF16)
    gd = mm_tn(h, gf).astype(BF16).reshape(sent_ref.shape[0], 2, *sent_ref.shape[1:])
    kept_ref[...] = jnp.where(bits[2] == 0, gd[:, 0], gd[:, 1])
    sent_ref[...] = jnp.where(bits[2] == 0, gd[:, 1], gd[:, 0])


def ffn(facts, nf_own, nf_sib, gf_own, gf_sib, pieces):
    tok, width = nf_own.shape
    total_units = pieces[0].shape[2]
    units = total_units // UNIT_TILES
    span = min(pieces[0].shape[1], pieces[2].shape[1])
    cut = [p.reshape(p.shape[0], p.shape[1] // span, span, p.shape[2]) for p in pieces[:4]]
    below, above = pieces[4].shape[1], pieces[4].shape[0]
    whole = pl.BlockSpec((tok, width), lambda j: (0, 0))
    tall = pl.BlockSpec((width, 2 * units), lambda j: (0, j))
    flat = pl.BlockSpec((units, width), lambda j: (j, 0))
    return pl.pallas_call(
        ffn_kernel,
        grid=(UNIT_TILES,),
        in_specs=[pl.BlockSpec(memory_space=pltpu.SMEM), whole, whole, whole, whole, *[ANY] * 6],
        out_specs=[
            pl.BlockSpec((2 * tok, width), lambda j: (0, 0)),
            pl.BlockSpec((2 * tok, units), lambda j: (0, j)),
            pl.BlockSpec((2 * tok, 2 * units), lambda j: (0, j)),
            *[pl.BlockSpec((above // UNIT_TILES, below, width), lambda j: (j, 0, 0))] * 2,
            tall, flat,
        ],
        out_shape=[
            jax.ShapeDtypeStruct((2 * tok, width), BF16),
            jax.ShapeDtypeStruct((2 * tok, total_units), BF16),
            jax.ShapeDtypeStruct((2 * tok, 2 * total_units), BF16),
            *[jax.ShapeDtypeStruct((above, below, width), BF16)] * 2,
            jax.ShapeDtypeStruct((width, 2 * total_units), BF16),
            jax.ShapeDtypeStruct((total_units, width), BF16),
        ],
        scratch_shapes=[
            pltpu.VMEM((2 * tok, width), BF16),
            pltpu.VMEM((UNIT_TILES, width // span, span, 2 * units), BF16),
            pltpu.VMEM((above, 2, below, width), BF16),
            pltpu.SemaphoreType.DMA((UNIT_TILES, 2, max(p.shape[0] for p in cut))),
            pltpu.SemaphoreType.DMA((2,)),
        ],
        compiler_params=pltpu.CompilerParams(vmem_limit_bytes=VMEM_BYTES),
        name="ffn",
    )(facts, nf_own, nf_sib, gf_own, gf_sib, *cut, *pieces[4:])


def pack_mixer_kernel(place, in_ref, out_ref, gain_ref, mine_ref, send_ref):
    core = place[0]
    width = out_ref.shape[1]
    tile = width // TILES
    for j in range(TILES):
        at = slice(j * tile, (j + 1) * tile)
        pairs = (
            (in_ref[:, j * tile : (j + 1) * tile], in_ref[:, 2 * width + j * tile : 2 * width + (j + 1) * tile]),
            (in_ref[:, width + j * tile : width + (j + 1) * tile], out_ref[:, at]),
        )
        for i, (one, two) in enumerate(pairs):
            to = slice((2 * j + i) * tile, (2 * j + i + 1) * tile)
            mine_ref[:, to] = jnp.where(core == 0, one, two)
            send_ref[:, to] = jnp.where(core == 0, two, one)
    mine_ref[:, 2 * width :] = gain_ref[...]
    send_ref[:, 2 * width :] = gain_ref[...]


def pack_mixer(place, w_in, w_out, gains):
    rows, width = w_out.shape
    return pl.pallas_call(
        pack_mixer_kernel,
        in_specs=[pl.BlockSpec(memory_space=pltpu.SMEM), INSIDE, INSIDE, INSIDE],
        out_specs=[INSIDE, INSIDE],
        out_shape=[jax.ShapeDtypeStruct((rows, 2 * width + LANES), BF16)] * 2,
        name="pack_mixer",
    )(place, w_in, w_out, gains)


def pack_units_kernel(place, gu_ref, order_ref, mine_ref, send_ref, stack_ref):
    core = place[0]
    rows = gu_ref.shape[0]
    width = order_ref.shape[0]
    half = width // 2
    groups = gu_ref.shape[1] // width
    pitch = stack_ref.shape[0] // groups
    for i in range(groups):
        stack_ref[i * pitch : i * pitch + rows] = gu_ref[:, i * width : (i + 1) * width].astype(F32)
    sorted_rows = mm(stack_ref[...].astype(BF16), order_ref[...])
    for i in range(groups):
        block = sorted_rows[i * pitch : i * pitch + rows]
        spot = 2 * i if i < groups // 2 else 2 * i - groups + 1
        to = slice(spot * half, (spot + 1) * half)
        mine_ref[:, to] = jnp.where(core == 0, block[:, :half], block[:, half:]).astype(BF16)
        send_ref[:, to] = jnp.where(core == 0, block[:, half:], block[:, :half]).astype(BF16)


def pack_units(place, w_gu, order):
    rows, columns = w_gu.shape
    width = order.shape[0]
    pitch = -(-rows // 8) * 8
    return pl.pallas_call(
        pack_units_kernel,
        in_specs=[pl.BlockSpec(memory_space=pltpu.SMEM), INSIDE, INSIDE],
        out_specs=[INSIDE, INSIDE],
        out_shape=[jax.ShapeDtypeStruct((rows, columns // 2), BF16)] * 2,
        scratch_shapes=[pltpu.VMEM((columns // width * pitch, width), F32)],
        name="pack_units",
    )(place, w_gu, order)


def unpack_mixer_kernel(place, own_ref, far_ref, in_ref, out_ref, extra_ref):
    core = place[0]
    width = out_ref.shape[1]
    tile = width // TILES
    own, far = own_ref[...].astype(F32), far_ref[...].astype(F32)
    for j in range(TILES):
        for i in range(2):
            at = slice((2 * j + i) * tile, (2 * j + i + 1) * tile)
            one = jnp.where(core == 0, own[:, at], far[:, at])
            two = jnp.where(core == 0, far[:, at], own[:, at])
            in_ref[:, i * width + j * tile : i * width + (j + 1) * tile] = one
            if i == 0:
                in_ref[:, 2 * width + j * tile : 2 * width + (j + 1) * tile] = two
            else:
                out_ref[:, j * tile : (j + 1) * tile] = two
    extra_ref[...] = jnp.where(core == 0, own[:, 2 * width :], far[:, 2 * width :]).T[:8]


def unpack_mixer(place, own, far, width):
    rows = own.shape[0]
    return pl.pallas_call(
        unpack_mixer_kernel,
        in_specs=[pl.BlockSpec(memory_space=pltpu.SMEM), INSIDE, INSIDE],
        out_specs=[INSIDE] * 3,
        out_shape=[jax.ShapeDtypeStruct(shape, F32) for shape in ((rows, 3 * width), (rows, width), (8, rows))],
        name="unpack_mixer",
    )(place, own, far)


def unpack_units_kernel(place, own_ref, far_ref, order_ref, gu_ref, stack_ref):
    core = place[0]
    rows = gu_ref.shape[0]
    width = order_ref.shape[0]
    half = width // 2
    groups = gu_ref.shape[1] // width
    pitch = stack_ref.shape[0] // groups
    own, far = own_ref[...].astype(F32), far_ref[...].astype(F32)
    for i in range(groups):
        spot = 2 * i if i < groups // 2 else 2 * i - groups + 1
        at = slice(spot * half, (spot + 1) * half)
        to = slice(i * pitch, i * pitch + rows)
        stack_ref[to, :half] = jnp.where(core == 0, own[:, at], far[:, at])
        stack_ref[to, half:] = jnp.where(core == 0, far[:, at], own[:, at])
    sorted_rows = mm_nt(stack_ref[...].astype(BF16), order_ref[...])
    for i in range(groups):
        gu_ref[:, i * width : (i + 1) * width] = sorted_rows[i * pitch : i * pitch + rows]


def unpack_units(place, own, far, order):
    rows, columns = own.shape
    width = order.shape[0]
    pitch = -(-rows // 8) * 8
    return pl.pallas_call(
        unpack_units_kernel,
        in_specs=[pl.BlockSpec(memory_space=pltpu.SMEM), INSIDE, INSIDE, INSIDE],
        out_specs=INSIDE,
        out_shape=jax.ShapeDtypeStruct((rows, 2 * columns), F32),
        scratch_shapes=[pltpu.VMEM((2 * columns // width * pitch, width), F32)],
        name="unpack_units",
    )(place, own, far, order)


class Links:
    def __init__(self):
        self.outer = lax.axis_size("outer")
        self.narrow = lax.axis_size("narrow")
        self.core = lax.axis_index("core")
        self.bits = []
        for axis, size in (("outer", self.outer), ("narrow", self.narrow)):
            spot = lax.axis_index(axis)
            span = size
            while span > 1:
                span //= 2
                self.bits.append((axis, size, span, (spot // span) % 2))
        self.outer_bits = sum(bit[0] == "outer" for bit in self.bits)

    def chain(self, turn):
        rest = list(range(1, len(self.bits)))
        turn %= len(rest)
        return [0] + rest[turn:] + rest[:turn]

    def narrow_last(self):
        return [0] + [p for p in range(1, len(self.bits)) if p != self.outer_bits] + [self.outer_bits]

    def swap_core(self, values):
        return lax.ppermute(values, "core", [(0, 1), (1, 0)])

    def exchange(self, values, p):
        axis, size, stride, _ = self.bits[p]
        return lax.ppermute(values, axis, [(i, i ^ stride) for i in range(size)])

    def split(self, p, have, middle, rows):
        before = 2 ** sum(q < p for q in have)
        after = 2 ** sum(q > p for q in have)
        if p < self.outer_bits:
            return before, after * middle * rows
        return before * middle, after * rows

    def gather_step(self, block, p, have, middle):
        rows = block.shape[0] // (middle * 2 ** len(have))
        before, after = self.split(p, have, middle, rows)
        mine = block.reshape(before, 1, after, block.shape[1])
        other = self.exchange(block, p).reshape(mine.shape)
        bit = self.bits[p][3]
        side = lax.broadcasted_iota(jnp.int32, (1, 2, 1, 1), 1)
        both = jnp.where(side == bit, mine, other)
        return both.reshape(-1, block.shape[1])

    def gather_pieces(self, block, p, have, middle):
        rows = block.shape[0] // (middle * 2 ** len(have))
        before, after = self.split(p, have, middle, rows)
        shape = (before, after, block.shape[1])
        return block.reshape(shape), self.exchange(block, p).reshape(shape)

    def far_gather(self, blocks):
        rows = blocks[0].shape[0]
        flat = [b[i : i + rows] for b in blocks for i in range(0, b.shape[0], rows)]
        got = self.exchange(jnp.concatenate(flat, axis=1), 0)
        side = lax.broadcasted_iota(jnp.int32, (2, 1, 1), 0)
        grown, at = [], 0
        for b in blocks:
            other = []
            for _ in range(b.shape[0] // rows):
                other.append(got[:, at : at + b.shape[1]])
                at += b.shape[1]
            other = jnp.concatenate(other, axis=0)
            grown.append(jnp.where(side == self.bits[0][3], b[None], other[None]).reshape(-1, b.shape[1]))
        return grown

    def spread(self, block, middle):
        shape = (2,) * self.outer_bits + (middle,) + (2,) * (len(self.bits) - self.outer_bits)
        return [block.reshape(*shape, block.shape[0] // math.prod(shape), block.shape[1])]

    def spread_half(self, block, p):
        shape = [2] * self.outer_bits + [1] + [2] * (len(self.bits) - self.outer_bits)
        shape[p if p < self.outer_bits else p + 1] = 1
        return block.reshape(*shape, -1, block.shape[-1])

    def side(self, terms, p, other):
        bit = self.bits[p][3]
        dim = p if p < self.outer_bits else p + 1
        return [lax.dynamic_slice_in_dim(t, 1 - bit if other else bit, 1, dim) for t in terms]

    def scatter_step(self, terms, p):
        return [*self.side(terms, p, False), self.exchange(total(self.side(terms, p, True)), p)]

    def far_scatter(self, blocks):
        sent = [flat(total(self.side(terms, 0, True))) for terms in blocks]
        rows = sent[0].shape[0]
        cut = [m[i : i + rows] for m in sent for i in range(0, m.shape[0], rows)]
        got = self.exchange(jnp.concatenate(cut, axis=1), 0)
        sums, at = [], 0
        for terms, m in zip(blocks, sent):
            other = []
            for _ in range(m.shape[0] // rows):
                other.append(got[:, at : at + m.shape[1]])
                at += m.shape[1]
            kept = [flat(t) for t in self.side(terms, 0, False)]
            sums.append(total([*kept, jnp.concatenate(other, axis=0)]))
        return sums


def total(terms):
    return sum(t.astype(F32) for t in terms).astype(BF16)


def flat(block):
    return block.reshape(-1, block.shape[-1])


def unit_order(width, chunk):
    columns = np.arange(width)
    pairs = width // (2 * chunk)
    source = np.concatenate(
        [np.concatenate([(2 * i + core) * chunk + np.arange(chunk) for i in range(pairs)]) for core in range(2)]
    )
    return (columns[:, None] == source[None, :]).astype(ml_dtypes.bfloat16)


def on_device(tokens, cotangent, w_in, w_out, w_gu, w_down, gain_mix, gain_ffn, buckets, lengths):
    links = Links()
    core = links.core
    tok, width = tokens.shape
    rows = w_in.shape[0]
    ff = w_gu.shape[1] // 2
    units = ff // 2
    tile = width // TILES
    fence = lax.optimization_barrier

    tables = [jnp.asarray(t) for t in transform_tables(tok)]
    order = jnp.asarray(unit_order(width, ff // (2 * links.outer)))
    chains = [links.chain(2), links.chain(1), links.narrow_last()]
    bits = [links.bits[chain[-1]][3] for chain in chains]
    facts = jnp.concatenate([buckets, lengths[0], jnp.stack([core, *bits])]).astype(jnp.int32)
    middles = [2, 2, 1]
    count = len(links.bits)

    def grow(blocks, k, middles):
        return [links.gather_step(b, chain[k], set(chain[:k]), m) for b, chain, m in zip(blocks, chains, middles)]

    def shrink(blocks, k):
        return [links.scatter_step(terms, chain[k]) for terms, chain in zip(blocks, chains)]

    def both_rows(mine, send):
        other = links.swap_core(send)
        side = lax.broadcasted_iota(jnp.int32, (2, 1, 1), 0)
        return jnp.where(side == core, mine[None], other[None]).reshape(2 * mine.shape[0], mine.shape[1])

    lane = lax.broadcasted_iota(jnp.int32, (rows, LANES), 1)
    gains = jnp.where(lane == 0, gain_mix[:, None], jnp.where(lane == 1, gain_ffn[:, None], 0))
    place = core.reshape(1).astype(jnp.int32)
    mine, send = pack_mixer(place, w_in, w_out, gains)
    mine_gu, send_gu = pack_units(place, w_gu, order)
    mixer = links.gather_step(both_rows(mine, send), 0, set(), 2)
    gu = both_rows(mine_gu, send_gu)
    mixer, gu, wd = fence((mixer, gu, w_down))
    mask = pad_mask(facts[0], [facts[1 + i] for i in range(ROW_SLOTS)], (tok, 1), tok)
    gf = (fence((cotangent, mixer))[0].astype(F32) * mask).astype(BF16)
    gu, wd = links.far_gather([gu, wd])
    cuts = [0, 5 * LANES, 10 * LANES, mine.shape[1]]
    parts = [mixer[:, a:b] for a, b in zip(cuts[:-1], cuts[1:])]
    weights = [gu[:, :units], gu[:, units:], wd]
    for k in range(1, count):
        parts = grow(parts, k, [2] * TILES)
    for k in range(1, count - 1):
        weights = grow(weights, k, middles)
    parts = fence((parts, weights, gf))[0]
    parts = jnp.concatenate(parts, axis=1)
    siblings = links.swap_core(parts)

    normed, gated, mid, low_mid, nf, norms, gains, *kept = mix_forward(facts, tokens, parts, siblings, tables)

    nf = fence((nf, weights))[0]
    pieces = [
        piece
        for w, chain, m in zip(weights, chains, middles)
        for piece in links.gather_pieces(w, chain[-1], set(chain[:-1]), m)
    ]

    nf, gf = fence((nf, gf))
    nf2, h, dgu, down_kept, down_sent, wgu, wd = ffn(facts, nf, links.swap_core(nf), gf, links.swap_core(gf), pieces)
    back = mm_nt(dgu, wgu).astype(BF16)
    back_sib = links.swap_core(back[tok:])
    grad_gu = mm_tn(nf2, dgu).astype(BF16)
    grads = [links.spread(g, 2) for g in (grad_gu[:, :units], grad_gu[:, units:])]
    last = chains[2][-1]
    down_terms = [links.spread_half(m, last) for m in (down_kept, down_sent)]
    down_terms[1] = links.exchange(down_terms[1], last)
    grads = shrink(grads, count - 1) + [down_terms]

    devices = 2 * links.outer * links.narrow
    grad_tokens, keep, send = mix_back(
        facts, tokens, cotangent, gains, low_mid, back, back_sib, normed, gated, norms * (1.0 / devices), kept,
        parts, siblings, tables,
    )
    grads, keep, send, h = fence((grads, keep, send, h))
    sums = total([keep, links.swap_core(send)])
    sums = [links.spread(sums[:, a:b], 2) for a, b in zip(cuts[:-1], cuts[1:])]
    sent = [total(links.side(terms, chain[-1], True)) for terms, chain in zip(sums, chains)]
    kept = [links.side(terms, chain[-1], False) for terms, chain in zip(sums, chains)]
    grads = shrink(grads, count - 2)
    grads, sent, kept = fence((grads, sent, kept))
    for k in reversed(range(1, count - 2)):
        grads = shrink(grads, k)
    grads, h, held = fence((grads, h, sent[-1]))
    sent = [*sent[:-1], held]
    sums = [[total([*k, links.exchange(m, chain[-1])])] for k, m, chain in zip(kept, sent, chains)]
    out = mm(h, wd).astype(BF16)
    out_sib = links.swap_core(out[tok:])
    layer_out = ((mid + out[:tok].astype(F32) + out_sib.astype(F32)) * mask).astype(BF16)
    for k in reversed(range(1, count - 1)):
        sums = [[total(terms)] for terms in shrink(sums, k)]
    sum_gate, sum_up, sum_down = links.far_scatter(grads)
    def own_and_far(block):
        halves = block.reshape(2, rows, block.shape[1])
        own = lax.dynamic_index_in_dim(halves, core, 0, keepdims=False)
        return own, links.swap_core(lax.dynamic_index_in_dim(halves, 1 - core, 0, keepdims=False))

    grad_w_gu = unpack_units(place, *own_and_far(jnp.concatenate([sum_gate, sum_up], axis=1)), order)
    sums = links.far_scatter(sums)
    sums, grad_w_gu = fence((sums, grad_w_gu))
    grad_w_in, grad_w_out, extra = unpack_mixer(place, *own_and_far(jnp.concatenate(sums, axis=1)), width)
    return (
        layer_out, grad_tokens, grad_w_in, grad_w_out, grad_w_gu, sum_down.astype(F32), extra[0], extra[1], extra[2],
    )


def solution(mesh):
    wide, narrow = mesh.devices.shape
    split = jax.sharding.Mesh(mesh.devices.reshape(wide // 2, 2, narrow), ("outer", "core", "narrow"))
    every = ("outer", "core", "narrow")
    flat, tall = P(every), P(every, None)
    return jax.shard_map(
        on_device,
        mesh=split,
        in_specs=(tall, tall, tall, tall, tall, tall, flat, flat, flat, tall),
        out_specs=(tall, tall, tall, tall, tall, tall, flat, flat, flat),
        check_vma=False,
    )
```

```python
import math

import jax
import jax.numpy as jnp
import ml_dtypes
import numpy as np
from jax import lax
from jax.experimental import pallas as pl
from jax.experimental.pallas import tpu as pltpu
from jax.sharding import PartitionSpec as P

F32 = jnp.float32
BF16 = jnp.bfloat16
ROW_SLOTS = 4
BUCKETS = 3
VMEM_BYTES = 56 * 1024 * 1024


def transform_tables(tok_count):
    highs, lows = [], []
    for bucket in range(BUCKETS):
        rows = ROW_SLOTS >> bucket
        length = tok_count // rows
        half = length // 2
        angle = 2.0 * np.pi * (np.arange(half)[:, None] * np.arange(length)[None, :] % length) / length
        real = np.cos(angle) * np.sqrt(2.0 / length)
        imag = -np.sin(angle) * np.sqrt(2.0 / length)
        real[0] = 1.0 / np.sqrt(length)
        imag[0] = (1.0 - 2.0 * (np.arange(length) % 2)) / np.sqrt(length)
        table = np.zeros((tok_count, tok_count))
        for row in range(rows):
            at = slice(row * length, (row + 1) * length)
            table[row * half : (row + 1) * half, at] = real
            table[tok_count // 2 + row * half : tok_count // 2 + (row + 1) * half, at] = imag
        high = table.astype(ml_dtypes.bfloat16)
        highs.append(high)
        lows.append((table - high.astype(np.float64)).astype(ml_dtypes.bfloat16))
    high, low = np.stack(highs), np.stack(lows)
    return high, low, np.ascontiguousarray(high.transpose(0, 2, 1)), np.ascontiguousarray(low.transpose(0, 2, 1))


def mm(left, right):
    return jnp.dot(left, right, preferred_element_type=F32)


def mm_nt(left, right):
    return lax.dot_general(left, right, (((1,), (1,)), ((), ())), preferred_element_type=F32)


def mm_tn(left, right):
    return lax.dot_general(left, right, (((0,), (0,)), ((), ())), preferred_element_type=F32)


def transform(high, low, values):
    top = values.astype(BF16)
    rest = (values - top.astype(F32)).astype(BF16)
    return mm(high, top) + (mm(high, rest) + mm(low, top))


def transform_once(table, values):
    return mm(table, values.astype(BF16))


def bin_facts(bucket, shape, tok_count):
    half = lax.shift_left(jnp.int32(tok_count // (2 * ROW_SLOTS)), bucket)
    spot = lax.broadcasted_iota(jnp.int32, shape, 0)
    edge = (spot & (half - 1)) == 0
    length = (2 * half).astype(F32)
    scale = jnp.where(edge, jnp.sqrt(length), jnp.sqrt(0.5 * length))
    return edge, scale


def pad_mask(bucket, lengths, shape, tok_count):
    quarter = tok_count // ROW_SLOTS
    shift = (quarter.bit_length() - 1) + bucket
    spot = lax.broadcasted_iota(jnp.int32, shape, 0)
    slot = lax.shift_right_logical(spot, jnp.broadcast_to(shift, shape))
    within = spot - lax.shift_left(slot, jnp.broadcast_to(shift, shape))
    length = jnp.where(
        slot == 0, lengths[0], jnp.where(slot == 1, lengths[1], jnp.where(slot == 2, lengths[2], lengths[3]))
    )
    return (within < length).astype(F32)


def widen(values, width):
    return jnp.concatenate([values] * (width // values.shape[1]), axis=1)


def row_sums(bucket, values, tok_count):
    quarter = tok_count // ROW_SLOTS
    s = [jnp.sum(values[i * quarter : (i + 1) * quarter], axis=0, keepdims=True) for i in range(ROW_SLOTS)]
    left, right = s[0] + s[1], s[2] + s[3]
    whole = left + right
    pairs = (left, left, right, right)
    return [jnp.where(bucket == 0, s[i], jnp.where(bucket == 1, pairs[i], whole)) for i in range(ROW_SLOTS)]


def over_rows(parts, tok_count):
    quarter = tok_count // ROW_SLOTS
    return jnp.concatenate([jnp.broadcast_to(p, (quarter, p.shape[1])) for p in parts], axis=0)


TILES = 3
LANES = 128
ANY = pl.BlockSpec(memory_space=pl.ANY)
INSIDE = pl.BlockSpec(memory_space=pltpu.VMEM)


class Weights:
    def __init__(self, core, carried, sibling, halves, sems):
        self.core, self.carried, self.sibling, self.halves, self.sems = core, carried, sibling, halves, sems

    def copies(self, i, first, second):
        spot = self.halves[0][i]
        at = (slice(None), pl.ds(i * self.halves[0][0].shape[1], spot.shape[1]))
        return (
            lambda: pltpu.make_async_copy(first.at[at], spot, self.sems.at[0, i]),
            lambda: pltpu.make_async_copy(second.at[at], self.halves[1][i], self.sems.at[1, i]),
        )

    def start(self, order, sides=(0, 1)):
        @pl.when(self.core == 0)
        def _():
            for i in order:
                for side in sides:
                    self.copies(i, self.carried, self.sibling)[side]().start()

        @pl.when(self.core != 0)
        def _():
            for i in order:
                for side in sides:
                    self.copies(i, self.sibling, self.carried)[side]().start()

    def wait(self, i, sides=(0, 1)):
        for side in sides:
            self.copies(i, self.carried, self.sibling)[side]().wait()


def load_tables(bucket, tables, spots, sems):
    copies = [pltpu.make_async_copy(t.at[bucket], s, sems.at[i]) for i, (t, s) in enumerate(zip(tables, spots))]
    for copy in copies:
        copy.start()
    return copies


def mix_forward_kernel(facts, x_ref, *refs):
    carried, sibling, tables = refs[0], refs[1], refs[2:6]
    (
        normed_ref, gated_ref, mid_ref, low_mid_ref, nf_ref, norm_ref, gain_ref, t_out, s_out, mix_out, kf_out, vf_out,
        first, second, spots, kept, w_sems, t_sems, k_sems,
    ) = refs[6:]
    tok_count, width = x_ref.shape
    tile = width // TILES
    bucket = facts[0]
    lengths = [facts[1 + i] for i in range(ROW_SLOTS)]
    weights = Weights(facts[1 + ROW_SLOTS], carried, sibling, (first, second), w_sems)
    weights.start([TILES - 1, *range(TILES - 1)])
    copies = load_tables(bucket, tables, spots, t_sems)
    x = x_ref[...].astype(F32)
    r = lax.rsqrt(jnp.mean(x * x, axis=-1, keepdims=True) + 1e-06)
    scaled = x * r
    mask = pad_mask(bucket, lengths, (tok_count, tile), tok_count)
    weights.wait(TILES - 1)
    gains = first[TILES - 1][:, 2 * tile :].astype(F32).T[:8]
    gain_ref[...] = gains
    normed = (scaled * gains[0:1]).astype(BF16)
    normed_ref[...] = normed
    edge, scale = bin_facts(bucket, (tok_count // 2, tile), tok_count)
    half = tok_count // 2
    outs = (t_out, s_out, mix_out, kf_out, vf_out)
    stores = []
    for n, j in enumerate([TILES - 1, *range(TILES - 1)]):
        if n > 0:
            weights.wait(j)
        at = slice(j * tile, (j + 1) * tile)
        a = mm(normed, first[j][:, :tile])
        c = mm(normed, first[j][:, tile : 2 * tile])
        v = mm(normed, second[j][:, :tile]) * mask
        t = jnp.tanh(a) * mask
        norms = [jnp.sqrt(s + 1e-05) for s in row_sums(bucket, t * t, tok_count)]
        norm_ref[:, at] = (norms[0] + norms[1] + norms[2] + norms[3]) * (1.0 / ROW_SLOTS)
        unit = t * over_rows([1.0 / n for n in norms], tok_count)
        if n == 0:
            for copy in copies:
                copy.wait()
        kf = transform(spots[0][...], spots[1][...], unit)
        vf = transform(spots[0][...], spots[1][...], v)
        kr, ki, vr, vi = kf[:half], kf[half:], vf[:half], vf[half:]
        kivi = ki * vi
        pr = (kr * vr - jnp.where(edge, 0.0, kivi)) * scale
        pi = jnp.where(edge, kivi, kr * vi + ki * vr) * scale
        mixed = transform(spots[2][...], spots[3][...], jnp.concatenate([pr, pi], axis=0))
        sig = 1.0 / (1.0 + jnp.exp(-c))
        gated_ref[:, at] = (mixed * sig * mask).astype(BF16)
        for i, value in enumerate((t, sig, mixed, kf, vf)):
            kept[i][j] = value.astype(kept[i].dtype)
            store = pltpu.make_async_copy(kept[i].at[j], outs[i].at[j], k_sems.at[i, j])
            store.start()
            stores.append(store)
    gated = gated_ref[...]
    for i in range(TILES):
        at = slice(i * tile, (i + 1) * tile)
        mid_ref[:, at] = x_ref[:, at].astype(F32) + mm(gated, second[i][:, tile : 2 * tile])
    mid = mid_ref[...]
    low_mid_ref[...] = mid.astype(BF16)
    r = lax.rsqrt(jnp.mean(mid * mid, axis=-1, keepdims=True) + 1e-06)
    nf_ref[...] = (mid * r * gains[1:2]).astype(BF16)
    for store in stores:
        store.wait()


def table_spots(tok, count=4):
    return tuple(pltpu.VMEM((tok, tok), BF16) for _ in range(count))


def half_spots(width):
    tile = width // TILES
    shapes = [(width, 2 * tile)] * (TILES - 1) + [(width, 2 * tile + LANES)]
    return tuple(pltpu.VMEM(shape, BF16) for shape in shapes)


def mix_forward(facts, x, carried, sibling, tables):
    tok, width = x.shape
    tile = width // TILES
    kinds = (F32, F32, BF16, BF16, BF16)
    return pl.pallas_call(
        mix_forward_kernel,
        in_specs=[pl.BlockSpec(memory_space=pltpu.SMEM), INSIDE, *[ANY] * 6],
        out_specs=[*[INSIDE] * 7, *[ANY] * 5],
        out_shape=[
            jax.ShapeDtypeStruct((tok, width), BF16), jax.ShapeDtypeStruct((tok, width), BF16),
            jax.ShapeDtypeStruct((tok, width), F32), jax.ShapeDtypeStruct((tok, width), BF16),
            jax.ShapeDtypeStruct((tok, width), BF16), jax.ShapeDtypeStruct((1, width), F32), jax.ShapeDtypeStruct((8, width), F32),
            *[jax.ShapeDtypeStruct((TILES, tok, tile), kind) for kind in kinds],
        ],
        scratch_shapes=[
            half_spots(width), half_spots(width), table_spots(tok),
            tuple(pltpu.VMEM((TILES, tok, tile), kind) for kind in kinds),
            pltpu.SemaphoreType.DMA((2, TILES)), pltpu.SemaphoreType.DMA((4,)), pltpu.SemaphoreType.DMA((5, TILES)),
        ],
        compiler_params=pltpu.CompilerParams(vmem_limit_bytes=VMEM_BYTES),
        name="mix_forward",
    )(facts, x, carried, sibling, *tables)


def rms_back(values, gain, grad):
    r = lax.rsqrt(jnp.mean(values * values, axis=-1, keepdims=True) + 1e-06)
    scaled = values * r
    inner = grad * gain
    dot = jnp.mean(inner * scaled, axis=-1, keepdims=True)
    return r * (inner - scaled * dot), grad * scaled


def mix_back_kernel(facts, gain_ref, norm_ref, *refs):
    streams, residuals, (carried, sibling), tables, refs = refs[:7], refs[7:12], refs[12:14], refs[14:16], refs[16:]
    (tok_ref, keep, send), (spots_in, first, second, spots, held, g0, g1, gm_ref, acc_ref), sems = refs[:3], refs[3:12], refs[12:]
    s_sems, w_sems, t_sems, k_sems, o_sems = sems
    back_ref, sib_ref, mid_ref, cot_ref, gated_ref, normed_ref, x_ref = spots_in
    tok_count, width = x_ref.shape
    tile = width // TILES
    half = tok_count // 2
    bucket = facts[0]
    lengths = [facts[1 + i] for i in range(ROW_SLOTS)]
    core = facts[1 + ROW_SLOTS]
    sources = [streams[0].at[pl.ds(0, tok_count)], *streams[1:]]
    inputs = [pltpu.make_async_copy(a, b, s_sems.at[i]) for i, (a, b) in enumerate(zip(sources, spots_in))]
    for copy in inputs[:4]:
        copy.start()
    weights = Weights(core, carried, sibling, (first, second), w_sems)
    weights.start(range(TILES), (1,))
    loads = [
        [pltpu.make_async_copy(residuals[i].at[j], held[i].at[j], k_sems.at[i, j]) for i in range(5)]
        for j in range(TILES)
    ]
    mask = pad_mask(bucket, lengths, (tok_count, LANES), tok_count)
    edge, scale = bin_facts(bucket, (half, LANES), tok_count)
    edge = widen(jnp.where(edge, 1.0, 0.0), tile) > 0.5
    scale = widen(scale, tile)
    for copy in inputs[:4]:
        copy.wait()
    for copy in loads[0]:
        copy.start()
    copies = load_tables(bucket, tables, spots, t_sems)
    for copy in inputs[4:6]:
        copy.start()
    grad = back_ref[...].astype(F32) + sib_ref[...].astype(F32)
    back, terms = rms_back(mid_ref[...].astype(F32), gain_ref[1:2, :], grad)
    gain2 = jnp.sum(terms, axis=0, keepdims=True)
    grad_mid = cot_ref[...].astype(F32) * widen(mask, width) + back
    gm_ref[...] = grad_mid
    low = grad_mid.astype(BF16)
    mask = widen(mask, tile)
    for i in range(TILES):
        weights.wait(i, (1,))

    def put(j, act):
        at = (slice(None), pl.ds(2 * j * tile, 2 * tile + (LANES if j == TILES - 1 else 0)))
        for here, (one, two) in ((0, (keep, send)), (1, (send, keep))):
            @pl.when((core == 0) == (here == 0))
            def _():
                for i, (source, target) in enumerate(((g0, one), (g1, two))):
                    act(pltpu.make_async_copy(source.at[at], target.at[at], o_sems.at[i, j]))

    for j in range(TILES):
        at = slice(j * tile, (j + 1) * tile)
        grad_gated = sum(
            mm_nt(low[:, i * tile : (i + 1) * tile], second[i][at, tile : 2 * tile]) for i in range(TILES)
        )
        grad_gated = grad_gated * mask
        if j == 0:
            weights.start([0], (0,))
            for load in loads[1]:
                load.start()
            weights.start([1], (0,))
            for load in loads[2]:
                load.start()
            weights.start([2], (0,))
            inputs[6].start()
        for load in loads[j]:
            load.wait()
        if j == 0:
            for copy in copies:
                copy.wait()
        t, sig, mixed, kf, vf = (h[j].astype(F32) for h in held)
        dc = (grad_gated * mixed * (sig * (1.0 - sig))).astype(BF16)
        df = transform_once(spots[0][...], grad_gated * sig)
        kr, ki, vr, vi = kf[:half], kf[half:], vf[:half], vf[half:]
        dr, di = df[:half] * scale, df[half:] * scale
        divi, diki = di * vi, di * ki
        dkr = dr * vr + jnp.where(edge, 0.0, divi)
        dki = jnp.where(edge, divi, di * vr - dr * vi)
        dvr = dr * kr + jnp.where(edge, 0.0, diki)
        dvi = jnp.where(edge, diki, di * kr - dr * ki)
        du = transform_once(spots[1][...], jnp.concatenate([dkr, dki], axis=0))
        dv = (transform_once(spots[1][...], jnp.concatenate([dvr, dvi], axis=0)) * mask).astype(BF16)
        inverse = [lax.rsqrt(s + 1e-05) for s in row_sums(bucket, t * t, tok_count)]
        dots = row_sums(bucket, du * t, tok_count)
        coupling = [d * i * i * i for d, i in zip(dots, inverse)]
        dt = du * over_rows(inverse, tok_count) - t * over_rows(coupling, tok_count)
        da = (dt * mask * (1.0 - t * t)).astype(BF16)
        if j == 0:
            for copy in inputs[4:6]:
                copy.wait()
        normed, gated = normed_ref[...], gated_ref[...]
        for i, (one, two) in enumerate(
            ((mm_tn(normed, da), mm_tn(normed, dv)), (mm_tn(normed, dc), mm_tn(gated, low[:, at])))
        ):
            to = slice((2 * j + i) * tile, (2 * j + i + 1) * tile)
            g0[:, to] = one.astype(BF16)
            g1[:, to] = two.astype(BF16)
        if j < TILES - 1:
            put(j, lambda copy: copy.start())
        weights.wait(j, (0,))
        part = (
            mm_nt(da, first[j][:, :tile]) + mm_nt(dc, first[j][:, tile : 2 * tile]) + mm_nt(dv, second[j][:, :tile])
        )
        if j == 0:
            acc_ref[...] = part
        else:
            acc_ref[...] += part
    inputs[6].wait()
    back, terms = rms_back(x_ref[...].astype(F32), gain_ref[0:1, :], acc_ref[...])
    gain1 = jnp.sum(terms, axis=0, keepdims=True)
    extras = jnp.concatenate([gain1, gain2, norm_ref[...], jnp.zeros((LANES - 3, width), F32)], axis=0).T
    g0[:, 2 * width :] = extras.astype(BF16)
    g1[:, 2 * width :] = jnp.zeros((width, LANES), BF16)
    put(TILES - 1, lambda copy: copy.start())
    tok_ref[...] = (gm_ref[...] + back).astype(BF16)
    for j in range(TILES):
        put(j, lambda copy: copy.wait())


def mix_back(facts, x, cot, gains, mid, own, sib, normed, gated, norms, kept, carried, sibling, tables):
    tok, width = x.shape
    assert TILES * (width // TILES) == width
    part = jax.ShapeDtypeStruct((width, 2 * width + LANES), BF16)
    spots = [(tok, width)] * 7
    kinds = [BF16] * 7
    return pl.pallas_call(
        mix_back_kernel,
        in_specs=[pl.BlockSpec(memory_space=pltpu.SMEM), INSIDE, INSIDE, *[ANY] * (7 + 5 + 2 + 2)],
        out_specs=[INSIDE, ANY, ANY],
        out_shape=[jax.ShapeDtypeStruct((tok, width), BF16), part, part],
        scratch_shapes=[
            tuple(pltpu.VMEM(shape, kind) for shape, kind in zip(spots, kinds)),
            half_spots(width), half_spots(width), table_spots(tok, 2),
            tuple(pltpu.VMEM(k.shape, k.dtype) for k in kept),
            pltpu.VMEM(part.shape, BF16), pltpu.VMEM(part.shape, BF16),
            pltpu.VMEM((tok, width), F32), pltpu.VMEM((tok, width), F32),
            pltpu.SemaphoreType.DMA((7,)), pltpu.SemaphoreType.DMA((2, TILES)), pltpu.SemaphoreType.DMA((2,)),
            pltpu.SemaphoreType.DMA((5, TILES)), pltpu.SemaphoreType.DMA((2, TILES)),
        ],
        compiler_params=pltpu.CompilerParams(vmem_limit_bytes=VMEM_BYTES),
        name="mix_back",
    )(facts, gains, norms, own, sib, mid, cot, gated, normed, x, *kept, carried, sibling, tables[0], tables[2])


UNIT_TILES = 4


def ffn_kernel(facts, nfo_ref, nfs_ref, gfo_ref, gfs_ref, *refs):
    pieces, refs = refs[:6], refs[6:]
    nf_ref, h_ref, dgu_ref, kept_ref, sent_ref, wgu_ref, wd_ref, gf_ref, gu, downs, sems, down_sems = refs
    step = pl.program_id(0)
    tok, width = nfo_ref.shape
    units = h_ref.shape[1]
    span = gu.shape[2]
    bits = [facts[2 + ROW_SLOTS + i] for i in range(3)]

    def copies(t):
        chain, column = divmod(t, UNIT_TILES // 2)
        for side in range(2):
            half = bits[chain] if side == 0 else 1 - bits[chain]
            piece = pieces[2 * chain + side]
            count = piece.shape[1]
            for b in range(piece.shape[0]):
                yield pltpu.make_async_copy(
                    piece.at[b, :, :, pl.ds(2 * units * column, 2 * units)],
                    gu.at[t, pl.ds((2 * b + half) * count, count)],
                    sems.at[t, side, b],
                )

    def down_copies():
        for side in range(2):
            half = bits[2] if side == 0 else 1 - bits[2]
            yield pltpu.make_async_copy(pieces[4 + side], downs.at[:, half], down_sems.at[side])

    @pl.when(step == 0)
    def _():
        for copy in [*copies(0), *down_copies()]:
            copy.start()
        for t in range(1, UNIT_TILES):
            for copy in copies(t):
                copy.start()
        nf_ref[:tok] = nfo_ref[...]
        nf_ref[tok:] = nfs_ref[...]
        gf_ref[:tok] = gfo_ref[...]
        gf_ref[tok:] = gfs_ref[...]

    for t in range(UNIT_TILES):

        @pl.when(step == t)
        def _():
            for copy in copies(t):
                copy.wait()

    @pl.when(step == 0)
    def _():
        for copy in down_copies():
            copy.wait()

    nf, gf = nf_ref[...], gf_ref[...]
    wgu = gu[step].reshape(gu.shape[1] * span, 2 * units)
    wd = downs.reshape(UNIT_TILES * units, width)[pl.ds(pl.multiple_of(step * units, units), units)]
    wgu_ref[...], wd_ref[...] = wgu, wd
    both = mm(nf, wgu)
    g, u = both[:, :units], both[:, units:]
    dh = mm_nt(gf, wd)
    sig = 0.5 + 0.5 * jnp.tanh(0.5 * g)
    silu = g * sig
    h = (silu * u).astype(BF16)
    h_ref[...] = h
    dgu_ref[:, units:] = (dh * silu).astype(BF16)
    dgu_ref[:, :units] = (dh * u * (sig * (1.0 + g * (1.0 - sig)))).astype(BF16)
    gd = mm_tn(h, gf).astype(BF16).reshape(sent_ref.shape[0], 2, *sent_ref.shape[1:])
    kept_ref[...] = jnp.where(bits[2] == 0, gd[:, 0], gd[:, 1])
    sent_ref[...] = jnp.where(bits[2] == 0, gd[:, 1], gd[:, 0])


def ffn(facts, nf_own, nf_sib, gf_own, gf_sib, pieces):
    tok, width = nf_own.shape
    total_units = pieces[0].shape[2]
    units = total_units // UNIT_TILES
    span = min(pieces[0].shape[1], pieces[2].shape[1])
    cut = [p.reshape(p.shape[0], p.shape[1] // span, span, p.shape[2]) for p in pieces[:4]]
    below, above = pieces[4].shape[1], pieces[4].shape[0]
    whole = pl.BlockSpec((tok, width), lambda j: (0, 0))
    tall = pl.BlockSpec((width, 2 * units), lambda j: (0, j))
    flat = pl.BlockSpec((units, width), lambda j: (j, 0))
    return pl.pallas_call(
        ffn_kernel,
        grid=(UNIT_TILES,),
        in_specs=[pl.BlockSpec(memory_space=pltpu.SMEM), whole, whole, whole, whole, *[ANY] * 6],
        out_specs=[
            pl.BlockSpec((2 * tok, width), lambda j: (0, 0)),
            pl.BlockSpec((2 * tok, units), lambda j: (0, j)),
            pl.BlockSpec((2 * tok, 2 * units), lambda j: (0, j)),
            *[pl.BlockSpec((above // UNIT_TILES, below, width), lambda j: (j, 0, 0))] * 2,
            tall, flat,
        ],
        out_shape=[
            jax.ShapeDtypeStruct((2 * tok, width), BF16),
            jax.ShapeDtypeStruct((2 * tok, total_units), BF16),
            jax.ShapeDtypeStruct((2 * tok, 2 * total_units), BF16),
            *[jax.ShapeDtypeStruct((above, below, width), BF16)] * 2,
            jax.ShapeDtypeStruct((width, 2 * total_units), BF16),
            jax.ShapeDtypeStruct((total_units, width), BF16),
        ],
        scratch_shapes=[
            pltpu.VMEM((2 * tok, width), BF16),
            pltpu.VMEM((UNIT_TILES, width // span, span, 2 * units), BF16),
            pltpu.VMEM((above, 2, below, width), BF16),
            pltpu.SemaphoreType.DMA((UNIT_TILES, 2, max(p.shape[0] for p in cut))),
            pltpu.SemaphoreType.DMA((2,)),
        ],
        compiler_params=pltpu.CompilerParams(vmem_limit_bytes=VMEM_BYTES),
        name="ffn",
    )(facts, nf_own, nf_sib, gf_own, gf_sib, *cut, *pieces[4:])


def pack_mixer_kernel(place, in_ref, out_ref, gain_ref, mine_ref, send_ref):
    core = place[0]
    width = out_ref.shape[1]
    tile = width // TILES
    for j in range(TILES):
        at = slice(j * tile, (j + 1) * tile)
        pairs = (
            (in_ref[:, j * tile : (j + 1) * tile], in_ref[:, 2 * width + j * tile : 2 * width + (j + 1) * tile]),
            (in_ref[:, width + j * tile : width + (j + 1) * tile], out_ref[:, at]),
        )
        for i, (one, two) in enumerate(pairs):
            to = slice((2 * j + i) * tile, (2 * j + i + 1) * tile)
            mine_ref[:, to] = jnp.where(core == 0, one, two)
            send_ref[:, to] = jnp.where(core == 0, two, one)
    mine_ref[:, 2 * width :] = gain_ref[...]
    send_ref[:, 2 * width :] = gain_ref[...]


def pack_mixer(place, w_in, w_out, gains):
    rows, width = w_out.shape
    return pl.pallas_call(
        pack_mixer_kernel,
        in_specs=[pl.BlockSpec(memory_space=pltpu.SMEM), INSIDE, INSIDE, INSIDE],
        out_specs=[INSIDE, INSIDE],
        out_shape=[jax.ShapeDtypeStruct((rows, 2 * width + LANES), BF16)] * 2,
        name="pack_mixer",
    )(place, w_in, w_out, gains)


def pack_units_kernel(place, gu_ref, order_ref, mine_ref, send_ref, stack_ref):
    core = place[0]
    rows = gu_ref.shape[0]
    width = order_ref.shape[0]
    half = width // 2
    groups = gu_ref.shape[1] // width
    pitch = stack_ref.shape[0] // groups
    for i in range(groups):
        stack_ref[i * pitch : i * pitch + rows] = gu_ref[:, i * width : (i + 1) * width].astype(F32)
    sorted_rows = mm(stack_ref[...].astype(BF16), order_ref[...])
    for i in range(groups):
        block = sorted_rows[i * pitch : i * pitch + rows]
        spot = 2 * i if i < groups // 2 else 2 * i - groups + 1
        to = slice(spot * half, (spot + 1) * half)
        mine_ref[:, to] = jnp.where(core == 0, block[:, :half], block[:, half:]).astype(BF16)
        send_ref[:, to] = jnp.where(core == 0, block[:, half:], block[:, :half]).astype(BF16)


def pack_units(place, w_gu, order):
    rows, columns = w_gu.shape
    width = order.shape[0]
    pitch = -(-rows // 8) * 8
    return pl.pallas_call(
        pack_units_kernel,
        in_specs=[pl.BlockSpec(memory_space=pltpu.SMEM), INSIDE, INSIDE],
        out_specs=[INSIDE, INSIDE],
        out_shape=[jax.ShapeDtypeStruct((rows, columns // 2), BF16)] * 2,
        scratch_shapes=[pltpu.VMEM((columns // width * pitch, width), F32)],
        name="pack_units",
    )(place, w_gu, order)


def unpack_mixer_kernel(place, own_ref, far_ref, in_ref, out_ref, extra_ref):
    core = place[0]
    width = out_ref.shape[1]
    tile = width // TILES
    own, far = own_ref[...].astype(F32), far_ref[...].astype(F32)
    for j in range(TILES):
        for i in range(2):
            at = slice((2 * j + i) * tile, (2 * j + i + 1) * tile)
            one = jnp.where(core == 0, own[:, at], far[:, at])
            two = jnp.where(core == 0, far[:, at], own[:, at])
            in_ref[:, i * width + j * tile : i * width + (j + 1) * tile] = one
            if i == 0:
                in_ref[:, 2 * width + j * tile : 2 * width + (j + 1) * tile] = two
            else:
                out_ref[:, j * tile : (j + 1) * tile] = two
    extra_ref[...] = jnp.where(core == 0, own[:, 2 * width :], far[:, 2 * width :]).T[:8]


def unpack_mixer(place, own, far, width):
    rows = own.shape[0]
    return pl.pallas_call(
        unpack_mixer_kernel,
        in_specs=[pl.BlockSpec(memory_space=pltpu.SMEM), INSIDE, INSIDE],
        out_specs=[INSIDE] * 3,
        out_shape=[jax.ShapeDtypeStruct(shape, F32) for shape in ((rows, 3 * width), (rows, width), (8, rows))],
        name="unpack_mixer",
    )(place, own, far)


def unpack_units_kernel(place, own_ref, far_ref, order_ref, gu_ref, stack_ref):
    core = place[0]
    rows = gu_ref.shape[0]
    width = order_ref.shape[0]
    half = width // 2
    groups = gu_ref.shape[1] // width
    pitch = stack_ref.shape[0] // groups
    own, far = own_ref[...].astype(F32), far_ref[...].astype(F32)
    for i in range(groups):
        spot = 2 * i if i < groups // 2 else 2 * i - groups + 1
        at = slice(spot * half, (spot + 1) * half)
        to = slice(i * pitch, i * pitch + rows)
        stack_ref[to, :half] = jnp.where(core == 0, own[:, at], far[:, at])
        stack_ref[to, half:] = jnp.where(core == 0, far[:, at], own[:, at])
    sorted_rows = mm_nt(stack_ref[...].astype(BF16), order_ref[...])
    for i in range(groups):
        gu_ref[:, i * width : (i + 1) * width] = sorted_rows[i * pitch : i * pitch + rows]


def unpack_units(place, own, far, order):
    rows, columns = own.shape
    width = order.shape[0]
    pitch = -(-rows // 8) * 8
    return pl.pallas_call(
        unpack_units_kernel,
        in_specs=[pl.BlockSpec(memory_space=pltpu.SMEM), INSIDE, INSIDE, INSIDE],
        out_specs=INSIDE,
        out_shape=jax.ShapeDtypeStruct((rows, 2 * columns), F32),
        scratch_shapes=[pltpu.VMEM((2 * columns // width * pitch, width), F32)],
        name="unpack_units",
    )(place, own, far, order)


class Links:
    def __init__(self):
        self.outer = lax.axis_size("outer")
        self.narrow = lax.axis_size("narrow")
        self.core = lax.axis_index("core")
        self.bits = []
        for axis, size in (("outer", self.outer), ("narrow", self.narrow)):
            spot = lax.axis_index(axis)
            span = size
            while span > 1:
                span //= 2
                self.bits.append((axis, size, span, (spot // span) % 2))
        self.outer_bits = sum(bit[0] == "outer" for bit in self.bits)

    def chain(self, turn):
        rest = list(range(1, len(self.bits)))
        turn %= len(rest)
        return [0] + rest[turn:] + rest[:turn]

    def narrow_last(self):
        return [0] + [p for p in range(1, len(self.bits)) if p != self.outer_bits] + [self.outer_bits]

    def swap_core(self, values):
        return lax.ppermute(values, "core", [(0, 1), (1, 0)])

    def exchange(self, values, p):
        axis, size, stride, _ = self.bits[p]
        return lax.ppermute(values, axis, [(i, i ^ stride) for i in range(size)])

    def split(self, p, have, middle, rows):
        before = 2 ** sum(q < p for q in have)
        after = 2 ** sum(q > p for q in have)
        if p < self.outer_bits:
            return before, after * middle * rows
        return before * middle, after * rows

    def gather_step(self, block, p, have, middle):
        rows = block.shape[0] // (middle * 2 ** len(have))
        before, after = self.split(p, have, middle, rows)
        mine = block.reshape(before, 1, after, block.shape[1])
        other = self.exchange(block, p).reshape(mine.shape)
        bit = self.bits[p][3]
        side = lax.broadcasted_iota(jnp.int32, (1, 2, 1, 1), 1)
        both = jnp.where(side == bit, mine, other)
        return both.reshape(-1, block.shape[1])

    def gather_pieces(self, block, p, have, middle):
        rows = block.shape[0] // (middle * 2 ** len(have))
        before, after = self.split(p, have, middle, rows)
        shape = (before, after, block.shape[1])
        return block.reshape(shape), self.exchange(block, p).reshape(shape)

    def far_gather(self, blocks):
        rows = blocks[0].shape[0]
        flat = [b[i : i + rows] for b in blocks for i in range(0, b.shape[0], rows)]
        got = self.exchange(jnp.concatenate(flat, axis=1), 0)
        side = lax.broadcasted_iota(jnp.int32, (2, 1, 1), 0)
        grown, at = [], 0
        for b in blocks:
            other = []
            for _ in range(b.shape[0] // rows):
                other.append(got[:, at : at + b.shape[1]])
                at += b.shape[1]
            other = jnp.concatenate(other, axis=0)
            grown.append(jnp.where(side == self.bits[0][3], b[None], other[None]).reshape(-1, b.shape[1]))
        return grown

    def spread(self, block, middle):
        shape = (2,) * self.outer_bits + (middle,) + (2,) * (len(self.bits) - self.outer_bits)
        return [block.reshape(*shape, block.shape[0] // math.prod(shape), block.shape[1])]

    def spread_half(self, block, p):
        shape = [2] * self.outer_bits + [1] + [2] * (len(self.bits) - self.outer_bits)
        shape[p if p < self.outer_bits else p + 1] = 1
        return block.reshape(*shape, -1, block.shape[-1])

    def side(self, terms, p, other):
        bit = self.bits[p][3]
        dim = p if p < self.outer_bits else p + 1
        return [lax.dynamic_slice_in_dim(t, 1 - bit if other else bit, 1, dim) for t in terms]

    def scatter_step(self, terms, p):
        return [*self.side(terms, p, False), self.exchange(total(self.side(terms, p, True)), p)]

    def far_scatter(self, blocks):
        sent = [flat(total(self.side(terms, 0, True))) for terms in blocks]
        rows = sent[0].shape[0]
        cut = [m[i : i + rows] for m in sent for i in range(0, m.shape[0], rows)]
        got = self.exchange(jnp.concatenate(cut, axis=1), 0)
        sums, at = [], 0
        for terms, m in zip(blocks, sent):
            other = []
            for _ in range(m.shape[0] // rows):
                other.append(got[:, at : at + m.shape[1]])
                at += m.shape[1]
            kept = [flat(t) for t in self.side(terms, 0, False)]
            sums.append(total([*kept, jnp.concatenate(other, axis=0)]))
        return sums


def total(terms):
    return sum(t.astype(F32) for t in terms).astype(BF16)


def flat(block):
    return block.reshape(-1, block.shape[-1])


def unit_order(width, chunk):
    columns = np.arange(width)
    pairs = width // (2 * chunk)
    source = np.concatenate(
        [np.concatenate([(2 * i + core) * chunk + np.arange(chunk) for i in range(pairs)]) for core in range(2)]
    )
    return (columns[:, None] == source[None, :]).astype(ml_dtypes.bfloat16)


def on_device(tokens, cotangent, w_in, w_out, w_gu, w_down, gain_mix, gain_ffn, buckets, lengths):
    links = Links()
    core = links.core
    tok, width = tokens.shape
    rows = w_in.shape[0]
    ff = w_gu.shape[1] // 2
    units = ff // 2
    tile = width // TILES
    fence = lax.optimization_barrier

    tables = [jnp.asarray(t) for t in transform_tables(tok)]
    order = jnp.asarray(unit_order(width, ff // (2 * links.outer)))
    chains = [links.chain(2), links.chain(1), links.narrow_last()]
    bits = [links.bits[chain[-1]][3] for chain in chains]
    facts = jnp.concatenate([buckets, lengths[0], jnp.stack([core, *bits])]).astype(jnp.int32)
    middles = [2, 2, 1]
    count = len(links.bits)

    def grow(blocks, k, middles):
        return [links.gather_step(b, chain[k], set(chain[:k]), m) for b, chain, m in zip(blocks, chains, middles)]

    def shrink(blocks, k):
        return [links.scatter_step(terms, chain[k]) for terms, chain in zip(blocks, chains)]

    def both_rows(mine, send):
        other = links.swap_core(send)
        side = lax.broadcasted_iota(jnp.int32, (2, 1, 1), 0)
        return jnp.where(side == core, mine[None], other[None]).reshape(2 * mine.shape[0], mine.shape[1])

    lane = lax.broadcasted_iota(jnp.int32, (rows, LANES), 1)
    gains = jnp.where(lane == 0, gain_mix[:, None], jnp.where(lane == 1, gain_ffn[:, None], 0))
    place = core.reshape(1).astype(jnp.int32)
    mine, send = pack_mixer(place, w_in, w_out, gains)
    mine_gu, send_gu = pack_units(place, w_gu, order)
    wd = links.gather_step(w_down, 0, set(), 1)
    mixer, wd = fence((both_rows(mine, send), wd))
    mixer = links.gather_step(mixer, 0, set(), 2)
    gu = both_rows(mine_gu, send_gu)
    mixer, gu = fence((mixer, gu))
    mask = pad_mask(facts[0], [facts[1 + i] for i in range(ROW_SLOTS)], (tok, 1), tok)
    gf = (fence((cotangent, mixer))[0].astype(F32) * mask).astype(BF16)
    (gu,) = links.far_gather([gu])
    cuts = [0, 5 * LANES, 10 * LANES, mine.shape[1]]
    parts = [mixer[:, a:b] for a, b in zip(cuts[:-1], cuts[1:])]
    weights = [gu[:, :units], gu[:, units:], wd]
    for k in range(1, count):
        parts = grow(parts, k, [2] * TILES)
    for k in range(1, count - 1):
        weights = grow(weights, k, middles)
    parts = fence((parts, weights, gf))[0]
    parts = jnp.concatenate(parts, axis=1)
    siblings = links.swap_core(parts)

    normed, gated, mid, low_mid, nf, norms, gains, *kept = mix_forward(facts, tokens, parts, siblings, tables)

    nf = fence((nf, weights))[0]
    pieces = [
        piece
        for w, chain, m in zip(weights, chains, middles)
        for piece in links.gather_pieces(w, chain[-1], set(chain[:-1]), m)
    ]

    nf, gf = fence((nf, gf))
    nf2, h, dgu, down_kept, down_sent, wgu, wd = ffn(facts, nf, links.swap_core(nf), gf, links.swap_core(gf), pieces)
    back = mm_nt(dgu, wgu).astype(BF16)
    back_sib = links.swap_core(back[tok:])
    grad_gu = mm_tn(nf2, dgu).astype(BF16)
    grads = [links.spread(g, 2) for g in (grad_gu[:, :units], grad_gu[:, units:])]
    last = chains[2][-1]
    down_terms = [links.spread_half(m, last) for m in (down_kept, down_sent)]
    down_terms[1] = links.exchange(down_terms[1], last)
    grads = shrink(grads, count - 1) + [down_terms]

    devices = 2 * links.outer * links.narrow
    grad_tokens, keep, send = mix_back(
        facts, tokens, cotangent, gains, low_mid, back, back_sib, normed, gated, norms * (1.0 / devices), kept,
        parts, siblings, tables,
    )
    grads, keep, send, h = fence((grads, keep, send, h))
    sums = total([keep, links.swap_core(send)])
    sums = [links.spread(sums[:, a:b], 2) for a, b in zip(cuts[:-1], cuts[1:])]
    sent = [total(links.side(terms, chain[-1], True)) for terms, chain in zip(sums, chains)]
    kept = [links.side(terms, chain[-1], False) for terms, chain in zip(sums, chains)]
    grads = shrink(grads, count - 2)
    grads, sent, kept = fence((grads, sent, kept))
    for k in reversed(range(1, count - 2)):
        grads = shrink(grads, k)
    grads, h, held = fence((grads, h, sent[-1]))
    sent = [*sent[:-1], held]
    sums = [[total([*k, links.exchange(m, chain[-1])])] for k, m, chain in zip(kept, sent, chains)]
    out = mm(h, wd).astype(BF16)
    out_sib = links.swap_core(out[tok:])
    layer_out = ((mid + out[:tok].astype(F32) + out_sib.astype(F32)) * mask).astype(BF16)
    for k in reversed(range(1, count - 1)):
        sums = [[total(terms)] for terms in shrink(sums, k)]
    sum_gate, sum_up, sum_down = links.far_scatter(grads)
    def own_and_far(block):
        halves = block.reshape(2, rows, block.shape[1])
        own = lax.dynamic_index_in_dim(halves, core, 0, keepdims=False)
        return own, links.swap_core(lax.dynamic_index_in_dim(halves, 1 - core, 0, keepdims=False))

    grad_w_gu = unpack_units(place, *own_and_far(jnp.concatenate([sum_gate, sum_up], axis=1)), order)
    sums = links.far_scatter(sums)
    sums, grad_w_gu = fence((sums, grad_w_gu))
    grad_w_in, grad_w_out, extra = unpack_mixer(place, *own_and_far(jnp.concatenate(sums, axis=1)), width)
    return (
        layer_out, grad_tokens, grad_w_in, grad_w_out, grad_w_gu, sum_down.astype(F32), extra[0], extra[1], extra[2],
    )


def solution(mesh):
    wide, narrow = mesh.devices.shape
    split = jax.sharding.Mesh(mesh.devices.reshape(wide // 2, 2, narrow), ("outer", "core", "narrow"))
    every = ("outer", "core", "narrow")
    flat, tall = P(every), P(every, None)
    return jax.shard_map(
        on_device,
        mesh=split,
        in_specs=(tall, tall, tall, tall, tall, tall, flat, flat, flat, tall),
        out_specs=(tall, tall, tall, tall, tall, tall, flat, flat, flat),
        check_vma=False,
    )
```
